256 devices in a mesh: row: 4 (over y), col: 64 (over x, z, core).
Axes of the slice: x: 4, y: 4, z: 8, core: 2. Of those that a mesh axis runs over, the one named last changes fastest.
Arguments:
- slide_band: bfloat16 [3, 64, 32768], P(None, 'row', 'col'), may hold values from -21 to 21
- cotangent: bfloat16 [64, 32, 16384], P(None, 'row', 'col'), may hold values from -0.058004853 to 0.058004853
- stem_weight: bfloat16 [64, 7, 7, 3], replicated, may hold values from -0.5 to 0.5
- mid_weight: bfloat16 [2, 64, 3, 3, 64], replicated, may hold values from -0.25 to 0.25
- norm_gains: float32 [3, 64], replicated, may hold values from 0.1 to 1.9
- norm_shifts: float32 [3, 64], replicated, may hold values from -0.5 to 0.5
Outputs:
- activation: bfloat16 [64, 32, 16384], P(None, 'row', 'col')
- grad_stem: float32 [64, 7, 7, 3], replicated
- grad_mid: float32 [2, 64, 3, 3, 64], replicated
- grad_gains: float32 [3, 64], replicated
- grad_shifts: float32 [3, 64], replicated
The draws below stay inside these ranges and needn't reach their ends.
All inputs are finite; a program needn't handle non-finite values.
Results may differ from the reference program's by a relative error of at most 0.005.
The reference program's roundings to bfloat16 on the way count: a program that leaves them out, or rounds other values in their place, can miss the bound.
Values may be sent and summed in bfloat16 or wider, within the bound.
A program may use at most 64 MiB of HBM per device.

```python
import math
import jax
import jax.numpy as jnp
from jax import lax

C1 = 64
IN_CH = 3
LAYERS = 2
HEIGHT = 64
WIDTH_PX = 32768
OUT_ROWS = 32
OUT_COLS = 16384
PIXELS = 524288


def scale_profile(key, height, width):
    row_key, col_key = jax.random.split(key)
    row_pos = jnp.arange(height, dtype=jnp.float32) / max(height - 1, 1)
    col_pos = jnp.arange(width, dtype=jnp.float32) / max(width - 1, 1)
    row_scale = 3.0 ** row_pos * jnp.exp(jax.random.uniform(row_key, (height,), jnp.float32, 0.0, math.log(3.4)))
    col_scale = 3.0 ** col_pos * jnp.exp(jax.random.uniform(col_key, (width,), jnp.float32, 0.0, math.log(3.4)))
    return row_scale[:, None] * col_scale[None, :]


def draw_slide_band(key, part):
    key = jax.random.fold_in(key, 11)
    noise_key, scale_key = jax.random.split(key)
    profile = scale_profile(scale_key, HEIGHT, WIDTH_PX)
    noise = jnp.clip(jax.random.normal(noise_key, (IN_CH, HEIGHT, WIDTH_PX), jnp.float32), -4.0, 4.0)
    return (0.05 * profile[None] * noise).astype(jnp.bfloat16)


def draw_cotangent(key, part):
    key = jax.random.fold_in(key, 12)
    noise_key, scale_key = jax.random.split(key)
    profile = scale_profile(scale_key, OUT_ROWS, OUT_COLS)
    noise = jnp.clip(jax.random.normal(noise_key, (C1, OUT_ROWS, OUT_COLS), jnp.float32), -4.0, 4.0)
    return (0.1 * PIXELS ** (-0.5) * profile[None] * noise).astype(jnp.bfloat16)


def normal_values(stream_key, dims, spread, most, kind=jnp.bfloat16):
    return jnp.clip(spread * jax.random.normal(stream_key, dims, jnp.float32), -most, most).astype(kind)


def setup_inputs(seed: int = 0) -> dict:
    arg_keys = jax.random.split(jax.random.key(seed), 7)
    return {
        "slide_band": draw_slide_band(jax.random.fold_in(arg_keys[6], 71), 0),
        "cotangent": draw_cotangent(jax.random.fold_in(arg_keys[6], 71), 0),
        "stem_weight": normal_values(arg_keys[2], (C1, 7, 7, IN_CH), (49 * IN_CH) ** -0.5, 0.5),
        "mid_weight": normal_values(arg_keys[3], (LAYERS, C1, 3, 3, C1), (9 * C1) ** -0.5, 0.25),
        "norm_gains": jnp.clip(1.0 + 0.18 * jax.random.normal(arg_keys[4], (LAYERS + 1, C1), jnp.float32), 0.1, 1.9),
        "norm_shifts": jnp.clip(jax.random.uniform(arg_keys[5], (LAYERS + 1, C1), jnp.float32, -0.5, 0.5), -0.5, 0.5),
    }


EPS = 1e-05

def stem_conv(image_f, weight_f):
    return lax.conv_general_dilated(image_f[None], weight_f.transpose(0, 3, 1, 2), (2, 2), ((3, 3), (3, 3)), dimension_numbers=('NCHW', 'OIHW', 'NCHW'), precision=lax.Precision.HIGHEST)[0]

def mid_conv(act_f, weight_f):
    return lax.conv_general_dilated(act_f[None], weight_f.transpose(0, 3, 1, 2), (1, 1), ((1, 1), (1, 1)), dimension_numbers=('NCHW', 'OIHW', 'NCHW'), precision=lax.Precision.HIGHEST)[0]

def silu_slope(normed):
    sig = jax.nn.sigmoid(normed)
    return sig * (1.0 + normed * (1.0 - sig))

def normalize(pre_act, gain_row, shift_row):
    mean_value = lax.optimization_barrier(jnp.mean(pre_act, axis=(1, 2)))
    centred = pre_act - mean_value[:, None, None]
    variance = lax.optimization_barrier(jnp.mean(centred * centred, axis=(1, 2)))
    inv_std = lax.rsqrt(variance + EPS)
    whitened = centred * inv_std[:, None, None]
    normed = gain_row[:, None, None] * whitened + shift_row[:, None, None]
    return (whitened, normed, inv_std)

def norm_back(grad_out, whitened, gain_row, inv_std, pixel_count):
    shift_sum = lax.optimization_barrier(jnp.sum(grad_out, axis=(1, 2)))
    gain_sum = lax.optimization_barrier(jnp.sum(grad_out * whitened, axis=(1, 2)))
    scaled = (gain_row * inv_std)[:, None, None]
    grad_pre = scaled * (grad_out - shift_sum[:, None, None] / pixel_count - whitened * gain_sum[:, None, None] / pixel_count)
    return (grad_pre.astype(jnp.bfloat16), gain_sum, shift_sum)

def reference(slide_band, cotangent, stem_weight, mid_weight, norm_gains, norm_shifts):
    gains_f = norm_gains.astype(jnp.float32)
    shifts_f = norm_shifts.astype(jnp.float32)
    image_f = slide_band.astype(jnp.float32)
    stem_f = stem_weight.astype(jnp.float32)
    pre_stem = stem_conv(image_f, stem_f)
    pixel_count = jnp.asarray(pre_stem.shape[1] * pre_stem.shape[2], jnp.float32)
    whitened, normed, inv_std = normalize(pre_stem, gains_f[0], shifts_f[0])
    acts = [jax.nn.silu(normed).astype(jnp.bfloat16)]
    white_list = [whitened]
    normed_list = [normed]
    inv_list = [inv_std]
    for layer_index in range(LAYERS):
        pre_act = mid_conv(acts[-1].astype(jnp.float32), mid_weight[layer_index].astype(jnp.float32))
        whitened, normed, inv_std = normalize(pre_act, gains_f[layer_index + 1], shifts_f[layer_index + 1])
        acts.append(jax.nn.silu(normed).astype(jnp.bfloat16))
        white_list.append(whitened)
        normed_list.append(normed)
        inv_list.append(inv_std)
    grad_out = cotangent.astype(jnp.float32) * silu_slope(normed_list[-1])
    gain_grads = [None] * (LAYERS + 1)
    shift_grads = [None] * (LAYERS + 1)
    weight_grads = [None] * LAYERS
    for layer_index in reversed(range(LAYERS)):
        norm_index = layer_index + 1
        grad_pre, gain_grads[norm_index], shift_grads[norm_index] = norm_back(grad_out, white_list[norm_index], gains_f[norm_index], inv_list[norm_index], pixel_count)
        unused, conv_back = jax.vjp(mid_conv, acts[layer_index].astype(jnp.float32), mid_weight[layer_index].astype(jnp.float32))
        grad_in, weight_grads[layer_index] = conv_back(grad_pre.astype(jnp.float32))
        grad_out = grad_in * silu_slope(normed_list[layer_index])
    grad_pre, gain_grads[0], shift_grads[0] = norm_back(grad_out, white_list[0], gains_f[0], inv_list[0], pixel_count)
    unused, stem_back = jax.vjp(lambda weight_f: stem_conv(image_f, weight_f), stem_f)
    grad_stem = stem_back(grad_pre.astype(jnp.float32))[0]
    return (acts[-1], grad_stem, jnp.stack(weight_grads), jnp.stack(gain_grads), jnp.stack(shift_grads))
```

```python
import jax
import jax.numpy as jnp
from jax import lax
from jax.experimental import pallas as pl
from jax.experimental.pallas import tpu as pltpu
from jax.sharding import PartitionSpec as P

EPS = 1e-05
MESH = pl.DeviceIdType.MESH
F32 = jnp.float32
BF16 = jnp.bfloat16

CH = 64
ROWS = 8
COLS = 256
TAPS = 9 * CH
LOCAL = ROWS * COLS
PIXELS = 524288.0
GROUP = 16
STEM_ROWS = 21
GRAD_LANES = 1536


def dot(a, b):
    return jnp.dot(a, b, preferred_element_type=F32)


def dot_nt(a, b):
    return lax.dot_general(a, b, (((1,), (1,)), ((), ())), preferred_element_type=F32)


def kernel(
    img, cot, w0, wm, wt, params,
    act_out, grad_out, gains_out, shifts_out,
    tiles, sel, patches, wbig, x0, x1, dmap, dstem,
    pre, white, slope, up, rowhalo, colsend, colrecv,
    ar_a, ar_b, gbuf, rsbuf, bbuf, cbuf,
    img_send, img_recv, halo_send, halo_recv, ar_send, ar_recv, fin_send, fin_recv,
):
    row, col = lax.axis_index("row"), lax.axis_index("col")
    not_top = jnp.where(row == 0, 0.0, 1.0).astype(F32)
    not_bottom = jnp.where(row == 3, 0.0, 1.0).astype(F32)
    not_left = jnp.where(col == 0, 0.0, 1.0).astype(F32)
    not_right = jnp.where(col == 63, 0.0, 1.0).astype(F32)
    rank_a = col % GROUP
    rank_b = row * 4 + col // GROUP

    def peer_a(k):
        return (row, (col // GROUP) * GROUP + (rank_a + k) % GROUP)

    def peer_b(k):
        other = (rank_b + k) % GROUP
        return (other // 4, (other % 4) * GROUP + rank_a)

    def near(dr, dc):
        return ((row + dr + 4) % 4, (col + dc + 64) % 64)

    around = [(1, 0), (-1, 0), (0, 1), (0, -1), (1, 1), (1, -1), (-1, 1), (-1, -1)]

    barrier = pltpu.get_barrier_semaphore()
    for k in range(1, GROUP):
        pl.semaphore_signal(barrier, inc=1, device_id=peer_a(k), device_id_type=MESH)
        pl.semaphore_signal(barrier, inc=1, device_id=peer_b(k), device_id_type=MESH)
    for dr, dc in around:
        pl.semaphore_signal(barrier, inc=1, device_id=near(dr, dc), device_id_type=MESH)
    pl.semaphore_wait(barrier, 2 * (GROUP - 1) + len(around))

    copies = []
    for n, (dr, dc) in enumerate(around):
        src = img if dc == 0 else (img.at[:, 384:512] if dc == 1 else img.at[:, 0:128])
        lanes = slice(128, 640) if dc == 0 else (slice(0, 128) if dc == 1 else slice(640, 768))
        first = 48 * (1 - dr)
        copies.append(
            pltpu.make_async_remote_copy(
                src_ref=src,
                dst_ref=tiles.at[first : first + 48, lanes],
                send_sem=img_send.at[n],
                recv_sem=img_recv.at[n],
                device_id=near(dr, dc),
                device_id_type=MESH,
            )
        )
    for copy in copies:
        copy.start()
    tiles[48:96, 128:640] = img[...]

    diff = lax.broadcasted_iota(jnp.int32, (768, 384), 0) - 2 * lax.broadcasted_iota(
        jnp.int32, (768, 384), 1
    )
    sel[0] = jnp.where(diff == 124, 1.0, 0.0).astype(BF16)
    sel[1] = jnp.where(diff == 125, 1.0, 0.0).astype(BF16)
    w0v = w0[...]
    for i in range(ROWS):
        wbig[CH * i : CH * (i + 1), :] = (pltpu.roll(w0v, 2 * i, 1) if i else w0v).astype(BF16)
    columns = params[...].T
    gain = [columns[0:CH, k : k + 1] for k in range(3)]
    shift = [columns[0:CH, 3 + k : 4 + k] for k in range(3)]

    m = lax.broadcasted_iota(jnp.int32, (64, 144), 0)
    n = lax.broadcasted_iota(jnp.int32, (64, 144), 1)

    def steps(v, edges):
        return sum(jnp.where(v >= e, 1, 0) for e in edges)

    m_c = steps(m, (21, 42, 63))
    m_r = m - 21 * m_c
    n_t = steps(n, (48, 96))
    n_in = n - 48 * n_t
    n_c = steps(n_in, (16, 32))
    n_r = 16 * n_t + n_in - 16 * n_c
    pick = jnp.where((m_c == n_c) & (n_r == m_r + 13), 1.0, 0.0).astype(BF16)

    for copy in copies:
        copy.wait()

    def scale_tile(rows, lanes, factor):
        tiles[rows, lanes] = (tiles[rows, lanes].astype(F32) * factor).astype(BF16)

    scale_tile(slice(0, 48), slice(0, 768), not_top)
    scale_tile(slice(96, 144), slice(0, 768), not_bottom)
    scale_tile(slice(0, 144), slice(0, 128), not_left)
    scale_tile(slice(0, 144), slice(640, 768), not_right)

    image_rows = dot(pick, tiles[...]).astype(BF16)
    planes = [dot(image_rows, sel[0]), dot(image_rows, sel[1])]
    for b in range(7):
        shift_by = (b - 3) // 2 + 2
        plane = planes[(b - 3) % 2]
        moved = pltpu.roll(plane, 384 - shift_by, 1) if shift_by else plane
        patches[CH * b : CH * (b + 1), :] = moved[:, 0:COLS].astype(BF16)
    patches[448:512, :] = jnp.zeros((64, COLS), BF16)

    lane128 = lax.broadcasted_iota(jnp.int32, (CH, 128), 1)
    lane256 = lax.broadcasted_iota(jnp.int32, (CH, COLS), 1)
    lane1 = lax.broadcasted_iota(jnp.int32, (1, 128), 1)

    def fold(v):
        return v[:, 0:128] + v[:, 128:256]

    def to_row(first, second):
        both = jnp.where(lane128 == 0, first, jnp.where(lane128 == 1, second, 0.0)).T
        return jnp.concatenate([both[0:1, :], both[1:2, :]], axis=1)

    def to_columns(row_value):
        turned = jnp.broadcast_to(row_value, (8, 128)).T
        return turned[0:CH, 0:1], turned[CH : 2 * CH, 0:1]

    def gather(buf, value, peer, rank, send, recv):
        buf[pl.ds(rank, 1)] = value[None]
        for k in range(1, GROUP):
            pltpu.make_async_remote_copy(
                src_ref=buf.at[rank],
                dst_ref=buf.at[rank],
                send_sem=send,
                recv_sem=recv,
                device_id=peer(k),
                device_id_type=MESH,
            ).start()
        part = buf.at[0 : GROUP - 1]
        pltpu.make_async_copy(part, part, recv).wait()
        pltpu.make_async_copy(part, part, send).wait()
        return buf[...]

    def exchange(index, value, combine):
        got = gather(ar_a.at[index], value, peer_a, rank_a, ar_send.at[index, 0], ar_recv.at[index, 0])
        value = combine(got, float(LOCAL))
        got = gather(ar_b.at[index], value, peer_b, rank_b, ar_send.at[index, 1], ar_recv.at[index, 1])
        return combine(got, float(LOCAL * GROUP))

    def combine_moments(got, count):
        total = jnp.sum(got, axis=0)
        mean = total * (1.0 / GROUP)
        off = got - mean[None]
        spread = jnp.sum(off * off, axis=0) * count
        return jnp.where(lane1 < CH, mean, total + pltpu.roll(spread, CH, 1))

    def combine_sums(got, count):
        return jnp.sum(got, axis=0)

    def start_halo(index, ref):
        for side, lane in ((0, 0), (1, COLS - 1)):
            pack = jnp.zeros((CH, 128), F32)
            for i in range(ROWS):
                pack = jnp.where(lane128 == i, ref[i, :, lane : lane + 1], pack)
            colsend[index, side] = pack
        started = []
        for n, (dr, dc) in enumerate(around):
            if dc == 0:
                src = ref.at[ROWS - 1 if dr == 1 else 0]
                dst = rowhalo.at[index, 0 if dr == 1 else 1]
            else:
                src = colsend.at[index, 1 if dc == 1 else 0]
                dst = colrecv.at[index, (0 if dc == 1 else 3) + 1 - dr]
            copy = pltpu.make_async_remote_copy(
                src_ref=src,
                dst_ref=dst,
                send_sem=halo_send.at[index, n],
                recv_sem=halo_recv.at[index, n],
                device_id=near(dr, dc),
                device_id_type=MESH,
            )
            copy.start()
            started.append(copy)
        return started

    def build(dst, center, top, bottom, left, right):
        for r in range(ROWS + 2):
            value = top if r == 0 else (bottom if r == ROWS + 1 else center(r - 1))
            place, lane = (0, ROWS - 1) if r == 0 else ((2, 0) if r == ROWS + 1 else (1, r - 1))
            before = jnp.where(lane256 == 0, left[place][:, lane : lane + 1], pltpu.roll(value, 1, 1))
            after = jnp.where(
                lane256 == COLS - 1, right[place][:, lane : lane + 1], pltpu.roll(value, COLS - 1, 1)
            )
            base = 3 * CH * r
            dst[base : base + CH, :] = before.astype(BF16)
            dst[base + CH : base + 2 * CH, :] = value.astype(BF16)
            dst[base + 2 * CH : base + 3 * CH, :] = after.astype(BF16)

    edge = [not_top, 1.0, not_bottom]

    def build_with_halo(dst, center, apply_halo, index):
        top = apply_halo("row", 0) * not_top
        bottom = apply_halo("row", 1) * not_bottom
        left = [apply_halo("col", p) * (edge[p] * not_left) for p in range(3)]
        right = [apply_halo("col", 3 + p) * (edge[p] * not_right) for p in range(3)]
        build(dst, center, top, bottom, left, right)

    def conv(weight, src, out, after=None):
        for i in range(ROWS):
            value = dot(weight, src[3 * CH * i : 3 * CH * i + TAPS, :])
            out[i] = value if after is None else after(i, value)

    def moments(index):
        ref = pre.at[index]
        total = jnp.zeros((CH, 128), F32)
        for i in range(ROWS):
            total = total + fold(ref[i])
        mean = jnp.sum(total, axis=1, keepdims=True) * (1.0 / LOCAL)
        total = jnp.zeros((CH, 128), F32)
        for i in range(ROWS):
            off = ref[i] - mean
            total = total + fold(off * off)
        local = to_row(mean, jnp.sum(total, axis=1, keepdims=True))
        mean, squares = to_columns(exchange(index, local, combine_moments))
        return mean, lax.rsqrt(squares * (1.0 / PIXELS) + EPS)

    def halo_block(index, kind, place):
        return rowhalo[index, place] if kind == "row" else colrecv[index, place]

    mean, inv = [None] * 3, [None] * 3

    def forward_norm(index, dst, halo):
        mean[index], inv[index] = moments(index)
        mu, sd, g, s = mean[index], inv[index], gain[index], shift[index]

        def center(i):
            whitened = (pre[index, i] - mu) * sd
            white[index, i] = whitened
            normed = g * whitened + s
            sig = jax.nn.sigmoid(normed)
            slope[index, i] = sig * (1.0 + normed * (1.0 - sig))
            return normed * sig

        def outside(kind, place):
            normed = g * ((halo_block(index, kind, place) - mu) * sd) + s
            return normed * jax.nn.sigmoid(normed)

        for copy in halo:
            copy.wait()
        if dst is None:
            for i in range(ROWS):
                act_out[i] = center(i).astype(BF16)
        else:
            build_with_halo(dst, center, outside, index)

    stem = dot(wbig[...], patches[...])
    for i in range(ROWS):
        pre[0, i] = stem[CH * i : CH * (i + 1), :]
    halo = start_halo(0, pre.at[0])
    forward_norm(0, x0, halo)
    conv(wm[0], x0, pre.at[1])
    halo = start_halo(1, pre.at[1])
    forward_norm(1, x1, halo)
    conv(wm[1], x1, pre.at[2])
    halo = start_halo(2, pre.at[2])
    forward_norm(2, None, halo)

    def norm_sums(index):
        shift_total = jnp.zeros((CH, 128), F32)
        gain_total = jnp.zeros((CH, 128), F32)
        for i in range(ROWS):
            shift_total = shift_total + fold(up[index, i])
            gain_total = gain_total + fold(up[index, i] * white[index, i])
        local = to_row(
            jnp.sum(shift_total, axis=1, keepdims=True), jnp.sum(gain_total, axis=1, keepdims=True)
        )
        sums = exchange(3 + index, local, combine_sums)
        shifts_out[index : index + 1, :] = sums[:, 0:CH]
        gains_out[index : index + 1, :] = sums[:, CH : 2 * CH]
        shift_sum, gain_sum = to_columns(sums)
        return shift_sum * (1.0 / PIXELS), gain_sum * (1.0 / PIXELS)

    def down(index, sums, up_value, whitened):
        return (gain[index] * inv[index]) * (up_value - sums[0] - whitened * sums[1])

    def backward_norm(index, halo, halo_index):
        sums = norm_sums(index)

        def center(i):
            return down(index, sums, up[index, i], white[index, i])

        def outside(kind, place):
            whitened = (halo_block(index, kind, place) - mean[index]) * inv[index]
            return down(index, sums, halo_block(halo_index, kind, place), whitened)

        for copy in halo:
            copy.wait()
        build_with_halo(dmap, center, outside, index)

    def kernel_grad(src):
        total = jnp.zeros((CH, TAPS), F32)
        for i in range(ROWS):
            base = 3 * CH * (i + 1) + CH
            total = total + dot_nt(dmap[base : base + CH, :], src[3 * CH * i : 3 * CH * i + TAPS, :])
        return total

    def put_grad(value, first):
        for k in range(GROUP):
            gbuf[k, :, first : first + value.shape[1]] = value[4 * k : 4 * k + 4, :]

    gbuf[...] = jnp.zeros(gbuf.shape, F32)
    for i in range(ROWS):
        up[2, i] = cot[i].astype(F32) * slope[2, i]
    halo = start_halo(3, up.at[2])
    backward_norm(2, halo, 3)
    conv(wt[1], dmap, up.at[1], lambda i, value: value * slope[1, i])
    halo = start_halo(4, up.at[1])
    put_grad(kernel_grad(x1), 640)
    backward_norm(1, halo, 4)
    conv(wt[0], dmap, up.at[0], lambda i, value: value * slope[0, i])
    put_grad(kernel_grad(x0), 0)
    sums = norm_sums(0)
    for i in range(ROWS):
        dstem[CH * i : CH * (i + 1), :] = down(0, sums, up[0, i], white[0, i]).astype(BF16)
    banded = dot_nt(dstem[...], patches[...])
    total = banded[0:CH, :]
    for i in range(1, ROWS):
        total = total + pltpu.roll(banded[CH * i : CH * (i + 1), :], 512 - 2 * i, 1)
    src = lax.broadcasted_iota(jnp.int32, (512, 256), 0)
    dst = lax.broadcasted_iota(jnp.int32, (512, 256), 1)
    dst_a = steps(dst, range(21, 148, 21))
    dst_in = dst - 21 * dst_a
    dst_b = steps(dst_in, range(3, 19, 3))
    dst_c = dst_in - 3 * dst_b
    place = jnp.where(dst < 147, CH * dst_b + STEM_ROWS * dst_c + dst_a, -1)
    choose = jnp.where(src == place, 1.0, 0.0).astype(BF16)
    high = total.astype(BF16)
    rest = total - high.astype(F32)
    mid = rest.astype(BF16)
    low = (rest - mid.astype(F32)).astype(BF16)
    put_grad(dot(high, choose) + dot(mid, choose) + dot(low, choose), 1280)

    rsbuf[pl.ds(rank_a, 1)] = gbuf[pl.ds(rank_a, 1)]
    for k in range(1, GROUP):
        pltpu.make_async_remote_copy(
            src_ref=gbuf.at[(rank_a + k) % GROUP],
            dst_ref=rsbuf.at[rank_a],
            send_sem=fin_send.at[0],
            recv_sem=fin_recv.at[0],
            device_id=peer_a(k),
            device_id_type=MESH,
        ).start()
    part = rsbuf.at[0 : GROUP - 1]
    pltpu.make_async_copy(part, part, fin_recv.at[0]).wait()
    pltpu.make_async_copy(part, part, fin_send.at[0]).wait()
    value = jnp.sum(rsbuf[...], axis=0)
    value = jnp.sum(gather(bbuf, value, peer_b, rank_b, fin_send.at[1], fin_recv.at[1]), axis=0)
    grad_out[...] = gather(cbuf, value, peer_a, rank_a, fin_send.at[2], fin_recv.at[2])


def shards(slide_band, cotangent, stem_weight, mid_weight, norm_gains, norm_shifts):
    img = slide_band.reshape(48, 512)
    cot = cotangent.transpose(1, 0, 2)
    w0 = jnp.pad(
        stem_weight.transpose(0, 2, 3, 1), ((0, 0), (0, 0), (0, 0), (0, STEM_ROWS - 7))
    ).reshape(CH, 7, 63)
    w0 = jnp.pad(w0, ((0, 0), (0, 1), (0, 1))).reshape(CH, 512).astype(F32)
    wm = mid_weight.reshape(2, CH, TAPS)
    wt = mid_weight[:, :, ::-1, ::-1, :].transpose(0, 4, 2, 3, 1).reshape(2, CH, TAPS)
    params = jnp.pad(jnp.concatenate([norm_gains, norm_shifts]), ((0, 2), (0, 128 - CH)))
    vmem = pl.BlockSpec(memory_space=pltpu.VMEM)
    dma = pltpu.SemaphoreType.DMA
    act, grads, gains, shifts = pl.pallas_call(
        kernel,
        out_shape=(
            jax.ShapeDtypeStruct((ROWS, CH, COLS), BF16),
            jax.ShapeDtypeStruct((GROUP, 4, GRAD_LANES), F32),
            jax.ShapeDtypeStruct((3, CH), F32),
            jax.ShapeDtypeStruct((3, CH), F32),
        ),
        in_specs=[vmem] * 6,
        out_specs=(vmem,) * 4,
        scratch_shapes=[
            pltpu.VMEM((144, 768), BF16),
            pltpu.VMEM((2, 768, 384), BF16),
            pltpu.VMEM((512, COLS), BF16),
            pltpu.VMEM((512, 512), BF16),
            pltpu.VMEM((3 * CH * (ROWS + 2), COLS), BF16),
            pltpu.VMEM((3 * CH * (ROWS + 2), COLS), BF16),
            pltpu.VMEM((3 * CH * (ROWS + 2), COLS), BF16),
            pltpu.VMEM((512, COLS), BF16),
            pltpu.VMEM((3, ROWS, CH, COLS), F32),
            pltpu.VMEM((3, ROWS, CH, COLS), F32),
            pltpu.VMEM((3, ROWS, CH, COLS), F32),
            pltpu.VMEM((3, ROWS, CH, COLS), F32),
            pltpu.VMEM((5, 2, CH, COLS), F32),
            pltpu.VMEM((5, 2, CH, 128), F32),
            pltpu.VMEM((5, 6, CH, 128), F32),
            pltpu.VMEM((6, GROUP, 1, 128), F32),
            pltpu.VMEM((6, GROUP, 1, 128), F32),
            pltpu.VMEM((GROUP, 4, GRAD_LANES), F32),
            pltpu.VMEM((GROUP, 4, GRAD_LANES), F32),
            pltpu.VMEM((GROUP, 4, GRAD_LANES), F32),
            pltpu.VMEM((GROUP, 4, GRAD_LANES), F32),
            dma((8,)), dma((8,)), dma((5, 8)), dma((5, 8)),
            dma((6, 2)), dma((6, 2)), dma((3,)), dma((3,)),
        ],
        compiler_params=pltpu.CompilerParams(
            collective_id=0, has_side_effects=True, vmem_limit_bytes=40 * 1024 * 1024
        ),
    )(img, cot, w0, wm, wt, params)
    rows = grads.reshape(CH, GRAD_LANES)
    grad_mid = jnp.stack([rows[:, 0:TAPS], rows[:, 640 : 640 + TAPS]])
    return (
        act.transpose(1, 0, 2),
        rows[:, 1280 : 1280 + 147].reshape(stem_weight.shape),
        grad_mid.reshape(mid_weight.shape),
        gains,
        shifts,
    )


def solution(mesh):
    return jax.shard_map(
        shards,
        mesh=mesh,
        in_specs=(P(None, "row", "col"), P(None, "row", "col"), P(), P(), P(), P()),
        out_specs=(P(None, "row", "col"), P(), P(), P(), P()),
        check_vma=False,
    )
```

```python
import jax
import jax.numpy as jnp
from jax import lax
from jax.experimental import pallas as pl
from jax.experimental.pallas import tpu as pltpu
from jax.sharding import PartitionSpec as P

EPS = 1e-05
MESH = pl.DeviceIdType.MESH
F32 = jnp.float32
BF16 = jnp.bfloat16

CH = 64
ROWS = 8
COLS = 256
TAPS = 9 * CH
LOCAL = ROWS * COLS
PIXELS = 524288.0
CHIPS = 128
PLANE = 32
DEPTH = 8
STEM_ROWS = 21


def dot(a, b):
    return jnp.dot(a, b, preferred_element_type=F32)


def dot_nt(a, b):
    return lax.dot_general(a, b, (((1,), (1,)), ((), ())), preferred_element_type=F32)


def hops(offset):
    return sum(min(d, n - d) for d, n in zip(offset, (4, 4, 8)))


CHIP_OFFSETS = sorted(
    ((dy, dx, dz) for dy in range(4) for dx in range(4) for dz in range(8) if dy or dx or dz),
    key=lambda offset: -hops(offset),
)
PLANE_OFFSETS = sorted(
    ((dy, dx, dc) for dy in range(4) for dx in range(4) for dc in range(2) if dy or dx or dc),
    key=lambda offset: -hops((offset[0], offset[1], 0)),
)
DEPTH_OFFSETS = (4, 3, 5, 2, 6, 1, 7)


def kernel(
    img, cot, w0_in, wm_in, gains_in, shifts_in,
    act_out, stem_out, mid_out, gains_out, shifts_out,
    cot_raw, w0_raw, wm_raw, norm_raw, w0_flat, wm, wt, cot_flat, cot_rows, act_rows, choose,
    tiles, sel, patches, wbig, x0, x1, dmap, dstem,
    pre, white, slope, up, rowhalo, colsend, colrecv,
    ar_a, ar_b, gsend, grecv, gdepth, gfull, ssend, srecv, sdepth, sfull, rows_full,
    in_sem, img_send, img_recv, halo_send, halo_recv, ar_send, ar_recv, fin_send, fin_recv,
):
    row, col = lax.axis_index("row"), lax.axis_index("col")
    chip_x, chip_z, core = col // 16, (col // 2) % 8, col % 2
    not_top = jnp.where(row == 0, 0.0, 1.0).astype(F32)
    not_bottom = jnp.where(row == 3, 0.0, 1.0).astype(F32)
    not_left = jnp.where(col == 0, 0.0, 1.0).astype(F32)
    not_right = jnp.where(col == 63, 0.0, 1.0).astype(F32)
    chip_rank = (row * 4 + chip_x) * 8 + chip_z
    plane_rank = (row * 4 + chip_x) * 2 + core

    def device(y, x, z, c):
        return (y, x * 16 + z * 2 + c)

    other_core = device(row, chip_x, chip_z, 1 - core)

    def chip_peer(offset):
        dy, dx, dz = offset
        return device((row + dy) % 4, (chip_x + dx) % 4, (chip_z + dz) % 8, core)

    def plane_peer(offset):
        dy, dx, dc = offset
        y, x, c = (row + dy) % 4, (chip_x + dx) % 4, (core + dc) % 2
        return (y * 4 + x) * 2 + c, device(y, x, chip_z, c)

    def near(dr, dc):
        return ((row + dr + 4) % 4, (col + dc + 64) % 64)

    around = [(1, 0), (-1, 0), (0, 1), (0, -1), (1, 1), (1, -1), (-1, 1), (-1, -1)]

    barrier = pltpu.get_barrier_semaphore()

    def greet(where):
        pl.semaphore_signal(barrier, inc=1, device_id=where, device_id_type=MESH)

    for offset in CHIP_OFFSETS:
        greet(chip_peer(offset))
    for offset in PLANE_OFFSETS:
        if offset[2]:
            greet(plane_peer(offset)[1])
    for dr, dc in around:
        greet(near(dr, dc))

    loads = [
        pltpu.make_async_copy(src, dst, in_sem.at[n])
        for n, (src, dst) in enumerate(
            (
                (img, tiles.at[48:96, 128:640]),
                (w0_in, w0_raw),
                (wm_in, wm_raw),
                (gains_in, norm_raw.at[0]),
                (shifts_in, norm_raw.at[1]),
                (cot, cot_raw),
            )
        )
    ]
    for load in loads:
        load.start()

    def steps(v, edges):
        return sum(jnp.where(v >= e, 1, 0) for e in edges)

    src = lax.broadcasted_iota(jnp.int32, (512, 256), 0)
    dst = lax.broadcasted_iota(jnp.int32, (1, 256), 1)
    dst_q, dst_b = dst // 8, dst % 8
    dst_a = steps(dst_q, range(3, 21, 3))
    dst_c = dst_q - 3 * dst_a
    place = jnp.where((dst_b < 7) & (dst_q < 21), CH * dst_b + STEM_ROWS * dst_c + dst_a, -1)
    choose[...] = jnp.where(src == place, 1.0, 0.0).astype(BF16)
    diff = lax.broadcasted_iota(jnp.int32, (768, 384), 0) - 2 * lax.broadcasted_iota(
        jnp.int32, (768, 384), 1
    )
    sel[0] = jnp.where(diff == 124, 1.0, 0.0).astype(BF16)
    sel[1] = jnp.where(diff == 125, 1.0, 0.0).astype(BF16)

    m = lax.broadcasted_iota(jnp.int32, (64, 144), 0)
    n = lax.broadcasted_iota(jnp.int32, (64, 144), 1)
    m_c = steps(m, (21, 42, 63))
    m_r = m - 21 * m_c
    n_t = steps(n, (48, 96))
    n_in = n - 48 * n_t
    n_c = steps(n_in, (16, 32))
    n_r = 16 * n_t + n_in - 16 * n_c
    pick = jnp.where((m_c == n_c) & (n_r == m_r + 13), 1.0, 0.0).astype(BF16)

    w0_flat[...] = jnp.zeros(w0_flat.shape, F32)
    gsend[...] = jnp.zeros(gsend.shape, F32)
    for load in loads:
        load.wait()

    for k in range(21):
        w0_flat[8 * k : 8 * k + 7, 0:CH] = w0_raw[k].astype(F32)
    w0 = dot_nt(w0_flat[...].T[0:CH, :].astype(BF16), choose[...])
    for i in range(ROWS):
        wbig[CH * i : CH * (i + 1), :] = (pltpu.roll(w0, 2 * i, 1) if i else w0).astype(BF16)
    for layer in range(2):
        taps = [wm_raw[9 * layer + t].astype(F32) for t in range(9)]
        turned = [taps[8 - t].T for t in range(9)]
        for source, target in ((taps, wm), (turned, wt)):
            for t in range(0, 9, 2):
                part = source[t : t + 2]
                value = jnp.concatenate(part, axis=1) if len(part) == 2 else part[0]
                target[layer, :, CH * t : CH * (t + len(part))] = value.astype(BF16)
    w0_flat[0:3, 0:CH] = norm_raw[0]
    w0_flat[8:11, 0:CH] = norm_raw[1]
    columns = w0_flat[0:16, :].T
    gain = [columns[0:CH, k : k + 1] for k in range(3)]
    shift = [columns[0:CH, 8 + k : 9 + k] for k in range(3)]

    pl.semaphore_wait(barrier, len(CHIP_OFFSETS) + 16 + len(around))

    copies = []
    for n, (dr, dc) in enumerate(around):
        span = slice(128, 640) if dc == 0 else (slice(512, 640) if dc == 1 else slice(128, 256))
        lanes = slice(128, 640) if dc == 0 else (slice(0, 128) if dc == 1 else slice(640, 768))
        first = 48 * (1 - dr)
        copies.append(
            pltpu.make_async_remote_copy(
                src_ref=tiles.at[48:96, span],
                dst_ref=tiles.at[first : first + 48, lanes],
                send_sem=img_send.at[n],
                recv_sem=img_recv.at[n],
                device_id=near(dr, dc),
                device_id_type=MESH,
            )
        )
    for copy in copies:
        copy.start()
    for copy in copies:
        copy.wait()

    def scale_tile(rows, lanes, factor):
        tiles[rows, lanes] = (tiles[rows, lanes].astype(F32) * factor).astype(BF16)

    scale_tile(slice(0, 48), slice(0, 768), not_top)
    scale_tile(slice(96, 144), slice(0, 768), not_bottom)
    scale_tile(slice(0, 144), slice(0, 128), not_left)
    scale_tile(slice(0, 144), slice(640, 768), not_right)

    image_rows = dot(pick, tiles[...]).astype(BF16)
    planes = [dot(image_rows, sel[0]), dot(image_rows, sel[1])]
    for b in range(7):
        shift_by = (b - 3) // 2 + 2
        plane = planes[(b - 3) % 2]
        moved = pltpu.roll(plane, 384 - shift_by, 1) if shift_by else plane
        patches[CH * b : CH * (b + 1), :] = moved[:, 0:COLS].astype(BF16)
    patches[448:512, :] = jnp.zeros((64, COLS), BF16)

    lane128 = lax.broadcasted_iota(jnp.int32, (CH, 128), 1)
    lane256 = lax.broadcasted_iota(jnp.int32, (CH, COLS), 1)
    lane1 = lax.broadcasted_iota(jnp.int32, (1, 128), 1)

    def fold(v):
        return v[:, 0:128] + v[:, 128:256]

    def to_row(first, second):
        both = jnp.where(lane128 == 0, first, jnp.where(lane128 == 1, second, 0.0)).T
        return jnp.concatenate([both[0:1, :], both[1:2, :]], axis=1)

    def to_columns(row_value):
        turned = jnp.broadcast_to(row_value, (8, 128)).T
        return turned[0:CH, 0:1], turned[CH : 2 * CH, 0:1]

    def drain(buf, count, sem):
        part = buf.at[0:count]
        pltpu.make_async_copy(part, part, sem).wait()

    def send(src, dst, send_sem, recv_sem, where):
        pltpu.make_async_remote_copy(
            src_ref=src,
            dst_ref=dst,
            send_sem=send_sem,
            recv_sem=recv_sem,
            device_id=where,
            device_id_type=MESH,
        ).start()

    def exchange(index, value, combine, meanwhile):
        buf, sems = ar_a.at[index], (ar_send.at[index, 0], ar_recv.at[index, 0])
        buf[pl.ds(core, 1)] = value[None]
        send(buf.at[core], buf.at[core], *sems, other_core)
        drain(buf, 1, sems[1])
        value = combine(buf[...], float(LOCAL))
        drain(buf, 1, sems[0])
        buf, sems = ar_b.at[index], (ar_send.at[index, 1], ar_recv.at[index, 1])
        buf[pl.ds(chip_rank, 1)] = value[None]
        for offset in CHIP_OFFSETS:
            send(buf.at[chip_rank], buf.at[chip_rank], *sems, chip_peer(offset))
        meanwhile()
        drain(buf, CHIPS - 1, sems[1])
        drain(buf, CHIPS - 1, sems[0])
        return combine(buf[...], float(LOCAL * 2))

    def total_of(got):
        if got.shape[0] == CHIPS:
            got = jnp.sum(got.reshape(8, 16, 1, 128), axis=0)
        return jnp.sum(got, axis=0)

    def combine_moments(got, count):
        total = total_of(got)
        mean = total * (1.0 / got.shape[0])
        off = got - mean[None]
        spread = total_of(off * off) * count
        return jnp.where(lane1 < CH, mean, total + pltpu.roll(spread, CH, 1))

    def combine_sums(got, count):
        return total_of(got)

    def start_halo(index, ref):
        for side, lane in ((0, 0), (1, COLS - 1)):
            pack = jnp.zeros((CH, 128), F32)
            for i in range(ROWS):
                pack = jnp.where(lane128 == i, ref[i, :, lane : lane + 1], pack)
            colsend[index, side] = pack
        started = []
        for n, (dr, dc) in enumerate(around):
            if dc == 0:
                src = ref.at[ROWS - 1 if dr == 1 else 0]
                dst = rowhalo.at[index, 0 if dr == 1 else 1]
            else:
                src = colsend.at[index, 1 if dc == 1 else 0]
                dst = colrecv.at[index, (0 if dc == 1 else 3) + 1 - dr]
            copy = pltpu.make_async_remote_copy(
                src_ref=src,
                dst_ref=dst,
                send_sem=halo_send.at[index, n],
                recv_sem=halo_recv.at[index, n],
                device_id=near(dr, dc),
                device_id_type=MESH,
            )
            copy.start()
            started.append(copy)
        return started

    def build(dst, center, top, bottom, left, right):
        for r in range(ROWS + 2):
            value = top if r == 0 else (bottom if r == ROWS + 1 else center(r - 1))
            place, lane = (0, ROWS - 1) if r == 0 else ((2, 0) if r == ROWS + 1 else (1, r - 1))
            before = jnp.where(lane256 == 0, left[place][:, lane : lane + 1], pltpu.roll(value, 1, 1))
            after = jnp.where(
                lane256 == COLS - 1, right[place][:, lane : lane + 1], pltpu.roll(value, COLS - 1, 1)
            )
            base = 3 * CH * r
            dst[base : base + CH, :] = before.astype(BF16)
            dst[base + CH : base + 2 * CH, :] = value.astype(BF16)
            dst[base + 2 * CH : base + 3 * CH, :] = after.astype(BF16)

    edge = [not_top, 1.0, not_bottom]

    def build_with_halo(dst, center, apply_halo, index):
        top = apply_halo("row", 0) * not_top
        bottom = apply_halo("row", 1) * not_bottom
        left = [apply_halo("col", p) * (edge[p] * not_left) for p in range(3)]
        right = [apply_halo("col", 3 + p) * (edge[p] * not_right) for p in range(3)]
        build(dst, center, top, bottom, left, right)

    def conv(weight, src, out, after=None):
        for i in range(ROWS):
            value = dot(weight, src[3 * CH * i : 3 * CH * i + TAPS, :])
            out[i] = value if after is None else after(i, value)

    def moments(index, meanwhile):
        ref = pre.at[index]
        total = jnp.zeros((CH, 128), F32)
        for i in range(ROWS):
            total = total + fold(ref[i])
        mean = jnp.sum(total, axis=1, keepdims=True) * (1.0 / LOCAL)
        total = jnp.zeros((CH, 128), F32)
        for i in range(ROWS):
            off = ref[i] - mean
            total = total + fold(off * off)
        local = to_row(mean, jnp.sum(total, axis=1, keepdims=True))
        mean, squares = to_columns(exchange(index, local, combine_moments, meanwhile))
        return mean, lax.rsqrt(squares * (1.0 / PIXELS) + EPS)

    def halo_block(index, kind, place):
        return rowhalo[index, place] if kind == "row" else colrecv[index, place]

    mean, inv = [None] * 3, [None] * 3

    def forward_norm(index, meanwhile):
        halo = []

        def shadow():
            halo.extend(start_halo(index, pre.at[index]))
            meanwhile()

        mean[index], inv[index] = moments(index, shadow)
        for copy in halo:
            copy.wait()

    def forward_rows(index, i):
        normed_white = (pre[index, i] - mean[index]) * inv[index]
        white[index, i] = normed_white
        normed = gain[index] * normed_white + shift[index]
        sig = jax.nn.sigmoid(normed)
        slope[index, i] = sig * (1.0 + normed * (1.0 - sig))
        return normed * sig

    def forward_build(index, dst):
        def outside(kind, place):
            block = halo_block(index, kind, place)
            normed = gain[index] * ((block - mean[index]) * inv[index]) + shift[index]
            return normed * jax.nn.sigmoid(normed)

        build_with_halo(dst, lambda i: forward_rows(index, i), outside, index)

    def spread_cotangent():
        cot_flat[...] = cot_raw[...].astype(F32)
        for i in range(ROWS):
            cot_rows[i] = cot_flat[:, i, :]

    def nothing():
        pass

    stem = dot(wbig[...], patches[...])
    for i in range(ROWS):
        pre[0, i] = stem[CH * i : CH * (i + 1), :]
    forward_norm(0, spread_cotangent)
    forward_build(0, x0)
    conv(wm[0], x0, pre.at[1])
    forward_norm(1, nothing)
    forward_build(1, x1)
    conv(wm[1], x1, pre.at[2])
    forward_norm(2, nothing)
    for i in range(ROWS):
        act_rows[i] = forward_rows(2, i)
        up[2, i] = cot_rows[i] * slope[2, i]

    def norm_sums(index, meanwhile):
        shift_total = jnp.zeros((CH, 128), F32)
        gain_total = jnp.zeros((CH, 128), F32)
        for i in range(ROWS):
            shift_total = shift_total + fold(up[index, i])
            gain_total = gain_total + fold(up[index, i] * white[index, i])
        local = to_row(
            jnp.sum(shift_total, axis=1, keepdims=True), jnp.sum(gain_total, axis=1, keepdims=True)
        )
        sums = exchange(3 + index, local, combine_sums, meanwhile)
        shifts_out[index : index + 1, :] = sums[:, 0:CH]
        gains_out[index : index + 1, :] = sums[:, CH : 2 * CH]
        shift_sum, gain_sum = to_columns(sums)
        return shift_sum * (1.0 / PIXELS), gain_sum * (1.0 / PIXELS)

    def down(index, sums, up_value, whitened):
        return (gain[index] * inv[index]) * (up_value - sums[0] - whitened * sums[1])

    def backward_norm(index, halo_index, meanwhile):
        halo = []

        def shadow():
            halo.extend(start_halo(halo_index, up.at[index]))
            meanwhile()

        sums = norm_sums(index, shadow)

        def center(i):
            return down(index, sums, up[index, i], white[index, i])

        def outside(kind, place):
            whitened = (halo_block(index, kind, place) - mean[index]) * inv[index]
            return down(index, sums, halo_block(halo_index, kind, place), whitened)

        for copy in halo:
            copy.wait()
        build_with_halo(dmap, center, outside, index)

    def kernel_grad(src):
        total = jnp.zeros((CH, TAPS), F32)
        for i in range(ROWS):
            base = 3 * CH * (i + 1) + CH
            total = total + dot_nt(dmap[base : base + CH, :], src[3 * CH * i : 3 * CH * i + TAPS, :])
        return total

    def put(buf, value):
        for k in range(PLANE):
            buf[k, :, 0 : value.shape[1]] = value[2 * k : 2 * k + 2, :]

    def scatter(n, mine, got):
        got[pl.ds(plane_rank, 1)] = mine[pl.ds(plane_rank, 1)]
        for offset in PLANE_OFFSETS:
            rank, where = plane_peer(offset)
            send(mine.at[rank], got.at[plane_rank], fin_send.at[n, 0], fin_recv.at[n, 0], where)

    def along_depth(n, got, depth):
        drain(got, PLANE - 1, fin_recv.at[n, 0])
        depth[pl.ds(chip_z, 1)] = jnp.sum(got[...], axis=0)[None]
        for dz in DEPTH_OFFSETS:
            where = device(row, chip_x, (chip_z + dz) % DEPTH, core)
            send(depth.at[chip_z], depth.at[chip_z], fin_send.at[n, 1], fin_recv.at[n, 1], where)

    def spread(n, depth, full):
        drain(depth, DEPTH - 1, fin_recv.at[n, 1])
        full[pl.ds(plane_rank, 1)] = jnp.sum(depth[...], axis=0)[None]
        for offset in PLANE_OFFSETS:
            where = plane_peer(offset)[1]
            send(full.at[plane_rank], full.at[plane_rank], fin_send.at[n, 2], fin_recv.at[n, 2], where)

    def collect(n, full, lanes):
        drain(full, PLANE - 1, fin_recv.at[n, 2])
        for k in range(PLANE):
            rows_full[2 * k : 2 * k + 2, 0:lanes] = full[k]

    def finish_mid(layer):
        collect(layer, gfull.at[layer], 640)
        for t in range(9):
            mid_out[9 * layer + t] = rows_full[:, CH * t : CH * (t + 1)]

    def grad_stage_1(layer, src):
        put(gsend.at[layer], kernel_grad(src))
        scatter(layer, gsend.at[layer], grecv.at[layer])

    def turn_activation():
        for i in range(ROWS):
            cot_flat[:, i, :] = act_rows[i]
        act_out[...] = cot_flat[...].astype(BF16)

    backward_norm(2, 3, turn_activation)
    conv(wt[1], dmap, up.at[1], lambda i, value: value * slope[1, i])
    backward_norm(1, 4, lambda: grad_stage_1(1, x1))
    conv(wt[0], dmap, up.at[0], lambda i, value: value * slope[0, i])
    along_depth(1, grecv.at[1], gdepth.at[1])

    def last_shadow():
        grad_stage_1(0, x0)
        spread(1, gdepth.at[1], gfull.at[1])

    sums = norm_sums(0, last_shadow)
    for i in range(ROWS):
        dstem[CH * i : CH * (i + 1), :] = down(0, sums, up[0, i], white[0, i]).astype(BF16)
    banded = dot_nt(dstem[...], patches[...])
    total = banded[0:CH, :]
    for i in range(1, ROWS):
        total = total + pltpu.roll(banded[CH * i : CH * (i + 1), :], 512 - 2 * i, 1)
    high = total.astype(BF16)
    rest = total - high.astype(F32)
    mid = rest.astype(BF16)
    low = (rest - mid.astype(F32)).astype(BF16)
    put(ssend, dot(high, choose[...]) + dot(mid, choose[...]) + dot(low, choose[...]))
    scatter(2, ssend, srecv)
    along_depth(0, grecv.at[0], gdepth.at[0])
    along_depth(2, srecv, sdepth)
    finish_mid(1)
    spread(0, gdepth.at[0], gfull.at[0])
    spread(2, sdepth, sfull)
    finish_mid(0)
    collect(2, sfull, 256)
    turned = rows_full[:, 0:256].T
    stem_out[...] = turned[0:168, :].reshape(STEM_ROWS, 8, CH)[:, 0:7, :]
    for n, (a, b, c) in enumerate(
        ((gsend.at[0], gdepth.at[0], gfull.at[0]), (gsend.at[1], gdepth.at[1], gfull.at[1]), (ssend, sdepth, sfull))
    ):
        drain(a, PLANE - 1, fin_send.at[n, 0])
        drain(b, DEPTH - 1, fin_send.at[n, 1])
        drain(c, PLANE - 1, fin_send.at[n, 2])


def write_out(*refs):
    sources, results, sems = refs[0:5], refs[5:10], refs[10]
    copies = [pltpu.make_async_copy(a, b, sems.at[n]) for n, (a, b) in enumerate(zip(sources, results))]
    for copy in copies:
        copy.start()
    for copy in copies:
        copy.wait()


def shards(slide_band, cotangent, stem_weight, mid_weight, norm_gains, norm_shifts):
    img = slide_band.reshape(48, 512)
    w0 = stem_weight.transpose(1, 3, 2, 0).reshape(STEM_ROWS, 7, CH)
    wm = mid_weight.transpose(0, 2, 3, 1, 4).reshape(18, CH, CH)
    vmem = pl.BlockSpec(memory_space=pltpu.VMEM)
    hbm = pl.BlockSpec(memory_space=pltpu.HBM)
    dma = pltpu.SemaphoreType.DMA
    shapes = (
        jax.ShapeDtypeStruct((CH, ROWS, COLS), BF16),
        jax.ShapeDtypeStruct((STEM_ROWS, 7, CH), F32),
        jax.ShapeDtypeStruct((18, CH, CH), F32),
        jax.ShapeDtypeStruct((3, CH), F32),
        jax.ShapeDtypeStruct((3, CH), F32),
    )
    results = pl.pallas_call(
        kernel,
        out_shape=shapes,
        in_specs=[hbm] * 6,
        out_specs=(vmem,) * 5,
        scratch_shapes=[
            pltpu.VMEM((CH, ROWS, COLS), BF16),
            pltpu.VMEM((STEM_ROWS, 7, CH), BF16),
            pltpu.VMEM((18, CH, CH), BF16),
            pltpu.VMEM((2, 3, CH), F32),
            pltpu.VMEM((256, 128), F32),
            pltpu.VMEM((2, CH, TAPS), BF16),
            pltpu.VMEM((2, CH, TAPS), BF16),
            pltpu.VMEM((CH, ROWS, COLS), F32),
            pltpu.VMEM((ROWS, CH, COLS), F32),
            pltpu.VMEM((ROWS, CH, COLS), F32),
            pltpu.VMEM((512, 256), BF16),
            pltpu.VMEM((144, 768), BF16),
            pltpu.VMEM((2, 768, 384), BF16),
            pltpu.VMEM((512, COLS), BF16),
            pltpu.VMEM((512, 512), BF16),
            pltpu.VMEM((3 * CH * (ROWS + 2), COLS), BF16),
            pltpu.VMEM((3 * CH * (ROWS + 2), COLS), BF16),
            pltpu.VMEM((3 * CH * (ROWS + 2), COLS), BF16),
            pltpu.VMEM((512, COLS), BF16),
            pltpu.VMEM((3, ROWS, CH, COLS), F32),
            pltpu.VMEM((3, ROWS, CH, COLS), F32),
            pltpu.VMEM((3, ROWS, CH, COLS), F32),
            pltpu.VMEM((3, ROWS, CH, COLS), F32),
            pltpu.VMEM((5, 2, CH, COLS), F32),
            pltpu.VMEM((5, 2, CH, 128), F32),
            pltpu.VMEM((5, 6, CH, 128), F32),
            pltpu.VMEM((6, 2, 1, 128), F32),
            pltpu.VMEM((6, CHIPS, 1, 128), F32),
            pltpu.VMEM((2, PLANE, 2, 640), F32),
            pltpu.VMEM((2, PLANE, 2, 640), F32),
            pltpu.VMEM((2, DEPTH, 2, 640), F32),
            pltpu.VMEM((2, PLANE, 2, 640), F32),
            pltpu.VMEM((PLANE, 2, 256), F32),
            pltpu.VMEM((PLANE, 2, 256), F32),
            pltpu.VMEM((DEPTH, 2, 256), F32),
            pltpu.VMEM((PLANE, 2, 256), F32),
            pltpu.VMEM((CH, 640), F32),
            dma((6,)),
            dma((8,)), dma((8,)), dma((5, 8)), dma((5, 8)),
            dma((6, 2)), dma((6, 2)), dma((3, 3)), dma((3, 3)),
        ],
        compiler_params=pltpu.CompilerParams(
            collective_id=0, has_side_effects=True, vmem_limit_bytes=40 * 1024 * 1024
        ),
    )(img, cotangent, w0, wm, norm_gains, norm_shifts)
    act, stem, mid, gains, shifts = pl.pallas_call(
        write_out,
        out_shape=shapes,
        in_specs=[vmem] * 5,
        out_specs=(hbm,) * 5,
        scratch_shapes=[dma((5,))],
    )(*results)
    return (
        act,
        stem.reshape(7, 3, 7, CH).transpose(3, 0, 2, 1),
        mid.reshape(2, 3, 3, CH, CH).transpose(0, 3, 1, 2, 4),
        gains,
        shifts,
    )


def solution(mesh):
    return jax.shard_map(
        shards,
        mesh=mesh,
        in_specs=(P(None, "row", "col"), P(None, "row", "col"), P(), P(), P(), P()),
        out_specs=(P(None, "row", "col"), P(), P(), P(), P()),
        check_vma=False,
    )
```

```python
import jax
import jax.numpy as jnp
from jax import lax
from jax.experimental import pallas as pl
from jax.experimental.pallas import tpu as pltpu
from jax.sharding import PartitionSpec as P

EPS = 1e-05
MESH = pl.DeviceIdType.MESH
F32 = jnp.float32
BF16 = jnp.bfloat16

CH = 64
ROWS = 8
COLS = 256
TAPS = 9 * CH
LOCAL = ROWS * COLS
PIXELS = 524288.0
CHIPS = 128
VMEM_BYTES = 62 * 1024 * 1024
PLANE = 32
DEPTH = 8
STEM_ROWS = 21


def dot(a, b):
    return jnp.dot(a, b, preferred_element_type=F32)


def dot_nt(a, b):
    return lax.dot_general(a, b, (((1,), (1,)), ((), ())), preferred_element_type=F32)


def hops(offset):
    return sum(min(d, n - d) for d, n in zip(offset, (4, 4, 8)))


CHIP_OFFSETS = sorted(
    ((dy, dx, dz) for dy in range(4) for dx in range(4) for dz in range(8) if dy or dx or dz),
    key=lambda offset: -hops(offset),
)
PLANE_OFFSETS = sorted(
    ((dy, dx, dc) for dy in range(4) for dx in range(4) for dc in range(2) if dy or dx or dc),
    key=lambda offset: -hops((offset[0], offset[1], 0)),
)
DEPTH_OFFSETS = (4, 3, 5, 2, 6, 1, 7)


def kernel(
    img, cot, w0_in, wm_in, gains_in, shifts_in,
    act_hbm, stem_hbm, mid_hbm, gains_hbm, shifts_hbm,
    act_out, stem_out, mid_out, gains_out, shifts_out,
    cot_raw, w0_raw, wm_raw, norm_raw, w0_flat, wm, wt, cot_flat, cot_rows, act_rows, choose,
    tiles, sel, patches, wbig, x0, x1, dmap, dstem,
    pre, white, slope, up, rowhalo, colsend, colrecv,
    ar_a, ar_b, gsend, grecv, gdepth, gfull, ssend, srecv, sdepth, sfull, rows_full,
    in_sem, out_sem, img_send, img_recv, halo_send, halo_recv, ar_send, ar_recv, fin_send, fin_recv,
):
    row, col = lax.axis_index("row"), lax.axis_index("col")
    chip_x, chip_z, core = col // 16, (col // 2) % 8, col % 2
    not_top = jnp.where(row == 0, 0.0, 1.0).astype(F32)
    not_bottom = jnp.where(row == 3, 0.0, 1.0).astype(F32)
    not_left = jnp.where(col == 0, 0.0, 1.0).astype(F32)
    not_right = jnp.where(col == 63, 0.0, 1.0).astype(F32)
    chip_rank = (row * 4 + chip_x) * 8 + chip_z
    plane_rank = (row * 4 + chip_x) * 2 + core

    def device(y, x, z, c):
        return (y, x * 16 + z * 2 + c)

    other_core = device(row, chip_x, chip_z, 1 - core)

    def chip_peer(offset):
        dy, dx, dz = offset
        return device((row + dy) % 4, (chip_x + dx) % 4, (chip_z + dz) % 8, core)

    def plane_peer(offset):
        dy, dx, dc = offset
        y, x, c = (row + dy) % 4, (chip_x + dx) % 4, (core + dc) % 2
        return (y * 4 + x) * 2 + c, device(y, x, chip_z, c)

    def near(dr, dc):
        return ((row + dr + 4) % 4, (col + dc + 64) % 64)

    around = [(1, 0), (-1, 0), (0, 1), (0, -1), (1, 1), (1, -1), (-1, 1), (-1, -1)]

    barrier = pltpu.get_barrier_semaphore()

    def greet(where):
        pl.semaphore_signal(barrier, inc=1, device_id=where, device_id_type=MESH)

    for offset in CHIP_OFFSETS:
        greet(chip_peer(offset))
    for offset in PLANE_OFFSETS:
        if offset[2]:
            greet(plane_peer(offset)[1])
    for dr, dc in around:
        greet(near(dr, dc))

    loads = [
        pltpu.make_async_copy(src, dst, in_sem.at[n])
        for n, (src, dst) in enumerate(
            (
                (img, tiles.at[48:96, 128:640]),
                (w0_in, w0_raw),
                (wm_in, wm_raw),
                (gains_in, norm_raw.at[0]),
                (shifts_in, norm_raw.at[1]),
                (cot, cot_raw),
            )
        )
    ]
    for load in loads:
        load.start()

    def steps(v, edges):
        return sum(jnp.where(v >= e, 1, 0) for e in edges)

    src = lax.broadcasted_iota(jnp.int32, (512, 256), 0)
    dst = lax.broadcasted_iota(jnp.int32, (1, 256), 1)
    dst_q, dst_b = dst // 8, dst % 8
    dst_a = steps(dst_q, range(3, 21, 3))
    dst_c = dst_q - 3 * dst_a
    place = jnp.where((dst_b < 7) & (dst_q < 21), CH * dst_b + STEM_ROWS * dst_c + dst_a, -1)
    choose[...] = jnp.where(src == place, 1.0, 0.0).astype(BF16)
    diff = lax.broadcasted_iota(jnp.int32, (768, 384), 0) - 2 * lax.broadcasted_iota(
        jnp.int32, (768, 384), 1
    )
    sel[0] = jnp.where(diff == 124, 1.0, 0.0).astype(BF16)
    sel[1] = jnp.where(diff == 125, 1.0, 0.0).astype(BF16)

    m = lax.broadcasted_iota(jnp.int32, (64, 144), 0)
    n = lax.broadcasted_iota(jnp.int32, (64, 144), 1)
    m_c = steps(m, (21, 42, 63))
    m_r = m - 21 * m_c
    n_t = steps(n, (48, 96))
    n_in = n - 48 * n_t
    n_c = steps(n_in, (16, 32))
    n_r = 16 * n_t + n_in - 16 * n_c
    pick = jnp.where((m_c == n_c) & (n_r == m_r + 13), 1.0, 0.0).astype(BF16)

    w0_flat[...] = jnp.zeros(w0_flat.shape, F32)
    gsend[...] = jnp.zeros(gsend.shape, F32)
    for load in loads:
        load.wait()

    for k in range(21):
        w0_flat[8 * k : 8 * k + 7, 0:CH] = w0_raw[k].astype(F32)
    w0 = dot_nt(w0_flat[...].T[0:CH, :].astype(BF16), choose[...])
    for i in range(ROWS):
        wbig[CH * i : CH * (i + 1), :] = (pltpu.roll(w0, 2 * i, 1) if i else w0).astype(BF16)
    for layer in range(2):
        taps = [wm_raw[9 * layer + t].astype(F32) for t in range(9)]
        turned = [taps[8 - t].T for t in range(9)]
        for source, target in ((taps, wm), (turned, wt)):
            for t in range(0, 9, 2):
                part = source[t : t + 2]
                value = jnp.concatenate(part, axis=1) if len(part) == 2 else part[0]
                target[layer, :, CH * t : CH * (t + len(part))] = value.astype(BF16)
    w0_flat[0:3, 0:CH] = norm_raw[0]
    w0_flat[8:11, 0:CH] = norm_raw[1]
    columns = w0_flat[0:16, :].T
    gain = [columns[0:CH, k : k + 1] for k in range(3)]
    shift = [columns[0:CH, 8 + k : 9 + k] for k in range(3)]

    pl.semaphore_wait(barrier, len(CHIP_OFFSETS) + 16 + len(around))

    copies = []
    for n, (dr, dc) in enumerate(around):
        span = slice(128, 640) if dc == 0 else (slice(512, 640) if dc == 1 else slice(128, 256))
        lanes = slice(128, 640) if dc == 0 else (slice(0, 128) if dc == 1 else slice(640, 768))
        first = 48 * (1 - dr)
        copies.append(
            pltpu.make_async_remote_copy(
                src_ref=tiles.at[48:96, span],
                dst_ref=tiles.at[first : first + 48, lanes],
                send_sem=img_send.at[n],
                recv_sem=img_recv.at[n],
                device_id=near(dr, dc),
                device_id_type=MESH,
            )
        )
    for copy in copies:
        copy.start()
    for copy in copies:
        copy.wait()

    def scale_tile(rows, lanes, factor):
        tiles[rows, lanes] = (tiles[rows, lanes].astype(F32) * factor).astype(BF16)

    scale_tile(slice(0, 48), slice(0, 768), not_top)
    scale_tile(slice(96, 144), slice(0, 768), not_bottom)
    scale_tile(slice(0, 144), slice(0, 128), not_left)
    scale_tile(slice(0, 144), slice(640, 768), not_right)

    image_rows = dot(pick, tiles[...]).astype(BF16)
    planes = [dot(image_rows, sel[0]), dot(image_rows, sel[1])]
    for b in range(7):
        shift_by = (b - 3) // 2 + 2
        plane = planes[(b - 3) % 2]
        moved = pltpu.roll(plane, 384 - shift_by, 1) if shift_by else plane
        patches[CH * b : CH * (b + 1), :] = moved[:, 0:COLS].astype(BF16)
    patches[448:512, :] = jnp.zeros((64, COLS), BF16)

    lane128 = lax.broadcasted_iota(jnp.int32, (CH, 128), 1)
    lane256 = lax.broadcasted_iota(jnp.int32, (CH, COLS), 1)
    lane1 = lax.broadcasted_iota(jnp.int32, (1, 128), 1)

    def fold(v):
        return v[:, 0:128] + v[:, 128:256]

    def to_row(first, second):
        both = jnp.where(lane128 == 0, first, jnp.where(lane128 == 1, second, 0.0)).T
        return jnp.concatenate([both[0:1, :], both[1:2, :]], axis=1)

    def to_columns(row_value):
        turned = jnp.broadcast_to(row_value, (8, 128)).T
        return turned[0:CH, 0:1], turned[CH : 2 * CH, 0:1]

    def drain(buf, count, sem):
        part = buf.at[0:count]
        pltpu.make_async_copy(part, part, sem).wait()

    def send(src, dst, send_sem, recv_sem, where):
        pltpu.make_async_remote_copy(
            src_ref=src,
            dst_ref=dst,
            send_sem=send_sem,
            recv_sem=recv_sem,
            device_id=where,
            device_id_type=MESH,
        ).start()

    def exchange(index, value, combine, meanwhile):
        buf, sems = ar_a.at[index], (ar_send.at[index, 0], ar_recv.at[index, 0])
        buf[pl.ds(core, 1)] = value[None]
        send(buf.at[core], buf.at[core], *sems, other_core)
        drain(buf, 1, sems[1])
        value = combine(buf[...], float(LOCAL))
        drain(buf, 1, sems[0])
        buf, sems = ar_b.at[index], (ar_send.at[index, 1], ar_recv.at[index, 1])
        buf[pl.ds(chip_rank, 1)] = value[None]
        for offset in CHIP_OFFSETS:
            send(buf.at[chip_rank], buf.at[chip_rank], *sems, chip_peer(offset))
        meanwhile()
        drain(buf, CHIPS - 1, sems[1])
        drain(buf, CHIPS - 1, sems[0])
        return combine(buf[...], float(LOCAL * 2))

    def total_of(got):
        if got.shape[0] == CHIPS:
            got = jnp.sum(got.reshape(8, 16, 1, 128), axis=0)
        return jnp.sum(got, axis=0)

    def combine_moments(got, count):
        total = total_of(got)
        mean = total * (1.0 / got.shape[0])
        off = got - mean[None]
        spread = total_of(off * off) * count
        return jnp.where(lane1 < CH, mean, total + pltpu.roll(spread, CH, 1))

    def combine_sums(got, count):
        return total_of(got)

    def start_halo(index, ref):
        for side, lane in ((0, 0), (1, COLS - 1)):
            pack = jnp.zeros((CH, 128), F32)
            for i in range(ROWS):
                pack = jnp.where(lane128 == i, ref[i, :, lane : lane + 1], pack)
            colsend[index, side] = pack
        started = []
        for n, (dr, dc) in enumerate(around):
            if dc == 0:
                src = ref.at[ROWS - 1 if dr == 1 else 0]
                dst = rowhalo.at[index, 0 if dr == 1 else 1]
            else:
                src = colsend.at[index, 1 if dc == 1 else 0]
                dst = colrecv.at[index, (0 if dc == 1 else 3) + 1 - dr]
            copy = pltpu.make_async_remote_copy(
                src_ref=src,
                dst_ref=dst,
                send_sem=halo_send.at[index, n],
                recv_sem=halo_recv.at[index, n],
                device_id=near(dr, dc),
                device_id_type=MESH,
            )
            copy.start()
            started.append(copy)
        return started

    def build(dst, center, top, bottom, left, right):
        for r in range(ROWS + 2):
            value = top if r == 0 else (bottom if r == ROWS + 1 else center(r - 1))
            place, lane = (0, ROWS - 1) if r == 0 else ((2, 0) if r == ROWS + 1 else (1, r - 1))
            before = jnp.where(lane256 == 0, left[place][:, lane : lane + 1], pltpu.roll(value, 1, 1))
            after = jnp.where(
                lane256 == COLS - 1, right[place][:, lane : lane + 1], pltpu.roll(value, COLS - 1, 1)
            )
            base = 3 * CH * r
            dst[base : base + CH, :] = before.astype(BF16)
            dst[base + CH : base + 2 * CH, :] = value.astype(BF16)
            dst[base + 2 * CH : base + 3 * CH, :] = after.astype(BF16)

    edge = [not_top, 1.0, not_bottom]

    def build_with_halo(dst, center, apply_halo, index):
        top = apply_halo("row", 0) * not_top
        bottom = apply_halo("row", 1) * not_bottom
        left = [apply_halo("col", p) * (edge[p] * not_left) for p in range(3)]
        right = [apply_halo("col", 3 + p) * (edge[p] * not_right) for p in range(3)]
        build(dst, center, top, bottom, left, right)

    def conv(weight, src, out, after=None):
        for i in range(ROWS):
            value = dot(weight, src[3 * CH * i : 3 * CH * i + TAPS, :])
            out[i] = value if after is None else after(i, value)

    def moments(index, meanwhile):
        ref = pre.at[index]
        total = jnp.zeros((CH, 128), F32)
        for i in range(ROWS):
            total = total + fold(ref[i])
        mean = jnp.sum(total, axis=1, keepdims=True) * (1.0 / LOCAL)
        total = jnp.zeros((CH, 128), F32)
        for i in range(ROWS):
            off = ref[i] - mean
            total = total + fold(off * off)
        local = to_row(mean, jnp.sum(total, axis=1, keepdims=True))
        mean, squares = to_columns(exchange(index, local, combine_moments, meanwhile))
        return mean, lax.rsqrt(squares * (1.0 / PIXELS) + EPS)

    def halo_block(index, kind, place):
        return rowhalo[index, place] if kind == "row" else colrecv[index, place]

    mean, inv = [None] * 3, [None] * 3

    def forward_norm(index, meanwhile):
        halo = []

        def shadow():
            halo.extend(start_halo(index, pre.at[index]))
            meanwhile()

        mean[index], inv[index] = moments(index, shadow)
        for copy in halo:
            copy.wait()

    def forward_rows(index, i):
        normed_white = (pre[index, i] - mean[index]) * inv[index]
        white[index, i] = normed_white
        normed = gain[index] * normed_white + shift[index]
        sig = jax.nn.sigmoid(normed)
        slope[index, i] = sig * (1.0 + normed * (1.0 - sig))
        return normed * sig

    def forward_build(index, dst):
        def outside(kind, place):
            block = halo_block(index, kind, place)
            normed = gain[index] * ((block - mean[index]) * inv[index]) + shift[index]
            return normed * jax.nn.sigmoid(normed)

        build_with_halo(dst, lambda i: forward_rows(index, i), outside, index)

    def spread_cotangent():
        cot_flat[...] = cot_raw[...].astype(F32)
        for i in range(ROWS):
            cot_rows[i] = cot_flat[:, i, :]

    def nothing():
        pass

    stem = dot(wbig[...], patches[...])
    for i in range(ROWS):
        pre[0, i] = stem[CH * i : CH * (i + 1), :]
    forward_norm(0, spread_cotangent)
    forward_build(0, x0)
    conv(wm[0], x0, pre.at[1])
    forward_norm(1, nothing)
    forward_build(1, x1)
    conv(wm[1], x1, pre.at[2])
    forward_norm(2, nothing)
    for i in range(ROWS):
        act_rows[i] = forward_rows(2, i)
        up[2, i] = cot_rows[i] * slope[2, i]

    def norm_sums(index, meanwhile):
        shift_total = jnp.zeros((CH, 128), F32)
        gain_total = jnp.zeros((CH, 128), F32)
        for i in range(ROWS):
            shift_total = shift_total + fold(up[index, i])
            gain_total = gain_total + fold(up[index, i] * white[index, i])
        local = to_row(
            jnp.sum(shift_total, axis=1, keepdims=True), jnp.sum(gain_total, axis=1, keepdims=True)
        )
        sums = exchange(3 + index, local, combine_sums, meanwhile)
        shifts_out[index : index + 1, :] = sums[:, 0:CH]
        gains_out[index : index + 1, :] = sums[:, CH : 2 * CH]
        shift_sum, gain_sum = to_columns(sums)
        return shift_sum * (1.0 / PIXELS), gain_sum * (1.0 / PIXELS)

    def down(index, sums, up_value, whitened):
        return (gain[index] * inv[index]) * (up_value - sums[0] - whitened * sums[1])

    def backward_norm(index, halo_index, meanwhile):
        halo = []

        def shadow():
            halo.extend(start_halo(halo_index, up.at[index]))
            meanwhile()

        sums = norm_sums(index, shadow)

        def center(i):
            return down(index, sums, up[index, i], white[index, i])

        def outside(kind, place):
            whitened = (halo_block(index, kind, place) - mean[index]) * inv[index]
            return down(index, sums, halo_block(halo_index, kind, place), whitened)

        for copy in halo:
            copy.wait()
        build_with_halo(dmap, center, outside, index)

    def kernel_grad(src):
        total = jnp.zeros((CH, TAPS), F32)
        for i in range(ROWS):
            base = 3 * CH * (i + 1) + CH
            total = total + dot_nt(dmap[base : base + CH, :], src[3 * CH * i : 3 * CH * i + TAPS, :])
        return total

    def put(buf, value):
        for k in range(PLANE):
            buf[k, :, 0 : value.shape[1]] = value[2 * k : 2 * k + 2, :]

    def scatter(n, mine, got):
        got[pl.ds(plane_rank, 1)] = mine[pl.ds(plane_rank, 1)]
        for offset in PLANE_OFFSETS:
            rank, where = plane_peer(offset)
            send(mine.at[rank], got.at[plane_rank], fin_send.at[n, 0], fin_recv.at[n, 0], where)

    def along_depth(n, got, depth):
        drain(got, PLANE - 1, fin_recv.at[n, 0])
        depth[pl.ds(chip_z, 1)] = jnp.sum(got[...], axis=0)[None]
        for dz in DEPTH_OFFSETS:
            where = device(row, chip_x, (chip_z + dz) % DEPTH, core)
            send(depth.at[chip_z], depth.at[chip_z], fin_send.at[n, 1], fin_recv.at[n, 1], where)

    def spread(n, depth, full):
        drain(depth, DEPTH - 1, fin_recv.at[n, 1])
        full[pl.ds(plane_rank, 1)] = jnp.sum(depth[...], axis=0)[None]
        for offset in PLANE_OFFSETS:
            where = plane_peer(offset)[1]
            send(full.at[plane_rank], full.at[plane_rank], fin_send.at[n, 2], fin_recv.at[n, 2], where)

    def collect(n, full, lanes):
        drain(full, PLANE - 1, fin_recv.at[n, 2])
        for k in range(PLANE):
            rows_full[2 * k : 2 * k + 2, 0:lanes] = full[k]

    leaving = []

    def leave(src, dst):
        copy = pltpu.make_async_copy(src, dst, out_sem.at[len(leaving)])
        copy.start()
        leaving.append(copy)

    def finish_mid(layer):
        collect(layer, gfull.at[layer], 640)
        for t in range(9):
            mid_out[9 * layer + t] = rows_full[:, CH * t : CH * (t + 1)]
        span = pl.ds(9 * layer, 9)
        leave(mid_out.at[span], mid_hbm.at[span])

    def grad_stage_1(layer, src):
        put(gsend.at[layer], kernel_grad(src))
        scatter(layer, gsend.at[layer], grecv.at[layer])

    def turn_activation():
        for i in range(ROWS):
            cot_flat[:, i, :] = act_rows[i]
        act_out[...] = cot_flat[...].astype(BF16)
        leave(act_out, act_hbm)

    backward_norm(2, 3, turn_activation)
    conv(wt[1], dmap, up.at[1], lambda i, value: value * slope[1, i])
    backward_norm(1, 4, lambda: grad_stage_1(1, x1))
    conv(wt[0], dmap, up.at[0], lambda i, value: value * slope[0, i])
    along_depth(1, grecv.at[1], gdepth.at[1])

    def last_shadow():
        grad_stage_1(0, x0)
        spread(1, gdepth.at[1], gfull.at[1])

    sums = norm_sums(0, last_shadow)
    leave(gains_out, gains_hbm)
    leave(shifts_out, shifts_hbm)
    along_depth(0, grecv.at[0], gdepth.at[0])
    for i in range(ROWS):
        dstem[CH * i : CH * (i + 1), :] = down(0, sums, up[0, i], white[0, i]).astype(BF16)
    banded = dot_nt(dstem[...], patches[...])
    total = banded[0:CH, :]
    for i in range(1, ROWS):
        total = total + pltpu.roll(banded[CH * i : CH * (i + 1), :], 512 - 2 * i, 1)
    high = total.astype(BF16)
    rest = total - high.astype(F32)
    mid = rest.astype(BF16)
    low = (rest - mid.astype(F32)).astype(BF16)
    put(ssend, dot(high, choose[...]) + dot(mid, choose[...]) + dot(low, choose[...]))
    scatter(2, ssend, srecv)
    spread(0, gdepth.at[0], gfull.at[0])
    finish_mid(1)
    along_depth(2, srecv, sdepth)
    finish_mid(0)
    spread(2, sdepth, sfull)
    collect(2, sfull, 256)
    turned = rows_full[:, 0:256].T
    stem_out[...] = turned[0:168, :].reshape(STEM_ROWS, 8, CH)[:, 0:7, :]
    leave(stem_out, stem_hbm)
    for n, (a, b, c) in enumerate(
        ((gsend.at[0], gdepth.at[0], gfull.at[0]), (gsend.at[1], gdepth.at[1], gfull.at[1]), (ssend, sdepth, sfull))
    ):
        drain(a, PLANE - 1, fin_send.at[n, 0])
        drain(b, DEPTH - 1, fin_send.at[n, 1])
        drain(c, PLANE - 1, fin_send.at[n, 2])
    for copy in leaving:
        copy.wait()


def write_out(*refs):
    ins, outs, held, sems = refs[0:5], refs[5:10], refs[10:15], refs[15]
    arriving = [pltpu.make_async_copy(a, b, sems.at[0, n]) for n, (a, b) in enumerate(zip(ins, held))]
    leaving = [pltpu.make_async_copy(a, b, sems.at[1, n]) for n, (a, b) in enumerate(zip(held, outs))]
    for copy in arriving:
        copy.start()
    for first, second in zip(arriving, leaving):
        first.wait()
        second.start()
    for copy in leaving:
        copy.wait()


def shards(slide_band, cotangent, stem_weight, mid_weight, norm_gains, norm_shifts):
    img = slide_band.reshape(48, 512)
    w0 = stem_weight.transpose(1, 3, 2, 0).reshape(STEM_ROWS, 7, CH)
    wm = mid_weight.transpose(0, 2, 3, 1, 4).reshape(18, CH, CH)
    hbm = pl.BlockSpec(memory_space=pltpu.HBM)
    dma = pltpu.SemaphoreType.DMA
    shapes = (
        jax.ShapeDtypeStruct((CH, ROWS, COLS), BF16),
        jax.ShapeDtypeStruct((STEM_ROWS, 7, CH), F32),
        jax.ShapeDtypeStruct((18, CH, CH), F32),
        jax.ShapeDtypeStruct((3, CH), F32),
        jax.ShapeDtypeStruct((3, CH), F32),
    )
    results = pl.pallas_call(
        kernel,
        out_shape=shapes,
        in_specs=[hbm] * 6,
        out_specs=(hbm,) * 5,
        scratch_shapes=[
            pltpu.VMEM((CH, ROWS, COLS), BF16),
            pltpu.VMEM((STEM_ROWS, 7, CH), F32),
            pltpu.VMEM((18, CH, CH), F32),
            pltpu.VMEM((3, CH), F32),
            pltpu.VMEM((3, CH), F32),
            pltpu.VMEM((CH, ROWS, COLS), BF16),
            pltpu.VMEM((STEM_ROWS, 7, CH), BF16),
            pltpu.VMEM((18, CH, CH), BF16),
            pltpu.VMEM((2, 3, CH), F32),
            pltpu.VMEM((256, 128), F32),
            pltpu.VMEM((2, CH, TAPS), BF16),
            pltpu.VMEM((2, CH, TAPS), BF16),
            pltpu.VMEM((CH, ROWS, COLS), F32),
            pltpu.VMEM((ROWS, CH, COLS), F32),
            pltpu.VMEM((ROWS, CH, COLS), F32),
            pltpu.VMEM((512, 256), BF16),
            pltpu.VMEM((144, 768), BF16),
            pltpu.VMEM((2, 768, 384), BF16),
            pltpu.VMEM((512, COLS), BF16),
            pltpu.VMEM((512, 512), BF16),
            pltpu.VMEM((3 * CH * (ROWS + 2), COLS), BF16),
            pltpu.VMEM((3 * CH * (ROWS + 2), COLS), BF16),
            pltpu.VMEM((3 * CH * (ROWS + 2), COLS), BF16),
            pltpu.VMEM((512, COLS), BF16),
            pltpu.VMEM((3, ROWS, CH, COLS), F32),
            pltpu.VMEM((3, ROWS, CH, COLS), F32),
            pltpu.VMEM((3, ROWS, CH, COLS), F32),
            pltpu.VMEM((3, ROWS, CH, COLS), F32),
            pltpu.VMEM((5, 2, CH, COLS), F32),
            pltpu.VMEM((5, 2, CH, 128), F32),
            pltpu.VMEM((5, 6, CH, 128), F32),
            pltpu.VMEM((6, 2, 1, 128), F32),
            pltpu.VMEM((6, CHIPS, 1, 128), F32),
            pltpu.VMEM((2, PLANE, 2, 640), F32),
            pltpu.VMEM((2, PLANE, 2, 640), F32),
            pltpu.VMEM((2, DEPTH, 2, 640), F32),
            pltpu.VMEM((2, PLANE, 2, 640), F32),
            pltpu.VMEM((PLANE, 2, 256), F32),
            pltpu.VMEM((PLANE, 2, 256), F32),
            pltpu.VMEM((DEPTH, 2, 256), F32),
            pltpu.VMEM((PLANE, 2, 256), F32),
            pltpu.VMEM((CH, 640), F32),
            dma((6,)), dma((6,)),
            dma((8,)), dma((8,)), dma((5, 8)), dma((5, 8)),
            dma((6, 2)), dma((6, 2)), dma((3, 3)), dma((3, 3)),
        ],
        compiler_params=pltpu.CompilerParams(
            collective_id=0, has_side_effects=True, vmem_limit_bytes=VMEM_BYTES
        ),
    )(img, cotangent, w0, wm, norm_gains, norm_shifts)
    act, stem, mid, gains, shifts = pl.pallas_call(
        write_out,
        out_shape=shapes,
        in_specs=[hbm] * 5,
        out_specs=(hbm,) * 5,
        scratch_shapes=[pltpu.VMEM(a.shape, a.dtype) for a in shapes] + [dma((2, 5))],
        compiler_params=pltpu.CompilerParams(vmem_limit_bytes=VMEM_BYTES),
    )(*results)
    return (
        act,
        stem.reshape(7, 3, 7, CH).transpose(3, 0, 2, 1),
        mid.reshape(2, 3, 3, CH, CH).transpose(0, 3, 1, 2, 4),
        gains,
        shifts,
    )


def solution(mesh):
    return jax.shard_map(
        shards,
        mesh=mesh,
        in_specs=(P(None, "row", "col"), P(None, "row", "col"), P(), P(), P(), P()),
        out_specs=(P(None, "row", "col"), P(), P(), P(), P()),
        check_vma=False,
    )
```

```python
import jax
import jax.numpy as jnp
from jax import lax
from jax.experimental import pallas as pl
from jax.experimental.pallas import tpu as pltpu
from jax.sharding import PartitionSpec as P

EPS = 1e-05
MESH = pl.DeviceIdType.MESH
F32 = jnp.float32
BF16 = jnp.bfloat16

CH = 64
ROWS = 8
COLS = 256
TAPS = 9 * CH
LOCAL = ROWS * COLS
PIXELS = 524288.0
CHIPS = 128
VMEM_BYTES = 62 * 1024 * 1024
PLANE = 32
DEPTH = 8
STEM_ROWS = 21


def dot(a, b):
    return jnp.dot(a, b, preferred_element_type=F32)


def dot_nt(a, b):
    return lax.dot_general(a, b, (((1,), (1,)), ((), ())), preferred_element_type=F32)


def hops(offset):
    return sum(min(d, n - d) for d, n in zip(offset, (4, 4, 8)))


CHIP_OFFSETS = sorted(
    ((dy, dx, dz) for dy in range(4) for dx in range(4) for dz in range(8) if dy or dx or dz),
    key=lambda offset: -hops(offset),
)
PLANE_OFFSETS = sorted(
    ((dy, dx, dc) for dy in range(4) for dx in range(4) for dc in range(2) if dy or dx or dc),
    key=lambda offset: -hops((offset[0], offset[1], 0)),
)
DEPTH_OFFSETS = (4, 3, 5, 2, 6, 1, 7)


def kernel(
    img, cot, w0_in, wm_in, gains_in, shifts_in,
    act_hbm, stem_hbm, mid_hbm, gains_hbm, shifts_hbm,
    act_out, stem_out, mid_out, gains_out, shifts_out,
    cot_raw, w0_raw, wm_raw, norm_raw, w0_flat, wm, wt, cot_flat, cot_rows, act_rows, choose,
    tiles, sel, patches, wbig, x0, x1, dmap, dstem,
    pre, white, slope, up, rowhalo, colsend, colrecv,
    first_a, first_b, ar_a, ar_b, gsend, grecv, gdepth, gfull, ssend, srecv, sdepth, sfull, rows_full,
    in_sem, out_sem, img_send, img_recv, halo_send, halo_recv, ar_send, ar_recv, fin_send, fin_recv,
):
    row, col = lax.axis_index("row"), lax.axis_index("col")
    chip_x, chip_z, core = col // 16, (col // 2) % 8, col % 2
    not_top = jnp.where(row == 0, 0.0, 1.0).astype(F32)
    not_bottom = jnp.where(row == 3, 0.0, 1.0).astype(F32)
    not_left = jnp.where(col == 0, 0.0, 1.0).astype(F32)
    not_right = jnp.where(col == 63, 0.0, 1.0).astype(F32)
    chip_rank = (row * 4 + chip_x) * 8 + chip_z
    plane_rank = (row * 4 + chip_x) * 2 + core

    def device(y, x, z, c):
        return (y, x * 16 + z * 2 + c)

    other_core = device(row, chip_x, chip_z, 1 - core)

    def chip_peer(offset):
        dy, dx, dz = offset
        return device((row + dy) % 4, (chip_x + dx) % 4, (chip_z + dz) % 8, core)

    def plane_peer(offset):
        dy, dx, dc = offset
        y, x, c = (row + dy) % 4, (chip_x + dx) % 4, (core + dc) % 2
        return (y * 4 + x) * 2 + c, device(y, x, chip_z, c)

    def near(dr, dc):
        return ((row + dr + 4) % 4, (col + dc + 64) % 64)

    around = [(1, 0), (-1, 0), (0, 1), (0, -1), (1, 1), (1, -1), (-1, 1), (-1, -1)]

    barrier = pltpu.get_barrier_semaphore()

    def greet(where):
        pl.semaphore_signal(barrier, inc=1, device_id=where, device_id_type=MESH)

    loads = [
        pltpu.make_async_copy(src, dst, in_sem.at[n])
        for n, (src, dst) in enumerate(
            (
                (img, tiles.at[48:96, 128:640]),
                (w0_in, w0_raw),
                (wm_in, wm_raw),
                (gains_in, norm_raw.at[0]),
                (shifts_in, norm_raw.at[1]),
                (cot, cot_raw),
            )
        )
    ]
    for load in loads:
        load.start()
    for dr, dc in around:
        greet(near(dr, dc))
    for offset in PLANE_OFFSETS:
        greet(plane_peer(offset)[1])
    for dz in DEPTH_OFFSETS:
        greet(device(row, chip_x, (chip_z + dz) % DEPTH, core))


    loads[0].wait()
    pl.semaphore_wait(barrier, len(around) + len(PLANE_OFFSETS) + len(DEPTH_OFFSETS))

    copies = []
    for n, (dr, dc) in enumerate(around):
        span = slice(128, 640) if dc == 0 else (slice(512, 640) if dc == 1 else slice(128, 256))
        lanes = slice(128, 640) if dc == 0 else (slice(0, 128) if dc == 1 else slice(640, 768))
        first = 48 * (1 - dr)
        copies.append(
            pltpu.make_async_remote_copy(
                src_ref=tiles.at[48:96, span],
                dst_ref=tiles.at[first : first + 48, lanes],
                send_sem=img_send.at[n],
                recv_sem=img_recv.at[n],
                device_id=near(dr, dc),
                device_id_type=MESH,
            )
        )
    for copy in copies:
        copy.start()

    def steps(v, edges):
        return sum(jnp.where(v >= e, 1, 0) for e in edges)

    src = lax.broadcasted_iota(jnp.int32, (512, 256), 0)
    dst = lax.broadcasted_iota(jnp.int32, (1, 256), 1)
    dst_q, dst_b = dst // 8, dst % 8
    dst_a = steps(dst_q, range(3, 21, 3))
    dst_c = dst_q - 3 * dst_a
    place = jnp.where((dst_b < 7) & (dst_q < 21), CH * dst_b + STEM_ROWS * dst_c + dst_a, -1)
    choose[...] = jnp.where(src == place, 1.0, 0.0).astype(BF16)
    diff = lax.broadcasted_iota(jnp.int32, (768, 384), 0) - 2 * lax.broadcasted_iota(
        jnp.int32, (768, 384), 1
    )
    sel[0] = jnp.where(diff == 124, 1.0, 0.0).astype(BF16)
    sel[1] = jnp.where(diff == 125, 1.0, 0.0).astype(BF16)

    m = lax.broadcasted_iota(jnp.int32, (64, 144), 0)
    n = lax.broadcasted_iota(jnp.int32, (64, 144), 1)
    m_c = steps(m, (21, 42, 63))
    m_r = m - 21 * m_c
    n_t = steps(n, (48, 96))
    n_in = n - 48 * n_t
    n_c = steps(n_in, (16, 32))
    n_r = 16 * n_t + n_in - 16 * n_c
    pick = jnp.where((m_c == n_c) & (n_r == m_r + 13), 1.0, 0.0).astype(BF16)

    w0_flat[...] = jnp.zeros(w0_flat.shape, F32)
    for load in loads[1:]:
        load.wait()

    for k in range(21):
        w0_flat[8 * k : 8 * k + 7, 0:CH] = w0_raw[k].astype(F32)
    w0 = dot_nt(w0_flat[...].T[0:CH, :].astype(BF16), choose[...])
    for i in range(ROWS):
        wbig[CH * i : CH * (i + 1), :] = (pltpu.roll(w0, 2 * i, 1) if i else w0).astype(BF16)
    w0_flat[0:3, 0:CH] = norm_raw[0]
    w0_flat[8:11, 0:CH] = norm_raw[1]
    columns = w0_flat[0:16, :].T
    gain = [columns[0:CH, k : k + 1] for k in range(3)]
    shift = [columns[0:CH, 8 + k : 9 + k] for k in range(3)]

    for copy in copies:
        copy.wait()

    def scale_tile(rows, lanes, factor):
        tiles[rows, lanes] = (tiles[rows, lanes].astype(F32) * factor).astype(BF16)

    scale_tile(slice(0, 48), slice(0, 768), not_top)
    scale_tile(slice(96, 144), slice(0, 768), not_bottom)
    scale_tile(slice(0, 144), slice(0, 128), not_left)
    scale_tile(slice(0, 144), slice(640, 768), not_right)

    image_rows = dot(pick, tiles[...]).astype(BF16)
    planes = [dot(image_rows, sel[0]), dot(image_rows, sel[1])]
    for b in range(7):
        shift_by = (b - 3) // 2 + 2
        plane = planes[(b - 3) % 2]
        moved = pltpu.roll(plane, 384 - shift_by, 1) if shift_by else plane
        patches[CH * b : CH * (b + 1), :] = moved[:, 0:COLS].astype(BF16)
    patches[448:512, :] = jnp.zeros((64, COLS), BF16)

    lane128 = lax.broadcasted_iota(jnp.int32, (CH, 128), 1)
    lane256 = lax.broadcasted_iota(jnp.int32, (CH, COLS), 1)
    lane1 = lax.broadcasted_iota(jnp.int32, (1, 128), 1)

    def fold(v):
        return v[:, 0:128] + v[:, 128:256]

    def to_row(first, second):
        both = jnp.where(lane128 == 0, first, jnp.where(lane128 == 1, second, 0.0)).T
        return jnp.concatenate([both[0:1, :], both[1:2, :]], axis=1)

    def to_columns(row_value):
        turned = jnp.broadcast_to(row_value, (8, 128)).T
        return turned[0:CH, 0:1], turned[CH : 2 * CH, 0:1]

    def drain(buf, count, sem):
        part = buf.at[0:count]
        pltpu.make_async_copy(part, part, sem).wait()

    def send(src, dst, send_sem, recv_sem, where):
        pltpu.make_async_remote_copy(
            src_ref=src,
            dst_ref=dst,
            send_sem=send_sem,
            recv_sem=recv_sem,
            device_id=where,
            device_id_type=MESH,
        ).start()

    def exchange(index, value, combine, meanwhile):
        if index == 0:
            return first_exchange(value, combine, meanwhile)
        buf, sems = ar_a.at[index], (ar_send.at[index, 0], ar_recv.at[index, 0])
        buf[pl.ds(core, 1)] = value[None]
        send(buf.at[core], buf.at[core], *sems, other_core)
        drain(buf, 1, sems[1])
        value = combine(buf[...], float(LOCAL))
        drain(buf, 1, sems[0])
        buf, sems = ar_b.at[index], (ar_send.at[index, 1], ar_recv.at[index, 1])
        buf[pl.ds(chip_rank, 1)] = value[None]
        for offset in CHIP_OFFSETS:
            send(buf.at[chip_rank], buf.at[chip_rank], *sems, chip_peer(offset))
        meanwhile()
        drain(buf, CHIPS - 1, sems[1])
        drain(buf, CHIPS - 1, sems[0])
        return combine(buf[...], float(LOCAL * 2))

    def first_exchange(value, combine, meanwhile):
        sems = (ar_send.at[0, 0], ar_recv.at[0, 0])
        first_a[pl.ds(plane_rank, 1)] = value[None]
        for offset in PLANE_OFFSETS:
            send(first_a.at[plane_rank], first_a.at[plane_rank], *sems, plane_peer(offset)[1])
        meanwhile()
        drain(first_a, PLANE - 1, sems[1])
        drain(first_a, PLANE - 1, sems[0])
        value = combine(first_a[...], float(LOCAL))
        sems = (ar_send.at[0, 1], ar_recv.at[0, 1])
        first_b[pl.ds(chip_z, 1)] = value[None]
        for dz in DEPTH_OFFSETS:
            where = device(row, chip_x, (chip_z + dz) % DEPTH, core)
            send(first_b.at[chip_z], first_b.at[chip_z], *sems, where)
        drain(first_b, DEPTH - 1, sems[1])
        drain(first_b, DEPTH - 1, sems[0])
        return combine(first_b[...], float(LOCAL * PLANE))

    def total_of(got):
        if got.shape[0] == CHIPS:
            got = jnp.sum(got.reshape(8, 16, 1, 128), axis=0)
        return jnp.sum(got, axis=0)

    def combine_moments(got, count):
        total = total_of(got)
        mean = total * (1.0 / got.shape[0])
        off = got - mean[None]
        spread = total_of(off * off) * count
        return jnp.where(lane1 < CH, mean, total + pltpu.roll(spread, CH, 1))

    def combine_sums(got, count):
        return total_of(got)

    def start_halo(index, ref):
        for side, lane in ((0, 0), (1, COLS - 1)):
            pack = jnp.zeros((CH, 128), F32)
            for i in range(ROWS):
                pack = jnp.where(lane128 == i, ref[i, :, lane : lane + 1], pack)
            pack = jnp.concatenate([pack, jnp.zeros((128 - CH, 128), F32)], axis=0)
            colsend[index, side] = pack.T[0:ROWS, :]
        started = []
        for n, (dr, dc) in enumerate(around):
            if dc == 0:
                src = ref.at[ROWS - 1 if dr == 1 else 0]
                dst = rowhalo.at[index, 0 if dr == 1 else 1]
            else:
                src = colsend.at[index, 1 if dc == 1 else 0]
                dst = colrecv.at[index, (0 if dc == 1 else 3) + 1 - dr]
            copy = pltpu.make_async_remote_copy(
                src_ref=src,
                dst_ref=dst,
                send_sem=halo_send.at[index, n],
                recv_sem=halo_recv.at[index, n],
                device_id=near(dr, dc),
                device_id_type=MESH,
            )
            copy.start()
            started.append(copy)
        return started

    def build(dst, center, top, bottom, sides):
        for r in range(ROWS + 2):
            value = top if r == 0 else (bottom if r == ROWS + 1 else center(r - 1))
            lane = ROWS - 1 if r == 0 else (2 * ROWS if r == ROWS + 1 else ROWS + r - 1)
            before = jnp.where(lane256 == 0, sides[:, lane : lane + 1], pltpu.roll(value, 1, 1))
            lane += 3 * ROWS
            after = jnp.where(
                lane256 == COLS - 1, sides[:, lane : lane + 1], pltpu.roll(value, COLS - 1, 1)
            )
            base = 3 * CH * r
            dst[base : base + CH, :] = before.astype(BF16)
            dst[base + CH : base + 2 * CH, :] = value.astype(BF16)
            dst[base + 2 * CH : base + 3 * CH, :] = after.astype(BF16)

    lane48 = lax.broadcasted_iota(jnp.int32, (1, 6 * ROWS), 1)
    edge = jnp.where(lane48 < 3 * ROWS, not_left, not_right)
    in_side = jnp.where(lane48 < 3 * ROWS, lane48, lane48 - 3 * ROWS)
    edge = edge * jnp.where(in_side < ROWS, not_top, jnp.where(in_side < 2 * ROWS, 1.0, not_bottom))

    def build_with_halo(dst, center, apply_halo, index):
        top = apply_halo("row", 0) * not_top
        bottom = apply_halo("row", 1) * not_bottom
        build(dst, center, top, bottom, apply_halo("col", None) * edge)

    def conv(weight, src, out, after=None):
        for i in range(ROWS):
            value = dot(weight, src[3 * CH * i : 3 * CH * i + TAPS, :])
            out[i] = value if after is None else after(i, value)

    def moments(index, meanwhile):
        ref = pre.at[index]
        total = jnp.zeros((CH, 128), F32)
        for i in range(ROWS):
            total = total + fold(ref[i])
        mean = jnp.sum(total, axis=1, keepdims=True) * (1.0 / LOCAL)
        total = jnp.zeros((CH, 128), F32)
        for i in range(ROWS):
            off = ref[i] - mean
            total = total + fold(off * off)
        local = to_row(mean, jnp.sum(total, axis=1, keepdims=True))
        mean, squares = to_columns(exchange(index, local, combine_moments, meanwhile))
        return mean, lax.rsqrt(squares * (1.0 / PIXELS) + EPS)

    def halo_block(index, kind, place):
        if kind == "row":
            return rowhalo[index, place]
        return colrecv[index].reshape(6 * ROWS, 128).T[0:CH, :]

    mean, inv = [None] * 3, [None] * 3

    def forward_norm(index, meanwhile):
        halo = []

        def shadow():
            halo.extend(start_halo(index, pre.at[index]))
            meanwhile()

        mean[index], inv[index] = moments(index, shadow)
        for copy in halo:
            copy.wait()

    def forward_rows(index, i):
        normed_white = (pre[index, i] - mean[index]) * inv[index]
        white[index, i] = normed_white
        normed = gain[index] * normed_white + shift[index]
        sig = jax.nn.sigmoid(normed)
        slope[index, i] = sig * (1.0 + normed * (1.0 - sig))
        return normed * sig

    def forward_build(index, dst):
        def outside(kind, place):
            block = halo_block(index, kind, place)
            normed = gain[index] * ((block - mean[index]) * inv[index]) + shift[index]
            return normed * jax.nn.sigmoid(normed)

        build_with_halo(dst, lambda i: forward_rows(index, i), outside, index)

    def taps_of(layer):
        return [wm_raw[9 * layer + t].astype(F32) for t in range(9)]

    def lay_taps(parts, target):
        for t in range(0, 9, 2):
            part = parts[t : t + 2]
            value = jnp.concatenate(part, axis=1) if len(part) == 2 else part[0]
            target[:, CH * t : CH * (t + len(part))] = value.astype(BF16)

    def lay_weights():
        for layer in range(2):
            lay_taps(taps_of(layer), wm.at[layer])

    def lay_turned():
        gsend[...] = jnp.zeros(gsend.shape, F32)
        for layer in range(2):
            parts = taps_of(layer)
            lay_taps([parts[8 - t].T for t in range(9)], wt.at[layer])

    def spread_cotangent():
        cot_flat[...] = cot_raw[...].astype(F32)
        for i in range(ROWS):
            cot_rows[i] = cot_flat[:, i, :]

    stem = dot(wbig[...], patches[...])
    for i in range(ROWS):
        pre[0, i] = stem[CH * i : CH * (i + 1), :]
    forward_norm(0, lay_weights)
    forward_build(0, x0)
    conv(wm[0], x0, pre.at[1])
    forward_norm(1, spread_cotangent)
    forward_build(1, x1)
    conv(wm[1], x1, pre.at[2])
    forward_norm(2, lay_turned)
    for i in range(ROWS):
        act_rows[i] = forward_rows(2, i)
        up[2, i] = cot_rows[i] * slope[2, i]

    def norm_sums(index, meanwhile):
        shift_total = jnp.zeros((CH, 128), F32)
        gain_total = jnp.zeros((CH, 128), F32)
        for i in range(ROWS):
            shift_total = shift_total + fold(up[index, i])
            gain_total = gain_total + fold(up[index, i] * white[index, i])
        local = to_row(
            jnp.sum(shift_total, axis=1, keepdims=True), jnp.sum(gain_total, axis=1, keepdims=True)
        )
        sums = exchange(3 + index, local, combine_sums, meanwhile)
        shifts_out[index : index + 1, :] = sums[:, 0:CH]
        gains_out[index : index + 1, :] = sums[:, CH : 2 * CH]
        shift_sum, gain_sum = to_columns(sums)
        return shift_sum * (1.0 / PIXELS), gain_sum * (1.0 / PIXELS)

    def down(index, sums, up_value, whitened):
        return (gain[index] * inv[index]) * (up_value - sums[0] - whitened * sums[1])

    def backward_norm(index, halo_index, meanwhile):
        halo = []

        def shadow():
            halo.extend(start_halo(halo_index, up.at[index]))
            meanwhile()

        sums = norm_sums(index, shadow)

        def center(i):
            return down(index, sums, up[index, i], white[index, i])

        def outside(kind, place):
            whitened = (halo_block(index, kind, place) - mean[index]) * inv[index]
            return down(index, sums, halo_block(halo_index, kind, place), whitened)

        for copy in halo:
            copy.wait()
        build_with_halo(dmap, center, outside, index)

    def kernel_grad(src):
        total = jnp.zeros((CH, TAPS), F32)
        for i in range(ROWS):
            base = 3 * CH * (i + 1) + CH
            total = total + dot_nt(dmap[base : base + CH, :], src[3 * CH * i : 3 * CH * i + TAPS, :])
        return total

    def put(buf, value):
        for k in range(PLANE):
            buf[k, :, 0 : value.shape[1]] = value[2 * k : 2 * k + 2, :]

    def scatter(n, mine, got):
        got[pl.ds(plane_rank, 1)] = mine[pl.ds(plane_rank, 1)]
        for offset in PLANE_OFFSETS:
            rank, where = plane_peer(offset)
            send(mine.at[rank], got.at[plane_rank], fin_send.at[n, 0], fin_recv.at[n, 0], where)

    def along_depth(n, got, depth):
        drain(got, PLANE - 1, fin_recv.at[n, 0])
        depth[pl.ds(chip_z, 1)] = jnp.sum(got[...], axis=0)[None]
        for dz in DEPTH_OFFSETS:
            where = device(row, chip_x, (chip_z + dz) % DEPTH, core)
            send(depth.at[chip_z], depth.at[chip_z], fin_send.at[n, 1], fin_recv.at[n, 1], where)

    def spread(n, depth, full):
        drain(depth, DEPTH - 1, fin_recv.at[n, 1])
        full[pl.ds(plane_rank, 1)] = jnp.sum(depth[...], axis=0)[None]
        for offset in PLANE_OFFSETS:
            where = plane_peer(offset)[1]
            send(full.at[plane_rank], full.at[plane_rank], fin_send.at[n, 2], fin_recv.at[n, 2], where)

    def collect(n, full, lanes):
        drain(full, PLANE - 1, fin_recv.at[n, 2])
        for k in range(PLANE):
            rows_full[2 * k : 2 * k + 2, 0:lanes] = full[k]

    leaving = []

    def leave(src, dst):
        copy = pltpu.make_async_copy(src, dst, out_sem.at[len(leaving)])
        copy.start()
        leaving.append(copy)

    def finish_mid(layer):
        collect(layer, gfull.at[layer], 640)
        for t in range(9):
            mid_out[9 * layer + t] = rows_full[:, CH * t : CH * (t + 1)]
        span = pl.ds(9 * layer, 9)
        leave(mid_out.at[span], mid_hbm.at[span])

    def grad_stage_1(layer, src):
        put(gsend.at[layer], kernel_grad(src))
        scatter(layer, gsend.at[layer], grecv.at[layer])

    def turn_activation():
        for i in range(ROWS):
            cot_flat[:, i, :] = act_rows[i]
        act_out[...] = cot_flat[...].astype(BF16)
        leave(act_out, act_hbm)

    backward_norm(2, 3, turn_activation)
    conv(wt[1], dmap, up.at[1], lambda i, value: value * slope[1, i])
    backward_norm(1, 4, lambda: grad_stage_1(1, x1))
    conv(wt[0], dmap, up.at[0], lambda i, value: value * slope[0, i])
    along_depth(1, grecv.at[1], gdepth.at[1])

    sums = norm_sums(0, lambda: grad_stage_1(0, x0))
    leave(gains_out, gains_hbm)
    leave(shifts_out, shifts_hbm)
    for i in range(ROWS):
        dstem[CH * i : CH * (i + 1), :] = down(0, sums, up[0, i], white[0, i]).astype(BF16)
    banded = dot_nt(dstem[...], patches[...])
    total = banded[0:CH, :]
    for i in range(1, ROWS):
        total = total + pltpu.roll(banded[CH * i : CH * (i + 1), :], 512 - 2 * i, 1)
    high = total.astype(BF16)
    rest = total - high.astype(F32)
    mid = rest.astype(BF16)
    low = (rest - mid.astype(F32)).astype(BF16)
    put(ssend, dot(high, choose[...]) + dot(mid, choose[...]) + dot(low, choose[...]))
    scatter(2, ssend, srecv)
    along_depth(0, grecv.at[0], gdepth.at[0])
    spread(1, gdepth.at[1], gfull.at[1])
    along_depth(2, srecv, sdepth)
    spread(0, gdepth.at[0], gfull.at[0])
    finish_mid(1)
    spread(2, sdepth, sfull)
    finish_mid(0)
    collect(2, sfull, 256)
    turned = rows_full[:, 0:256].T
    stem_out[...] = turned[0:168, :].reshape(STEM_ROWS, 8, CH)[:, 0:7, :]
    leave(stem_out, stem_hbm)
    for n, (a, b, c) in enumerate(
        ((gsend.at[0], gdepth.at[0], gfull.at[0]), (gsend.at[1], gdepth.at[1], gfull.at[1]), (ssend, sdepth, sfull))
    ):
        drain(a, PLANE - 1, fin_send.at[n, 0])
        drain(b, DEPTH - 1, fin_send.at[n, 1])
        drain(c, PLANE - 1, fin_send.at[n, 2])
    for copy in leaving:
        copy.wait()


def write_out(*refs):
    ins, outs, held, sems = refs[0:5], refs[5:10], refs[10:15], refs[15]
    arriving = [pltpu.make_async_copy(a, b, sems.at[0, n]) for n, (a, b) in enumerate(zip(ins, held))]
    leaving = [pltpu.make_async_copy(a, b, sems.at[1, n]) for n, (a, b) in enumerate(zip(held, outs))]
    for copy in arriving:
        copy.start()
    for first, second in zip(arriving, leaving):
        first.wait()
        second.start()
    for copy in leaving:
        copy.wait()


def shards(slide_band, cotangent, stem_weight, mid_weight, norm_gains, norm_shifts):
    img = slide_band.reshape(48, 512)
    w0 = stem_weight.transpose(1, 3, 2, 0).reshape(STEM_ROWS, 7, CH)
    wm = mid_weight.transpose(0, 2, 3, 1, 4).reshape(18, CH, CH)
    hbm = pl.BlockSpec(memory_space=pltpu.HBM)
    dma = pltpu.SemaphoreType.DMA
    shapes = (
        jax.ShapeDtypeStruct((CH, ROWS, COLS), BF16),
        jax.ShapeDtypeStruct((STEM_ROWS, 7, CH), F32),
        jax.ShapeDtypeStruct((18, CH, CH), F32),
        jax.ShapeDtypeStruct((3, CH), F32),
        jax.ShapeDtypeStruct((3, CH), F32),
    )
    results = pl.pallas_call(
        kernel,
        out_shape=shapes,
        in_specs=[hbm] * 6,
        out_specs=(hbm,) * 5,
        scratch_shapes=[
            pltpu.VMEM((CH, ROWS, COLS), BF16),
            pltpu.VMEM((STEM_ROWS, 7, CH), F32),
            pltpu.VMEM((18, CH, CH), F32),
            pltpu.VMEM((3, CH), F32),
            pltpu.VMEM((3, CH), F32),
            pltpu.VMEM((CH, ROWS, COLS), BF16),
            pltpu.VMEM((STEM_ROWS, 7, CH), BF16),
            pltpu.VMEM((18, CH, CH), BF16),
            pltpu.VMEM((2, 3, CH), F32),
            pltpu.VMEM((256, 128), F32),
            pltpu.VMEM((2, CH, TAPS), BF16),
            pltpu.VMEM((2, CH, TAPS), BF16),
            pltpu.VMEM((CH, ROWS, COLS), F32),
            pltpu.VMEM((ROWS, CH, COLS), F32),
            pltpu.VMEM((ROWS, CH, COLS), F32),
            pltpu.VMEM((512, 256), BF16),
            pltpu.VMEM((144, 768), BF16),
            pltpu.VMEM((2, 768, 384), BF16),
            pltpu.VMEM((512, COLS), BF16),
            pltpu.VMEM((512, 512), BF16),
            pltpu.VMEM((3 * CH * (ROWS + 2), COLS), BF16),
            pltpu.VMEM((3 * CH * (ROWS + 2), COLS), BF16),
            pltpu.VMEM((3 * CH * (ROWS + 2), COLS), BF16),
            pltpu.VMEM((512, COLS), BF16),
            pltpu.VMEM((3, ROWS, CH, COLS), F32),
            pltpu.VMEM((3, ROWS, CH, COLS), F32),
            pltpu.VMEM((3, ROWS, CH, COLS), F32),
            pltpu.VMEM((3, ROWS, CH, COLS), F32),
            pltpu.VMEM((5, 2, CH, COLS), F32),
            pltpu.VMEM((5, 2, ROWS, 128), F32),
            pltpu.VMEM((5, 6, ROWS, 128), F32),
            pltpu.VMEM((PLANE, 1, 128), F32),
            pltpu.VMEM((DEPTH, 1, 128), F32),
            pltpu.VMEM((6, 2, 1, 128), F32),
            pltpu.VMEM((6, CHIPS, 1, 128), F32),
            pltpu.VMEM((2, PLANE, 2, 640), F32),
            pltpu.VMEM((2, PLANE, 2, 640), F32),
            pltpu.VMEM((2, DEPTH, 2, 640), F32),
            pltpu.VMEM((2, PLANE, 2, 640), F32),
            pltpu.VMEM((PLANE, 2, 256), F32),
            pltpu.VMEM((PLANE, 2, 256), F32),
            pltpu.VMEM((DEPTH, 2, 256), F32),
            pltpu.VMEM((PLANE, 2, 256), F32),
            pltpu.VMEM((CH, 640), F32),
            dma((6,)), dma((6,)),
            dma((8,)), dma((8,)), dma((5, 8)), dma((5, 8)),
            dma((6, 2)), dma((6, 2)), dma((3, 3)), dma((3, 3)),
        ],
        compiler_params=pltpu.CompilerParams(
            collective_id=0, has_side_effects=True, vmem_limit_bytes=VMEM_BYTES
        ),
    )(img, cotangent, w0, wm, norm_gains, norm_shifts)
    act, stem, mid, gains, shifts = pl.pallas_call(
        write_out,
        out_shape=shapes,
        in_specs=[hbm] * 5,
        out_specs=(hbm,) * 5,
        scratch_shapes=[pltpu.VMEM(a.shape, a.dtype) for a in shapes] + [dma((2, 5))],
        compiler_params=pltpu.CompilerParams(vmem_limit_bytes=VMEM_BYTES),
    )(*results)
    return (
        act,
        stem.reshape(7, 3, 7, CH).transpose(3, 0, 2, 1),
        mid.reshape(2, 3, 3, CH, CH).transpose(0, 3, 1, 2, 4),
        gains,
        shifts,
    )


def solution(mesh):
    return jax.shard_map(
        shards,
        mesh=mesh,
        in_specs=(P(None, "row", "col"), P(None, "row", "col"), P(), P(), P(), P()),
        out_specs=(P(None, "row", "col"), P(), P(), P(), P()),
        check_vma=False,
    )
```

```python
import jax
import jax.numpy as jnp
from jax import lax
from jax.experimental import pallas as pl
from jax.experimental.pallas import tpu as pltpu
from jax.sharding import PartitionSpec as P

EPS = 1e-05
MESH = pl.DeviceIdType.MESH
F32 = jnp.float32
BF16 = jnp.bfloat16

CH = 64
ROWS = 8
COLS = 256
TAPS = 9 * CH
LOCAL = ROWS * COLS
PIXELS = 524288.0
CHIPS = 128
VMEM_BYTES = 62 * 1024 * 1024
PLANE = 32
DEPTH = 8
STEM_ROWS = 21


def dot(a, b):
    return jnp.dot(a, b, preferred_element_type=F32)


def dot_nt(a, b):
    return lax.dot_general(a, b, (((1,), (1,)), ((), ())), preferred_element_type=F32)


def hops(offset):
    return sum(min(d, n - d) for d, n in zip(offset, (4, 4, 8)))


CHIP_OFFSETS = sorted(
    ((dy, dx, dz) for dy in range(4) for dx in range(4) for dz in range(8) if dy or dx or dz),
    key=lambda offset: -hops(offset),
)
PLANE_OFFSETS = sorted(
    ((dy, dx, dc) for dy in range(4) for dx in range(4) for dc in range(2) if dy or dx or dc),
    key=lambda offset: -hops((offset[0], offset[1], 0)),
)
DEPTH_OFFSETS = (4, 3, 5, 2, 6, 1, 7)


def kernel(
    img, cot, w0_in, wm_in, gains_in, shifts_in,
    act_hbm, stem_hbm, mid_hbm, gains_hbm, shifts_hbm,
    act_out, stem_out, mid_out, gains_out, shifts_out,
    cot_raw, w0_raw, wm_raw, norm_raw, w0_flat, wm, wt, cot_flat, cot_rows, act_rows, choose,
    tiles, sel, patches, wbig, x0, x1, dmap, dstem,
    pre, white, slope, up, rowhalo, colsend, colrecv,
    first_a, first_b, ar_a, ar_b, gsend, grecv, gdepth, gfull, ssend, srecv, sdepth, sfull, rows_full,
    in_sem, out_sem, img_send, img_recv, halo_send, halo_recv, ar_send, ar_recv, fin_send, fin_recv,
):
    row, col = lax.axis_index("row"), lax.axis_index("col")
    chip_x, chip_z, core = lax.div(col, 16), lax.rem(lax.div(col, 2), 8), lax.rem(col, 2)
    not_top = jnp.where(row == 0, 0.0, 1.0).astype(F32)
    not_bottom = jnp.where(row == 3, 0.0, 1.0).astype(F32)
    not_left = jnp.where(col == 0, 0.0, 1.0).astype(F32)
    not_right = jnp.where(col == 63, 0.0, 1.0).astype(F32)
    chip_rank = (row * 4 + chip_x) * 8 + chip_z
    plane_rank = (row * 4 + chip_x) * 2 + core

    ring_y = [row] + [lax.rem(row + d, 4) for d in range(1, 4)]
    ring_x = [chip_x] + [lax.rem(chip_x + d, 4) for d in range(1, 4)]
    ring_z = [2 * chip_z + core] + [2 * lax.rem(chip_z + d, 8) + core for d in range(1, 8)]
    ring_core = [core, 1 - core]
    col_x = [16 * x for x in ring_x]
    col_core = [2 * chip_z + c for c in ring_core]
    other_core = (row, col_x[0] + col_core[1])

    def chip_peer(offset):
        dy, dx, dz = offset
        return (ring_y[dy], col_x[dx] + ring_z[dz])

    def plane_peer(offset):
        dy, dx, dc = offset
        return 8 * ring_y[dy] + 2 * ring_x[dx] + ring_core[dc], (ring_y[dy], col_x[dx] + col_core[dc])

    def depth_peer(dz):
        return (row, col_x[0] + ring_z[dz])

    def near(dr, dc):
        return (lax.rem(row + dr + 4, 4), lax.rem(col + dc + 64, 64))

    around = [(1, 0), (-1, 0), (0, 1), (0, -1), (1, 1), (1, -1), (-1, 1), (-1, -1)]

    barrier = pltpu.get_barrier_semaphore()

    def greet(where):
        pl.semaphore_signal(barrier, inc=1, device_id=where, device_id_type=MESH)

    loads = [
        pltpu.make_async_copy(src, dst, in_sem.at[n])
        for n, (src, dst) in enumerate(
            (
                (img, tiles.at[48:96, 128:640]),
                (w0_in, w0_raw),
                (wm_in, wm_raw),
                (gains_in, norm_raw.at[0]),
                (shifts_in, norm_raw.at[1]),
                (cot, cot_raw),
            )
        )
    ]
    for load in loads:
        load.start()
    for dr, dc in around:
        greet(near(dr, dc))
    for offset in PLANE_OFFSETS:
        greet(plane_peer(offset)[1])
    for dz in DEPTH_OFFSETS:
        greet(depth_peer(dz))


    loads[0].wait()
    pl.semaphore_wait(barrier, len(around) + len(PLANE_OFFSETS) + len(DEPTH_OFFSETS))

    copies = []
    for n, (dr, dc) in enumerate(around):
        span = slice(128, 640) if dc == 0 else (slice(512, 640) if dc == 1 else slice(128, 256))
        lanes = slice(128, 640) if dc == 0 else (slice(0, 128) if dc == 1 else slice(640, 768))
        first = 48 * (1 - dr)
        copies.append(
            pltpu.make_async_remote_copy(
                src_ref=tiles.at[48:96, span],
                dst_ref=tiles.at[first : first + 48, lanes],
                send_sem=img_send.at[n],
                recv_sem=img_recv.at[n],
                device_id=near(dr, dc),
                device_id_type=MESH,
            )
        )
    for copy in copies:
        copy.start()

    def steps(v, edges):
        return sum(jnp.where(v >= e, 1, 0) for e in edges)

    src = lax.broadcasted_iota(jnp.int32, (512, 256), 0)
    dst = lax.broadcasted_iota(jnp.int32, (1, 256), 1)
    dst_q, dst_b = dst // 8, dst % 8
    dst_a = steps(dst_q, range(3, 21, 3))
    dst_c = dst_q - 3 * dst_a
    place = jnp.where((dst_b < 7) & (dst_q < 21), CH * dst_b + STEM_ROWS * dst_c + dst_a, -1)
    choose[...] = jnp.where(src == place, 1.0, 0.0).astype(BF16)
    diff = lax.broadcasted_iota(jnp.int32, (768, 384), 0) - 2 * lax.broadcasted_iota(
        jnp.int32, (768, 384), 1
    )
    sel[0] = jnp.where(diff == 124, 1.0, 0.0).astype(BF16)
    sel[1] = jnp.where(diff == 125, 1.0, 0.0).astype(BF16)

    m = lax.broadcasted_iota(jnp.int32, (64, 144), 0)
    n = lax.broadcasted_iota(jnp.int32, (64, 144), 1)
    m_c = steps(m, (21, 42, 63))
    m_r = m - 21 * m_c
    n_t = steps(n, (48, 96))
    n_in = n - 48 * n_t
    n_c = steps(n_in, (16, 32))
    n_r = 16 * n_t + n_in - 16 * n_c
    pick = jnp.where((m_c == n_c) & (n_r == m_r + 13), 1.0, 0.0).astype(BF16)

    w0_flat[...] = jnp.zeros(w0_flat.shape, F32)
    for load in loads[1:]:
        load.wait()

    for k in range(21):
        w0_flat[8 * k : 8 * k + 7, 0:CH] = w0_raw[k].astype(F32)
    w0 = dot_nt(w0_flat[...].T[0:CH, :].astype(BF16), choose[...])
    for i in range(ROWS):
        wbig[CH * i : CH * (i + 1), :] = (pltpu.roll(w0, 2 * i, 1) if i else w0).astype(BF16)
    w0_flat[0:3, 0:CH] = norm_raw[0]
    w0_flat[8:11, 0:CH] = norm_raw[1]
    columns = w0_flat[0:16, :].T
    gain = [columns[0:CH, k : k + 1] for k in range(3)]
    shift = [columns[0:CH, 8 + k : 9 + k] for k in range(3)]

    for copy in copies:
        copy.wait()

    def scale_tile(rows, lanes, factor):
        tiles[rows, lanes] = (tiles[rows, lanes].astype(F32) * factor).astype(BF16)

    scale_tile(slice(0, 48), slice(0, 768), not_top)
    scale_tile(slice(96, 144), slice(0, 768), not_bottom)
    scale_tile(slice(0, 144), slice(0, 128), not_left)
    scale_tile(slice(0, 144), slice(640, 768), not_right)

    image_rows = dot(pick, tiles[...]).astype(BF16)
    planes = [dot(image_rows, sel[0]), dot(image_rows, sel[1])]
    for b in range(7):
        shift_by = (b - 3) // 2 + 2
        plane = planes[(b - 3) % 2]
        moved = pltpu.roll(plane, 384 - shift_by, 1) if shift_by else plane
        patches[CH * b : CH * (b + 1), :] = moved[:, 0:COLS].astype(BF16)
    patches[448:512, :] = jnp.zeros((64, COLS), BF16)

    lane128 = lax.broadcasted_iota(jnp.int32, (CH, 128), 1)
    lane256 = lax.broadcasted_iota(jnp.int32, (CH, COLS), 1)
    lane1 = lax.broadcasted_iota(jnp.int32, (1, 128), 1)

    def fold(v):
        return v[:, 0:128] + v[:, 128:256]

    def to_row(first, second):
        both = jnp.where(lane128 == 0, first, jnp.where(lane128 == 1, second, 0.0)).T
        return jnp.concatenate([both[0:1, :], both[1:2, :]], axis=1)

    def to_columns(row_value):
        turned = jnp.broadcast_to(row_value, (8, 128)).T
        return turned[0:CH, 0:1], turned[CH : 2 * CH, 0:1]

    def drain(buf, count, sem):
        part = buf.at[0:count]
        pltpu.make_async_copy(part, part, sem).wait()

    def send(src, dst, send_sem, recv_sem, where):
        pltpu.make_async_remote_copy(
            src_ref=src,
            dst_ref=dst,
            send_sem=send_sem,
            recv_sem=recv_sem,
            device_id=where,
            device_id_type=MESH,
        ).start()

    def exchange(index, value, combine, before, within, meanwhile):
        if index == 0:
            return first_exchange(value, combine, before, within, meanwhile)
        buf, sems = ar_a.at[index], (ar_send.at[index, 0], ar_recv.at[index, 0])
        buf[pl.ds(core, 1)] = value[None]
        send(buf.at[core], buf.at[core], *sems, other_core)
        before()
        drain(buf, 1, sems[1])
        value = combine(buf[...], float(LOCAL))
        drain(buf, 1, sems[0])
        buf, sems = ar_b.at[index], (ar_send.at[index, 1], ar_recv.at[index, 1])
        buf[pl.ds(chip_rank, 1)] = value[None]
        for place, offset in enumerate(CHIP_OFFSETS):
            if hops(offset) == 3 and hops(CHIP_OFFSETS[place - 1]) == 4:
                within()
            send(buf.at[chip_rank], buf.at[chip_rank], *sems, chip_peer(offset))
        meanwhile()
        drain(buf, CHIPS - 1, sems[1])
        drain(buf, CHIPS - 1, sems[0])
        return combine(buf[...], float(LOCAL * 2))

    def first_exchange(value, combine, before, within, meanwhile):
        sems = (ar_send.at[0, 0], ar_recv.at[0, 0])
        first_a[pl.ds(plane_rank, 1)] = value[None]
        for offset in PLANE_OFFSETS:
            send(first_a.at[plane_rank], first_a.at[plane_rank], *sems, plane_peer(offset)[1])
        before()
        within()
        meanwhile()
        drain(first_a, PLANE - 1, sems[1])
        drain(first_a, PLANE - 1, sems[0])
        value = combine(first_a[...], float(LOCAL))
        sems = (ar_send.at[0, 1], ar_recv.at[0, 1])
        first_b[pl.ds(chip_z, 1)] = value[None]
        for dz in DEPTH_OFFSETS:
            where = depth_peer(dz)
            send(first_b.at[chip_z], first_b.at[chip_z], *sems, where)
        drain(first_b, DEPTH - 1, sems[1])
        drain(first_b, DEPTH - 1, sems[0])
        return combine(first_b[...], float(LOCAL * PLANE))

    def total_of(got):
        if got.shape[0] == CHIPS:
            got = jnp.sum(got.reshape(8, 16, 1, 128), axis=0)
        return jnp.sum(got, axis=0)

    def combine_moments(got, count):
        total = total_of(got)
        mean = total * (1.0 / got.shape[0])
        off = got - mean[None]
        spread = total_of(off * off) * count
        return jnp.where(lane1 < CH, mean, total + pltpu.roll(spread, CH, 1))

    def combine_sums(got, count):
        return total_of(got)

    def pack_halo(index, ref):
        for side, lane in ((0, 0), (1, COLS - 1)):
            pack = jnp.zeros((CH, 128), F32)
            for i in range(ROWS):
                pack = jnp.where(lane128 == i, ref[i, :, lane : lane + 1], pack)
            pack = jnp.concatenate([pack, jnp.zeros((128 - CH, 128), F32)], axis=0)
            colsend[index, side] = pack.T[0:ROWS, :]

    def send_halo(index, ref):
        started = []
        for n, (dr, dc) in enumerate(around):
            if dc == 0:
                src = ref.at[ROWS - 1 if dr == 1 else 0]
                dst = rowhalo.at[index, 0 if dr == 1 else 1]
            else:
                src = colsend.at[index, 1 if dc == 1 else 0]
                dst = colrecv.at[index, (0 if dc == 1 else 3) + 1 - dr]
            copy = pltpu.make_async_remote_copy(
                src_ref=src,
                dst_ref=dst,
                send_sem=halo_send.at[index, n],
                recv_sem=halo_recv.at[index, n],
                device_id=near(dr, dc),
                device_id_type=MESH,
            )
            copy.start()
            started.append(copy)
        return started

    def build(dst, center, top, bottom, sides):
        for r in range(ROWS + 2):
            value = top if r == 0 else (bottom if r == ROWS + 1 else center(r - 1))
            lane = ROWS - 1 if r == 0 else (2 * ROWS if r == ROWS + 1 else ROWS + r - 1)
            before = jnp.where(lane256 == 0, sides[:, lane : lane + 1], pltpu.roll(value, 1, 1))
            lane += 3 * ROWS
            after = jnp.where(
                lane256 == COLS - 1, sides[:, lane : lane + 1], pltpu.roll(value, COLS - 1, 1)
            )
            base = 3 * CH * r
            dst[base : base + CH, :] = before.astype(BF16)
            dst[base + CH : base + 2 * CH, :] = value.astype(BF16)
            dst[base + 2 * CH : base + 3 * CH, :] = after.astype(BF16)

    lane48 = lax.broadcasted_iota(jnp.int32, (1, 6 * ROWS), 1)
    edge = jnp.where(lane48 < 3 * ROWS, not_left, not_right)
    in_side = jnp.where(lane48 < 3 * ROWS, lane48, lane48 - 3 * ROWS)
    edge = edge * jnp.where(in_side < ROWS, not_top, jnp.where(in_side < 2 * ROWS, 1.0, not_bottom))

    def build_with_halo(dst, center, apply_halo, index):
        top = apply_halo("row", 0) * not_top
        bottom = apply_halo("row", 1) * not_bottom
        build(dst, center, top, bottom, apply_halo("col", None) * edge)

    def conv(weight, src, out, after=None):
        for i in range(ROWS):
            value = dot(weight, src[3 * CH * i : 3 * CH * i + TAPS, :])
            out[i] = value if after is None else after(i, value)

    def moments(index, *hidden):
        ref = pre.at[index]
        total = jnp.zeros((CH, 128), F32)
        for i in range(ROWS):
            total = total + fold(ref[i])
        mean = jnp.sum(total, axis=1, keepdims=True) * (1.0 / LOCAL)
        total = jnp.zeros((CH, 128), F32)
        for i in range(ROWS):
            off = ref[i] - mean
            total = total + fold(off * off)
        local = to_row(mean, jnp.sum(total, axis=1, keepdims=True))
        mean, squares = to_columns(exchange(index, local, combine_moments, *hidden))
        return mean, lax.rsqrt(squares * (1.0 / PIXELS) + EPS)

    def halo_block(index, kind, place):
        if kind == "row":
            return rowhalo[index, place]
        return colrecv[index].reshape(6 * ROWS, 128).T[0:CH, :]

    mean, inv = [None] * 3, [None] * 3

    def forward_norm(index, meanwhile):
        halo, ref = [], pre.at[index]
        mean[index], inv[index] = moments(
            index,
            lambda: pack_halo(index, ref),
            lambda: halo.extend(send_halo(index, ref)),
            meanwhile,
        )
        for copy in halo:
            copy.wait()

    def forward_rows(index, i):
        normed_white = (pre[index, i] - mean[index]) * inv[index]
        white[index, i] = normed_white
        normed = gain[index] * normed_white + shift[index]
        sig = jax.nn.sigmoid(normed)
        slope[index, i] = sig * (1.0 + normed * (1.0 - sig))
        return normed * sig

    def forward_build(index, dst):
        def outside(kind, place):
            block = halo_block(index, kind, place)
            normed = gain[index] * ((block - mean[index]) * inv[index]) + shift[index]
            return normed * jax.nn.sigmoid(normed)

        build_with_halo(dst, lambda i: forward_rows(index, i), outside, index)

    def taps_of(layer):
        return [wm_raw[9 * layer + t].astype(F32) for t in range(9)]

    def lay_taps(parts, target):
        for t in range(0, 9, 2):
            part = parts[t : t + 2]
            value = jnp.concatenate(part, axis=1) if len(part) == 2 else part[0]
            target[:, CH * t : CH * (t + len(part))] = value.astype(BF16)

    def lay_weights():
        for layer in range(2):
            lay_taps(taps_of(layer), wm.at[layer])

    def lay_turned():
        gsend[...] = jnp.zeros(gsend.shape, F32)
        for layer in range(2):
            parts = taps_of(layer)
            lay_taps([parts[8 - t].T for t in range(9)], wt.at[layer])

    def spread_cotangent():
        cot_flat[...] = cot_raw[...].astype(F32)
        for i in range(ROWS):
            cot_rows[i] = cot_flat[:, i, :]

    stem = dot(wbig[...], patches[...])
    for i in range(ROWS):
        pre[0, i] = stem[CH * i : CH * (i + 1), :]
    forward_norm(0, lay_weights)
    forward_build(0, x0)
    conv(wm[0], x0, pre.at[1])
    forward_norm(1, spread_cotangent)
    forward_build(1, x1)
    conv(wm[1], x1, pre.at[2])
    forward_norm(2, lay_turned)
    for i in range(ROWS):
        act_rows[i] = forward_rows(2, i)
        up[2, i] = cot_rows[i] * slope[2, i]

    def norm_sums(index, *hidden):
        shift_total = jnp.zeros((CH, 128), F32)
        gain_total = jnp.zeros((CH, 128), F32)
        for i in range(ROWS):
            shift_total = shift_total + fold(up[index, i])
            gain_total = gain_total + fold(up[index, i] * white[index, i])
        local = to_row(
            jnp.sum(shift_total, axis=1, keepdims=True), jnp.sum(gain_total, axis=1, keepdims=True)
        )
        sums = exchange(3 + index, local, combine_sums, *hidden)
        shifts_out[index : index + 1, :] = sums[:, 0:CH]
        gains_out[index : index + 1, :] = sums[:, CH : 2 * CH]
        shift_sum, gain_sum = to_columns(sums)
        return shift_sum * (1.0 / PIXELS), gain_sum * (1.0 / PIXELS)

    def down(index, sums, up_value, whitened):
        return (gain[index] * inv[index]) * (up_value - sums[0] - whitened * sums[1])

    def backward_norm(index, halo_index, meanwhile):
        halo, ref = [], up.at[index]
        sums = norm_sums(
            index,
            lambda: pack_halo(halo_index, ref),
            lambda: halo.extend(send_halo(halo_index, ref)),
            meanwhile,
        )

        def center(i):
            return down(index, sums, up[index, i], white[index, i])

        def outside(kind, place):
            whitened = (halo_block(index, kind, place) - mean[index]) * inv[index]
            return down(index, sums, halo_block(halo_index, kind, place), whitened)

        for copy in halo:
            copy.wait()
        build_with_halo(dmap, center, outside, index)

    def kernel_grad(src):
        total = jnp.zeros((CH, TAPS), F32)
        for i in range(ROWS):
            base = 3 * CH * (i + 1) + CH
            total = total + dot_nt(dmap[base : base + CH, :], src[3 * CH * i : 3 * CH * i + TAPS, :])
        return total

    def put(buf, value):
        for k in range(PLANE):
            buf[k, :, 0 : value.shape[1]] = value[2 * k : 2 * k + 2, :]

    def scatter(n, mine, got):
        got[pl.ds(plane_rank, 1)] = mine[pl.ds(plane_rank, 1)]
        for offset in PLANE_OFFSETS:
            rank, where = plane_peer(offset)
            send(mine.at[rank], got.at[plane_rank], fin_send.at[n, 0], fin_recv.at[n, 0], where)

    def along_depth(n, got, depth):
        drain(got, PLANE - 1, fin_recv.at[n, 0])
        depth[pl.ds(chip_z, 1)] = jnp.sum(got[...], axis=0)[None]
        for dz in DEPTH_OFFSETS:
            where = depth_peer(dz)
            send(depth.at[chip_z], depth.at[chip_z], fin_send.at[n, 1], fin_recv.at[n, 1], where)

    def spread(n, depth, full):
        drain(depth, DEPTH - 1, fin_recv.at[n, 1])
        full[pl.ds(plane_rank, 1)] = jnp.sum(depth[...], axis=0)[None]
        for offset in PLANE_OFFSETS:
            where = plane_peer(offset)[1]
            send(full.at[plane_rank], full.at[plane_rank], fin_send.at[n, 2], fin_recv.at[n, 2], where)

    def collect(n, full, lanes):
        drain(full, PLANE - 1, fin_recv.at[n, 2])
        for k in range(PLANE):
            rows_full[2 * k : 2 * k + 2, 0:lanes] = full[k]

    leaving = []

    def leave(src, dst):
        copy = pltpu.make_async_copy(src, dst, out_sem.at[len(leaving)])
        copy.start()
        leaving.append(copy)

    def finish_mid(layer):
        collect(layer, gfull.at[layer], 640)
        for t in range(9):
            mid_out[9 * layer + t] = rows_full[:, CH * t : CH * (t + 1)]
        span = pl.ds(9 * layer, 9)
        leave(mid_out.at[span], mid_hbm.at[span])

    def grad_stage_1(layer, src):
        put(gsend.at[layer], kernel_grad(src))
        scatter(layer, gsend.at[layer], grecv.at[layer])

    def turn_activation():
        for i in range(ROWS):
            cot_flat[:, i, :] = act_rows[i]
        act_out[...] = cot_flat[...].astype(BF16)
        leave(act_out, act_hbm)

    backward_norm(2, 3, turn_activation)
    conv(wt[1], dmap, up.at[1], lambda i, value: value * slope[1, i])
    backward_norm(1, 4, lambda: grad_stage_1(1, x1))
    conv(wt[0], dmap, up.at[0], lambda i, value: value * slope[0, i])

    def last_shadow():
        along_depth(1, grecv.at[1], gdepth.at[1])
        grad_stage_1(0, x0)

    def nothing():
        pass

    sums = norm_sums(0, nothing, nothing, last_shadow)
    leave(gains_out, gains_hbm)
    leave(shifts_out, shifts_hbm)
    for i in range(ROWS):
        dstem[CH * i : CH * (i + 1), :] = down(0, sums, up[0, i], white[0, i]).astype(BF16)
    banded = dot_nt(dstem[...], patches[...])
    total = banded[0:CH, :]
    for i in range(1, ROWS):
        total = total + pltpu.roll(banded[CH * i : CH * (i + 1), :], 512 - 2 * i, 1)
    high = total.astype(BF16)
    rest = total - high.astype(F32)
    mid = rest.astype(BF16)
    low = (rest - mid.astype(F32)).astype(BF16)
    put(ssend, dot(high, choose[...]) + dot(mid, choose[...]) + dot(low, choose[...]))
    scatter(2, ssend, srecv)
    along_depth(0, grecv.at[0], gdepth.at[0])
    spread(1, gdepth.at[1], gfull.at[1])
    along_depth(2, srecv, sdepth)
    spread(0, gdepth.at[0], gfull.at[0])
    finish_mid(1)
    spread(2, sdepth, sfull)
    finish_mid(0)
    collect(2, sfull, 256)
    turned = rows_full[:, 0:256].T
    stem_out[...] = turned[0:168, :].reshape(STEM_ROWS, 8, CH)[:, 0:7, :]
    leave(stem_out, stem_hbm)
    for n, (a, b, c) in enumerate(
        ((gsend.at[0], gdepth.at[0], gfull.at[0]), (gsend.at[1], gdepth.at[1], gfull.at[1]), (ssend, sdepth, sfull))
    ):
        drain(a, PLANE - 1, fin_send.at[n, 0])
        drain(b, DEPTH - 1, fin_send.at[n, 1])
        drain(c, PLANE - 1, fin_send.at[n, 2])
    for copy in leaving:
        copy.wait()


def write_out(*refs):
    ins, outs, held, sems = refs[0:5], refs[5:10], refs[10:15], refs[15]
    arriving = [pltpu.make_async_copy(a, b, sems.at[0, n]) for n, (a, b) in enumerate(zip(ins, held))]
    leaving = [pltpu.make_async_copy(a, b, sems.at[1, n]) for n, (a, b) in enumerate(zip(held, outs))]
    for copy in arriving:
        copy.start()
    for first, second in zip(arriving, leaving):
        first.wait()
        second.start()
    for copy in leaving:
        copy.wait()


def shards(slide_band, cotangent, stem_weight, mid_weight, norm_gains, norm_shifts):
    img = slide_band.reshape(48, 512)
    w0 = stem_weight.transpose(1, 3, 2, 0).reshape(STEM_ROWS, 7, CH)
    wm = mid_weight.transpose(0, 2, 3, 1, 4).reshape(18, CH, CH)
    hbm = pl.BlockSpec(memory_space=pltpu.HBM)
    dma = pltpu.SemaphoreType.DMA
    shapes = (
        jax.ShapeDtypeStruct((CH, ROWS, COLS), BF16),
        jax.ShapeDtypeStruct((STEM_ROWS, 7, CH), F32),
        jax.ShapeDtypeStruct((18, CH, CH), F32),
        jax.ShapeDtypeStruct((3, CH), F32),
        jax.ShapeDtypeStruct((3, CH), F32),
    )
    results = pl.pallas_call(
        kernel,
        out_shape=shapes,
        in_specs=[hbm] * 6,
        out_specs=(hbm,) * 5,
        scratch_shapes=[
            pltpu.VMEM((CH, ROWS, COLS), BF16),
            pltpu.VMEM((STEM_ROWS, 7, CH), F32),
            pltpu.VMEM((18, CH, CH), F32),
            pltpu.VMEM((3, CH), F32),
            pltpu.VMEM((3, CH), F32),
            pltpu.VMEM((CH, ROWS, COLS), BF16),
            pltpu.VMEM((STEM_ROWS, 7, CH), BF16),
            pltpu.VMEM((18, CH, CH), BF16),
            pltpu.VMEM((2, 3, CH), F32),
            pltpu.VMEM((256, 128), F32),
            pltpu.VMEM((2, CH, TAPS), BF16),
            pltpu.VMEM((2, CH, TAPS), BF16),
            pltpu.VMEM((CH, ROWS, COLS), F32),
            pltpu.VMEM((ROWS, CH, COLS), F32),
            pltpu.VMEM((ROWS, CH, COLS), F32),
            pltpu.VMEM((512, 256), BF16),
            pltpu.VMEM((144, 768), BF16),
            pltpu.VMEM((2, 768, 384), BF16),
            pltpu.VMEM((512, COLS), BF16),
            pltpu.VMEM((512, 512), BF16),
            pltpu.VMEM((3 * CH * (ROWS + 2), COLS), BF16),
            pltpu.VMEM((3 * CH * (ROWS + 2), COLS), BF16),
            pltpu.VMEM((3 * CH * (ROWS + 2), COLS), BF16),
            pltpu.VMEM((512, COLS), BF16),
            pltpu.VMEM((3, ROWS, CH, COLS), F32),
            pltpu.VMEM((3, ROWS, CH, COLS), F32),
            pltpu.VMEM((3, ROWS, CH, COLS), F32),
            pltpu.VMEM((3, ROWS, CH, COLS), F32),
            pltpu.VMEM((5, 2, CH, COLS), F32),
            pltpu.VMEM((5, 2, ROWS, 128), F32),
            pltpu.VMEM((5, 6, ROWS, 128), F32),
            pltpu.VMEM((PLANE, 1, 128), F32),
            pltpu.VMEM((DEPTH, 1, 128), F32),
            pltpu.VMEM((6, 2, 1, 128), F32),
            pltpu.VMEM((6, CHIPS, 1, 128), F32),
            pltpu.VMEM((2, PLANE, 2, 640), F32),
            pltpu.VMEM((2, PLANE, 2, 640), F32),
            pltpu.VMEM((2, DEPTH, 2, 640), F32),
            pltpu.VMEM((2, PLANE, 2, 640), F32),
            pltpu.VMEM((PLANE, 2, 256), F32),
            pltpu.VMEM((PLANE, 2, 256), F32),
            pltpu.VMEM((DEPTH, 2, 256), F32),
            pltpu.VMEM((PLANE, 2, 256), F32),
            pltpu.VMEM((CH, 640), F32),
            dma((6,)), dma((6,)),
            dma((8,)), dma((8,)), dma((5, 8)), dma((5, 8)),
            dma((6, 2)), dma((6, 2)), dma((3, 3)), dma((3, 3)),
        ],
        compiler_params=pltpu.CompilerParams(
            collective_id=0, has_side_effects=True, vmem_limit_bytes=VMEM_BYTES
        ),
    )(img, cotangent, w0, wm, norm_gains, norm_shifts)
    act, stem, mid, gains, shifts = pl.pallas_call(
        write_out,
        out_shape=shapes,
        in_specs=[hbm] * 5,
        out_specs=(hbm,) * 5,
        scratch_shapes=[pltpu.VMEM(a.shape, a.dtype) for a in shapes] + [dma((2, 5))],
        compiler_params=pltpu.CompilerParams(vmem_limit_bytes=VMEM_BYTES),
    )(*results)
    return (
        act,
        stem.reshape(7, 3, 7, CH).transpose(3, 0, 2, 1),
        mid.reshape(2, 3, 3, CH, CH).transpose(0, 3, 1, 2, 4),
        gains,
        shifts,
    )


def solution(mesh):
    return jax.shard_map(
        shards,
        mesh=mesh,
        in_specs=(P(None, "row", "col"), P(None, "row", "col"), P(), P(), P(), P()),
        out_specs=(P(None, "row", "col"), P(), P(), P(), P()),
        check_vma=False,
    )
```

```python
import jax
import jax.numpy as jnp
from jax import lax
from jax.experimental import pallas as pl
from jax.experimental.pallas import tpu as pltpu
from jax.sharding import PartitionSpec as P

EPS = 1e-05
MESH = pl.DeviceIdType.MESH
F32 = jnp.float32
BF16 = jnp.bfloat16

CH = 64
ROWS = 8
COLS = 256
TAPS = 9 * CH
LOCAL = ROWS * COLS
PIXELS = 524288.0
CHIPS = 128
VMEM_BYTES = 62 * 1024 * 1024
PLANE = 32
DEPTH = 8
STEM_ROWS = 21


def dot(a, b):
    return jnp.dot(a, b, preferred_element_type=F32)


def dot_nt(a, b):
    return lax.dot_general(a, b, (((1,), (1,)), ((), ())), preferred_element_type=F32)


def hops(offset):
    return sum(min(d, n - d) for d, n in zip(offset, (4, 4, 8)))


CHIP_OFFSETS = sorted(
    ((dy, dx, dz) for dy in range(4) for dx in range(4) for dz in range(8) if dy or dx or dz),
    key=lambda offset: -hops(offset),
)
PLANE_OFFSETS = sorted(
    ((dy, dx, dc) for dy in range(4) for dx in range(4) for dc in range(2) if dy or dx or dc),
    key=lambda offset: -hops((offset[0], offset[1], 0)),
)
DEPTH_OFFSETS = (4, 3, 5, 2, 6, 1, 7)


def kernel(
    img, cot, w0_in, wm_in, gains_in, shifts_in,
    act_hbm, stem_hbm, mid_hbm, gains_hbm, shifts_hbm,
    act_out, stem_out, mid_out, gains_out, shifts_out,
    cot_raw, w0_raw, wm_raw, norm_raw, w0_flat, wm, wt, cot_flat, cot_rows, act_rows, choose,
    tiles, sel, patches, wbig, x0, x1, dmap, dstem,
    pre, white, slope, up, rowhalo, colsend, colrecv,
    first_a, first_b, ar_a, ar_b, gsend, grecv, gdepth, gfull, ssend, srecv, sdepth, sfull, rows_full,
    in_sem, out_sem, img_send, img_recv, halo_send, halo_recv, ar_send, ar_recv, fin_send, fin_recv,
):
    row, col = lax.axis_index("row"), lax.axis_index("col")
    chip_x, chip_z, core = lax.div(col, 16), lax.rem(lax.div(col, 2), 8), lax.rem(col, 2)
    not_top = jnp.where(row == 0, 0.0, 1.0).astype(F32)
    not_bottom = jnp.where(row == 3, 0.0, 1.0).astype(F32)
    not_left = jnp.where(col == 0, 0.0, 1.0).astype(F32)
    not_right = jnp.where(col == 63, 0.0, 1.0).astype(F32)
    chip_rank = (row * 4 + chip_x) * 8 + chip_z
    plane_rank = (row * 4 + chip_x) * 2 + core

    ring_y = [row] + [lax.rem(row + d, 4) for d in range(1, 4)]
    ring_x = [chip_x] + [lax.rem(chip_x + d, 4) for d in range(1, 4)]
    ring_z = [2 * chip_z + core] + [2 * lax.rem(chip_z + d, 8) + core for d in range(1, 8)]
    ring_core = [core, 1 - core]
    col_x = [16 * x for x in ring_x]
    col_core = [2 * chip_z + c for c in ring_core]
    other_core = (row, col_x[0] + col_core[1])

    def chip_peer(offset):
        dy, dx, dz = offset
        return (ring_y[dy], col_x[dx] + ring_z[dz])

    def plane_peer(offset):
        dy, dx, dc = offset
        return 8 * ring_y[dy] + 2 * ring_x[dx] + ring_core[dc], (ring_y[dy], col_x[dx] + col_core[dc])

    def depth_peer(dz):
        return (row, col_x[0] + ring_z[dz])

    def near(dr, dc):
        return (lax.rem(row + dr + 4, 4), lax.rem(col + dc + 64, 64))

    around = [(1, 0), (-1, 0), (0, 1), (0, -1), (1, 1), (1, -1), (-1, 1), (-1, -1)]

    barrier = pltpu.get_barrier_semaphore()

    def greet(where):
        pl.semaphore_signal(barrier, inc=1, device_id=where, device_id_type=MESH)

    loads = [
        pltpu.make_async_copy(src, dst, in_sem.at[n])
        for n, (src, dst) in enumerate(
            (
                (img, tiles.at[48:96, 128:640]),
                (w0_in, w0_raw),
                (wm_in, wm_raw),
                (gains_in, norm_raw.at[0]),
                (shifts_in, norm_raw.at[1]),
                (cot, cot_raw),
            )
        )
    ]
    for load in loads:
        load.start()
    partners = [(hops((dy, dx, 0)), plane_peer((dy, dx, dc))[1]) for dy, dx, dc in PLANE_OFFSETS]
    partners += [(hops((0, 0, dz)), depth_peer(dz)) for dz in DEPTH_OFFSETS]
    partners.sort(key=lambda partner: -partner[0])
    for distance, where in partners:
        if distance >= 3:
            greet(where)
    for dr, dc in around:
        greet(near(dr, dc))
    for distance, where in partners:
        if distance < 3:
            greet(where)


    loads[0].wait()
    pl.semaphore_wait(barrier, len(around) + len(PLANE_OFFSETS) + len(DEPTH_OFFSETS))

    copies = []
    for n, (dr, dc) in enumerate(around):
        span = slice(128, 640) if dc == 0 else (slice(512, 640) if dc == 1 else slice(128, 256))
        lanes = slice(128, 640) if dc == 0 else (slice(0, 128) if dc == 1 else slice(640, 768))
        first = 48 * (1 - dr)
        copies.append(
            pltpu.make_async_remote_copy(
                src_ref=tiles.at[48:96, span],
                dst_ref=tiles.at[first : first + 48, lanes],
                send_sem=img_send.at[n],
                recv_sem=img_recv.at[n],
                device_id=near(dr, dc),
                device_id_type=MESH,
            )
        )
    for copy in copies:
        copy.start()

    def steps(v, edges):
        return sum(jnp.where(v >= e, 1, 0) for e in edges)

    src = lax.broadcasted_iota(jnp.int32, (512, 256), 0)
    dst = lax.broadcasted_iota(jnp.int32, (1, 256), 1)
    dst_q, dst_b = dst // 8, dst % 8
    dst_a = steps(dst_q, range(3, 21, 3))
    dst_c = dst_q - 3 * dst_a
    place = jnp.where((dst_b < 7) & (dst_q < 21), CH * dst_b + STEM_ROWS * dst_c + dst_a, -1)
    choose[...] = jnp.where(src == place, 1.0, 0.0).astype(BF16)
    diff = lax.broadcasted_iota(jnp.int32, (768, 384), 0) - 2 * lax.broadcasted_iota(
        jnp.int32, (768, 384), 1
    )
    sel[0] = jnp.where(diff == 124, 1.0, 0.0).astype(BF16)
    sel[1] = jnp.where(diff == 125, 1.0, 0.0).astype(BF16)

    m = lax.broadcasted_iota(jnp.int32, (64, 144), 0)
    n = lax.broadcasted_iota(jnp.int32, (64, 144), 1)
    m_c = steps(m, (21, 42, 63))
    m_r = m - 21 * m_c
    n_t = steps(n, (48, 96))
    n_in = n - 48 * n_t
    n_c = steps(n_in, (16, 32))
    n_r = 16 * n_t + n_in - 16 * n_c
    pick = jnp.where((m_c == n_c) & (n_r == m_r + 13), 1.0, 0.0).astype(BF16)

    w0_flat[...] = jnp.zeros(w0_flat.shape, F32)
    for load in loads[1:]:
        load.wait()

    for k in range(21):
        w0_flat[8 * k : 8 * k + 7, 0:CH] = w0_raw[k].astype(F32)
    w0 = dot_nt(w0_flat[...].T[0:CH, :].astype(BF16), choose[...])
    for i in range(ROWS):
        wbig[CH * i : CH * (i + 1), :] = (pltpu.roll(w0, 2 * i, 1) if i else w0).astype(BF16)
    w0_flat[0:3, 0:CH] = norm_raw[0]
    w0_flat[8:11, 0:CH] = norm_raw[1]
    columns = w0_flat[0:16, :].T
    gain = [columns[0:CH, k : k + 1] for k in range(3)]
    shift = [columns[0:CH, 8 + k : 9 + k] for k in range(3)]

    for copy in copies:
        copy.wait()

    def scale_tile(rows, lanes, factor):
        tiles[rows, lanes] = (tiles[rows, lanes].astype(F32) * factor).astype(BF16)

    scale_tile(slice(0, 48), slice(0, 768), not_top)
    scale_tile(slice(96, 144), slice(0, 768), not_bottom)
    scale_tile(slice(0, 144), slice(0, 128), not_left)
    scale_tile(slice(0, 144), slice(640, 768), not_right)

    image_rows = dot(pick, tiles[...]).astype(BF16)
    planes = [dot(image_rows, sel[0]), dot(image_rows, sel[1])]
    for b in range(7):
        shift_by = (b - 3) // 2 + 2
        plane = planes[(b - 3) % 2]
        moved = pltpu.roll(plane, 384 - shift_by, 1) if shift_by else plane
        patches[CH * b : CH * (b + 1), :] = moved[:, 0:COLS].astype(BF16)
    patches[448:512, :] = jnp.zeros((64, COLS), BF16)

    lane128 = lax.broadcasted_iota(jnp.int32, (CH, 128), 1)
    lane256 = lax.broadcasted_iota(jnp.int32, (CH, COLS), 1)
    lane1 = lax.broadcasted_iota(jnp.int32, (1, 128), 1)

    def fold(v):
        return v[:, 0:128] + v[:, 128:256]

    def to_row(first, second):
        both = jnp.where(lane128 == 0, first, jnp.where(lane128 == 1, second, 0.0)).T
        return jnp.concatenate([both[0:1, :], both[1:2, :]], axis=1)

    def to_columns(row_value):
        turned = jnp.broadcast_to(row_value, (8, 128)).T
        return turned[0:CH, 0:1], turned[CH : 2 * CH, 0:1]

    def drain(buf, count, sem):
        part = buf.at[0:count]
        pltpu.make_async_copy(part, part, sem).wait()

    def send(src, dst, send_sem, recv_sem, where):
        pltpu.make_async_remote_copy(
            src_ref=src,
            dst_ref=dst,
            send_sem=send_sem,
            recv_sem=recv_sem,
            device_id=where,
            device_id_type=MESH,
        ).start()

    def exchange(index, value, combine, before, within, meanwhile):
        if index == 0:
            return first_exchange(value, combine, before, within, meanwhile)
        buf, sems = ar_a.at[index], (ar_send.at[index, 0], ar_recv.at[index, 0])
        buf[pl.ds(core, 1)] = value[None]
        send(buf.at[core], buf.at[core], *sems, other_core)
        before()
        drain(buf, 1, sems[1])
        value = combine(buf[...], float(LOCAL))
        drain(buf, 1, sems[0])
        buf, sems = ar_b.at[index], (ar_send.at[index, 1], ar_recv.at[index, 1])
        buf[pl.ds(chip_rank, 1)] = value[None]
        for place, offset in enumerate(CHIP_OFFSETS):
            if hops(offset) == 3 and hops(CHIP_OFFSETS[place - 1]) == 4:
                within()
            send(buf.at[chip_rank], buf.at[chip_rank], *sems, chip_peer(offset))
        meanwhile()
        drain(buf, CHIPS - 1, sems[1])
        drain(buf, CHIPS - 1, sems[0])
        return combine(buf[...], float(LOCAL * 2))

    def first_exchange(value, combine, before, within, meanwhile):
        sems = (ar_send.at[0, 0], ar_recv.at[0, 0])
        first_a[pl.ds(plane_rank, 1)] = value[None]
        for offset in PLANE_OFFSETS:
            send(first_a.at[plane_rank], first_a.at[plane_rank], *sems, plane_peer(offset)[1])
        before()
        within()
        meanwhile()
        drain(first_a, PLANE - 1, sems[1])
        drain(first_a, PLANE - 1, sems[0])
        value = combine(first_a[...], float(LOCAL))
        sems = (ar_send.at[0, 1], ar_recv.at[0, 1])
        first_b[pl.ds(chip_z, 1)] = value[None]
        for dz in DEPTH_OFFSETS:
            where = depth_peer(dz)
            send(first_b.at[chip_z], first_b.at[chip_z], *sems, where)
        drain(first_b, DEPTH - 1, sems[1])
        drain(first_b, DEPTH - 1, sems[0])
        return combine(first_b[...], float(LOCAL * PLANE))

    def total_of(got):
        if got.shape[0] == CHIPS:
            got = jnp.sum(got.reshape(8, 16, 1, 128), axis=0)
        return jnp.sum(got, axis=0)

    def combine_moments(got, count):
        total = total_of(got)
        mean = total * (1.0 / got.shape[0])
        off = got - mean[None]
        spread = total_of(off * off) * count
        return jnp.where(lane1 < CH, mean, total + pltpu.roll(spread, CH, 1))

    def combine_sums(got, count):
        return total_of(got)

    def pack_halo(index, ref):
        for side, lane in ((0, 0), (1, COLS - 1)):
            pack = jnp.zeros((CH, 128), F32)
            for i in range(ROWS):
                pack = jnp.where(lane128 == i, ref[i, :, lane : lane + 1], pack)
            pack = jnp.concatenate([pack, jnp.zeros((128 - CH, 128), F32)], axis=0)
            colsend[index, side] = pack.T[0:ROWS, :]

    def send_halo(index, ref):
        started = []
        for n, (dr, dc) in enumerate(around):
            if dc == 0:
                src = ref.at[ROWS - 1 if dr == 1 else 0]
                dst = rowhalo.at[index, 0 if dr == 1 else 1]
            else:
                src = colsend.at[index, 1 if dc == 1 else 0]
                dst = colrecv.at[index, (0 if dc == 1 else 3) + 1 - dr]
            copy = pltpu.make_async_remote_copy(
                src_ref=src,
                dst_ref=dst,
                send_sem=halo_send.at[index, n],
                recv_sem=halo_recv.at[index, n],
                device_id=near(dr, dc),
                device_id_type=MESH,
            )
            copy.start()
            started.append(copy)
        return started

    def build(dst, center, top, bottom, sides):
        for r in range(ROWS + 2):
            value = top if r == 0 else (bottom if r == ROWS + 1 else center(r - 1))
            lane = ROWS - 1 if r == 0 else (2 * ROWS if r == ROWS + 1 else ROWS + r - 1)
            before = jnp.where(lane256 == 0, sides[:, lane : lane + 1], pltpu.roll(value, 1, 1))
            lane += 3 * ROWS
            after = jnp.where(
                lane256 == COLS - 1, sides[:, lane : lane + 1], pltpu.roll(value, COLS - 1, 1)
            )
            base = 3 * CH * r
            dst[base : base + CH, :] = before.astype(BF16)
            dst[base + CH : base + 2 * CH, :] = value.astype(BF16)
            dst[base + 2 * CH : base + 3 * CH, :] = after.astype(BF16)

    lane48 = lax.broadcasted_iota(jnp.int32, (1, 6 * ROWS), 1)
    edge = jnp.where(lane48 < 3 * ROWS, not_left, not_right)
    in_side = jnp.where(lane48 < 3 * ROWS, lane48, lane48 - 3 * ROWS)
    edge = edge * jnp.where(in_side < ROWS, not_top, jnp.where(in_side < 2 * ROWS, 1.0, not_bottom))

    def build_with_halo(dst, center, apply_halo, index):
        top = apply_halo("row", 0) * not_top
        bottom = apply_halo("row", 1) * not_bottom
        build(dst, center, top, bottom, apply_halo("col", None) * edge)

    def conv(weight, src, out, after=None):
        for i in range(ROWS):
            value = dot(weight, src[3 * CH * i : 3 * CH * i + TAPS, :])
            out[i] = value if after is None else after(i, value)

    def moments(index, *hidden):
        ref = pre.at[index]
        total = jnp.zeros((CH, 128), F32)
        for i in range(ROWS):
            total = total + fold(ref[i])
        mean = jnp.sum(total, axis=1, keepdims=True) * (1.0 / LOCAL)
        total = jnp.zeros((CH, 128), F32)
        for i in range(ROWS):
            off = ref[i] - mean
            total = total + fold(off * off)
        local = to_row(mean, jnp.sum(total, axis=1, keepdims=True))
        mean, squares = to_columns(exchange(index, local, combine_moments, *hidden))
        return mean, lax.rsqrt(squares * (1.0 / PIXELS) + EPS)

    def halo_block(index, kind, place):
        if kind == "row":
            return rowhalo[index, place]
        return colrecv[index].reshape(6 * ROWS, 128).T[0:CH, :]

    mean, inv = [None] * 3, [None] * 3

    def forward_norm(index, meanwhile):
        halo, ref = [], pre.at[index]
        mean[index], inv[index] = moments(
            index,
            lambda: pack_halo(index, ref),
            lambda: halo.extend(send_halo(index, ref)),
            meanwhile,
        )
        for copy in halo:
            copy.wait()

    def forward_rows(index, i):
        normed_white = (pre[index, i] - mean[index]) * inv[index]
        white[index, i] = normed_white
        normed = gain[index] * normed_white + shift[index]
        sig = jax.nn.sigmoid(normed)
        slope[index, i] = sig * (1.0 + normed * (1.0 - sig))
        return normed * sig

    def forward_build(index, dst):
        def outside(kind, place):
            block = halo_block(index, kind, place)
            normed = gain[index] * ((block - mean[index]) * inv[index]) + shift[index]
            return normed * jax.nn.sigmoid(normed)

        build_with_halo(dst, lambda i: forward_rows(index, i), outside, index)

    def taps_of(layer):
        return [wm_raw[9 * layer + t].astype(F32) for t in range(9)]

    def lay_taps(parts, target):
        for t in range(0, 9, 2):
            part = parts[t : t + 2]
            value = jnp.concatenate(part, axis=1) if len(part) == 2 else part[0]
            target[:, CH * t : CH * (t + len(part))] = value.astype(BF16)

    def lay_weights():
        for layer in range(2):
            lay_taps(taps_of(layer), wm.at[layer])

    def lay_turned():
        gsend[...] = jnp.zeros(gsend.shape, F32)
        for layer in range(2):
            parts = taps_of(layer)
            lay_taps([parts[8 - t].T for t in range(9)], wt.at[layer])

    def spread_cotangent():
        cot_flat[...] = cot_raw[...].astype(F32)
        for i in range(ROWS):
            cot_rows[i] = cot_flat[:, i, :]

    stem = dot(wbig[...], patches[...])
    for i in range(ROWS):
        pre[0, i] = stem[CH * i : CH * (i + 1), :]
    forward_norm(0, lay_weights)
    forward_build(0, x0)
    conv(wm[0], x0, pre.at[1])
    forward_norm(1, spread_cotangent)
    forward_build(1, x1)
    conv(wm[1], x1, pre.at[2])
    forward_norm(2, lay_turned)
    for i in range(ROWS):
        act_rows[i] = forward_rows(2, i)
        up[2, i] = cot_rows[i] * slope[2, i]

    def norm_sums(index, *hidden):
        shift_total = jnp.zeros((CH, 128), F32)
        gain_total = jnp.zeros((CH, 128), F32)
        for i in range(ROWS):
            shift_total = shift_total + fold(up[index, i])
            gain_total = gain_total + fold(up[index, i] * white[index, i])
        local = to_row(
            jnp.sum(shift_total, axis=1, keepdims=True), jnp.sum(gain_total, axis=1, keepdims=True)
        )
        sums = exchange(3 + index, local, combine_sums, *hidden)
        shifts_out[index : index + 1, :] = sums[:, 0:CH]
        gains_out[index : index + 1, :] = sums[:, CH : 2 * CH]
        shift_sum, gain_sum = to_columns(sums)
        return shift_sum * (1.0 / PIXELS), gain_sum * (1.0 / PIXELS)

    def down(index, sums, up_value, whitened):
        return (gain[index] * inv[index]) * (up_value - sums[0] - whitened * sums[1])

    def backward_norm(index, halo_index, meanwhile):
        halo, ref = [], up.at[index]
        sums = norm_sums(
            index,
            lambda: pack_halo(halo_index, ref),
            lambda: halo.extend(send_halo(halo_index, ref)),
            meanwhile,
        )

        def center(i):
            return down(index, sums, up[index, i], white[index, i])

        def outside(kind, place):
            whitened = (halo_block(index, kind, place) - mean[index]) * inv[index]
            return down(index, sums, halo_block(halo_index, kind, place), whitened)

        for copy in halo:
            copy.wait()
        build_with_halo(dmap, center, outside, index)

    def kernel_grad(src):
        total = jnp.zeros((CH, TAPS), F32)
        for i in range(ROWS):
            base = 3 * CH * (i + 1) + CH
            total = total + dot_nt(dmap[base : base + CH, :], src[3 * CH * i : 3 * CH * i + TAPS, :])
        return total

    def put(buf, value):
        for k in range(PLANE):
            buf[k, :, 0 : value.shape[1]] = value[2 * k : 2 * k + 2, :]

    def scatter(n, mine, got):
        got[pl.ds(plane_rank, 1)] = mine[pl.ds(plane_rank, 1)]
        for offset in PLANE_OFFSETS:
            rank, where = plane_peer(offset)
            send(mine.at[rank], got.at[plane_rank], fin_send.at[n, 0], fin_recv.at[n, 0], where)

    def along_depth(n, got, depth):
        drain(got, PLANE - 1, fin_recv.at[n, 0])
        depth[pl.ds(chip_z, 1)] = jnp.sum(got[...], axis=0)[None]
        for dz in DEPTH_OFFSETS:
            where = depth_peer(dz)
            send(depth.at[chip_z], depth.at[chip_z], fin_send.at[n, 1], fin_recv.at[n, 1], where)

    def spread(n, depth, full):
        drain(depth, DEPTH - 1, fin_recv.at[n, 1])
        full[pl.ds(plane_rank, 1)] = jnp.sum(depth[...], axis=0)[None]
        for offset in PLANE_OFFSETS:
            where = plane_peer(offset)[1]
            send(full.at[plane_rank], full.at[plane_rank], fin_send.at[n, 2], fin_recv.at[n, 2], where)

    def collect(n, full, lanes):
        drain(full, PLANE - 1, fin_recv.at[n, 2])
        for k in range(PLANE):
            rows_full[2 * k : 2 * k + 2, 0:lanes] = full[k]

    leaving = []

    def leave(src, dst):
        copy = pltpu.make_async_copy(src, dst, out_sem.at[len(leaving)])
        copy.start()
        leaving.append(copy)

    def finish_mid(layer):
        collect(layer, gfull.at[layer], 640)
        for t in range(9):
            mid_out[9 * layer + t] = rows_full[:, CH * t : CH * (t + 1)]
        span = pl.ds(9 * layer, 9)
        leave(mid_out.at[span], mid_hbm.at[span])

    def grad_stage_1(layer, src):
        put(gsend.at[layer], kernel_grad(src))
        scatter(layer, gsend.at[layer], grecv.at[layer])

    def turn_activation():
        for i in range(ROWS):
            cot_flat[:, i, :] = act_rows[i]
        act_out[...] = cot_flat[...].astype(BF16)
        leave(act_out, act_hbm)

    backward_norm(2, 3, turn_activation)
    conv(wt[1], dmap, up.at[1], lambda i, value: value * slope[1, i])
    backward_norm(1, 4, lambda: grad_stage_1(1, x1))
    conv(wt[0], dmap, up.at[0], lambda i, value: value * slope[0, i])

    def last_shadow():
        along_depth(1, grecv.at[1], gdepth.at[1])
        grad_stage_1(0, x0)

    def nothing():
        pass

    sums = norm_sums(0, nothing, nothing, last_shadow)
    leave(gains_out, gains_hbm)
    leave(shifts_out, shifts_hbm)
    for i in range(ROWS):
        dstem[CH * i : CH * (i + 1), :] = down(0, sums, up[0, i], white[0, i]).astype(BF16)
    banded = dot_nt(dstem[...], patches[...])
    total = banded[0:CH, :]
    for i in range(1, ROWS):
        total = total + pltpu.roll(banded[CH * i : CH * (i + 1), :], 512 - 2 * i, 1)
    high = total.astype(BF16)
    rest = total - high.astype(F32)
    mid = rest.astype(BF16)
    low = (rest - mid.astype(F32)).astype(BF16)
    put(ssend, dot(high, choose[...]) + dot(mid, choose[...]) + dot(low, choose[...]))
    scatter(2, ssend, srecv)
    along_depth(0, grecv.at[0], gdepth.at[0])
    spread(1, gdepth.at[1], gfull.at[1])
    along_depth(2, srecv, sdepth)
    spread(0, gdepth.at[0], gfull.at[0])
    finish_mid(1)
    spread(2, sdepth, sfull)
    finish_mid(0)
    collect(2, sfull, 256)
    turned = rows_full[:, 0:256].T
    stem_out[...] = turned[0:168, :].reshape(STEM_ROWS, 8, CH)[:, 0:7, :]
    leave(stem_out, stem_hbm)
    for n, (a, b, c) in enumerate(
        ((gsend.at[0], gdepth.at[0], gfull.at[0]), (gsend.at[1], gdepth.at[1], gfull.at[1]), (ssend, sdepth, sfull))
    ):
        drain(a, PLANE - 1, fin_send.at[n, 0])
        drain(b, DEPTH - 1, fin_send.at[n, 1])
        drain(c, PLANE - 1, fin_send.at[n, 2])
    for copy in leaving:
        copy.wait()


def write_out(*refs):
    ins, outs, held, sems = refs[0:5], refs[5:10], refs[10:15], refs[15]
    arriving = [pltpu.make_async_copy(a, b, sems.at[0, n]) for n, (a, b) in enumerate(zip(ins, held))]
    leaving = [pltpu.make_async_copy(a, b, sems.at[1, n]) for n, (a, b) in enumerate(zip(held, outs))]
    for copy in arriving:
        copy.start()
    for first, second in zip(arriving, leaving):
        first.wait()
        second.start()
    for copy in leaving:
        copy.wait()


def shards(slide_band, cotangent, stem_weight, mid_weight, norm_gains, norm_shifts):
    img = slide_band.reshape(48, 512)
    w0 = stem_weight.transpose(1, 3, 2, 0).reshape(STEM_ROWS, 7, CH)
    wm = mid_weight.transpose(0, 2, 3, 1, 4).reshape(18, CH, CH)
    hbm = pl.BlockSpec(memory_space=pltpu.HBM)
    dma = pltpu.SemaphoreType.DMA
    shapes = (
        jax.ShapeDtypeStruct((CH, ROWS, COLS), BF16),
        jax.ShapeDtypeStruct((STEM_ROWS, 7, CH), F32),
        jax.ShapeDtypeStruct((18, CH, CH), F32),
        jax.ShapeDtypeStruct((3, CH), F32),
        jax.ShapeDtypeStruct((3, CH), F32),
    )
    results = pl.pallas_call(
        kernel,
        out_shape=shapes,
        in_specs=[hbm] * 6,
        out_specs=(hbm,) * 5,
        scratch_shapes=[
            pltpu.VMEM((CH, ROWS, COLS), BF16),
            pltpu.VMEM((STEM_ROWS, 7, CH), F32),
            pltpu.VMEM((18, CH, CH), F32),
            pltpu.VMEM((3, CH), F32),
            pltpu.VMEM((3, CH), F32),
            pltpu.VMEM((CH, ROWS, COLS), BF16),
            pltpu.VMEM((STEM_ROWS, 7, CH), BF16),
            pltpu.VMEM((18, CH, CH), BF16),
            pltpu.VMEM((2, 3, CH), F32),
            pltpu.VMEM((256, 128), F32),
            pltpu.VMEM((2, CH, TAPS), BF16),
            pltpu.VMEM((2, CH, TAPS), BF16),
            pltpu.VMEM((CH, ROWS, COLS), F32),
            pltpu.VMEM((ROWS, CH, COLS), F32),
            pltpu.VMEM((ROWS, CH, COLS), F32),
            pltpu.VMEM((512, 256), BF16),
            pltpu.VMEM((144, 768), BF16),
            pltpu.VMEM((2, 768, 384), BF16),
            pltpu.VMEM((512, COLS), BF16),
            pltpu.VMEM((512, 512), BF16),
            pltpu.VMEM((3 * CH * (ROWS + 2), COLS), BF16),
            pltpu.VMEM((3 * CH * (ROWS + 2), COLS), BF16),
            pltpu.VMEM((3 * CH * (ROWS + 2), COLS), BF16),
            pltpu.VMEM((512, COLS), BF16),
            pltpu.VMEM((3, ROWS, CH, COLS), F32),
            pltpu.VMEM((3, ROWS, CH, COLS), F32),
            pltpu.VMEM((3, ROWS, CH, COLS), F32),
            pltpu.VMEM((3, ROWS, CH, COLS), F32),
            pltpu.VMEM((5, 2, CH, COLS), F32),
            pltpu.VMEM((5, 2, ROWS, 128), F32),
            pltpu.VMEM((5, 6, ROWS, 128), F32),
            pltpu.VMEM((PLANE, 1, 128), F32),
            pltpu.VMEM((DEPTH, 1, 128), F32),
            pltpu.VMEM((6, 2, 1, 128), F32),
            pltpu.VMEM((6, CHIPS, 1, 128), F32),
            pltpu.VMEM((2, PLANE, 2, 640), F32),
            pltpu.VMEM((2, PLANE, 2, 640), F32),
            pltpu.VMEM((2, DEPTH, 2, 640), F32),
            pltpu.VMEM((2, PLANE, 2, 640), F32),
            pltpu.VMEM((PLANE, 2, 256), F32),
            pltpu.VMEM((PLANE, 2, 256), F32),
            pltpu.VMEM((DEPTH, 2, 256), F32),
            pltpu.VMEM((PLANE, 2, 256), F32),
            pltpu.VMEM((CH, 640), F32),
            dma((6,)), dma((6,)),
            dma((8,)), dma((8,)), dma((5, 8)), dma((5, 8)),
            dma((6, 2)), dma((6, 2)), dma((3, 3)), dma((3, 3)),
        ],
        compiler_params=pltpu.CompilerParams(
            collective_id=0, has_side_effects=True, vmem_limit_bytes=VMEM_BYTES
        ),
    )(img, cotangent, w0, wm, norm_gains, norm_shifts)
    act, stem, mid, gains, shifts = pl.pallas_call(
        write_out,
        out_shape=shapes,
        in_specs=[hbm] * 5,
        out_specs=(hbm,) * 5,
        scratch_shapes=[pltpu.VMEM(a.shape, a.dtype) for a in shapes] + [dma((2, 5))],
        compiler_params=pltpu.CompilerParams(vmem_limit_bytes=VMEM_BYTES),
    )(*results)
    return (
        act,
        stem.reshape(7, 3, 7, CH).transpose(3, 0, 2, 1),
        mid.reshape(2, 3, 3, CH, CH).transpose(0, 3, 1, 2, 4),
        gains,
        shifts,
    )


def solution(mesh):
    return jax.shard_map(
        shards,
        mesh=mesh,
        in_specs=(P(None, "row", "col"), P(None, "row", "col"), P(), P(), P(), P()),
        out_specs=(P(None, "row", "col"), P(), P(), P(), P()),
        check_vma=False,
    )
```

```python
import jax
import jax.numpy as jnp
from jax import lax
from jax.experimental import pallas as pl
from jax.experimental.pallas import tpu as pltpu
from jax.sharding import PartitionSpec as P

EPS = 1e-05
MESH = pl.DeviceIdType.MESH
F32 = jnp.float32
BF16 = jnp.bfloat16

CH = 64
ROWS = 8
COLS = 256
TAPS = 9 * CH
LOCAL = ROWS * COLS
PIXELS = 524288.0
CHIPS = 128
VMEM_BYTES = 62 * 1024 * 1024
PLANE = 32
DEPTH = 8
STEM_ROWS = 21


def dot(a, b):
    return jnp.dot(a, b, preferred_element_type=F32)


def dot_nt(a, b):
    return lax.dot_general(a, b, (((1,), (1,)), ((), ())), preferred_element_type=F32)


def hops(offset):
    return sum(min(d, n - d) for d, n in zip(offset, (4, 4, 8)))


CHIP_OFFSETS = sorted(
    ((dy, dx, dz) for dy in range(4) for dx in range(4) for dz in range(8) if dy or dx or dz),
    key=lambda offset: -hops(offset),
)
PLANE_OFFSETS = sorted(
    ((dy, dx, dc) for dy in range(4) for dx in range(4) for dc in range(2) if dy or dx or dc),
    key=lambda offset: -hops((offset[0], offset[1], 0)),
)
DEPTH_OFFSETS = (4, 3, 5, 2, 6, 1, 7)


def kernel(
    img, cot, w0_in, wm_in, gains_in, shifts_in,
    act_hbm, stem_hbm, mid_hbm, gains_hbm, shifts_hbm,
    act_out, stem_out, mid_out, gains_out, shifts_out,
    cot_raw, w0_raw, wm_raw, norm_raw, w0_flat, wm, wt, cot_flat, cot_rows, act_rows, choose,
    tiles, sel, patches, wbig, x0, x1, dmap, dstem,
    pre, white, slope, up, rowhalo, colsend, colrecv,
    first_a, first_b, ar_a, ar_b, gsend, grecv, gdepth, gfull, ssend, srecv, sdepth, sfull, rows_full,
    in_sem, out_sem, img_send, img_recv, halo_send, halo_recv, ar_send, ar_recv, fin_send, fin_recv,
):
    row, col = lax.axis_index("row"), lax.axis_index("col")
    chip_x, chip_z, core = lax.div(col, 16), lax.rem(lax.div(col, 2), 8), lax.rem(col, 2)
    not_top = jnp.where(row == 0, 0.0, 1.0).astype(F32)
    not_bottom = jnp.where(row == 3, 0.0, 1.0).astype(F32)
    not_left = jnp.where(col == 0, 0.0, 1.0).astype(F32)
    not_right = jnp.where(col == 63, 0.0, 1.0).astype(F32)
    chip_rank = (row * 4 + chip_x) * 8 + chip_z
    plane_rank = (row * 4 + chip_x) * 2 + core

    ring_y = [row] + [lax.rem(row + d, 4) for d in range(1, 4)]
    ring_x = [chip_x] + [lax.rem(chip_x + d, 4) for d in range(1, 4)]
    ring_z = [2 * chip_z + core] + [2 * lax.rem(chip_z + d, 8) + core for d in range(1, 8)]
    ring_core = [core, 1 - core]
    col_x = [16 * x for x in ring_x]
    col_core = [2 * chip_z + c for c in ring_core]
    other_core = (row, col_x[0] + col_core[1])

    def chip_peer(offset):
        dy, dx, dz = offset
        return (ring_y[dy], col_x[dx] + ring_z[dz])

    def plane_peer(offset):
        dy, dx, dc = offset
        return 8 * ring_y[dy] + 2 * ring_x[dx] + ring_core[dc], (ring_y[dy], col_x[dx] + col_core[dc])

    def depth_peer(dz):
        return (row, col_x[0] + ring_z[dz])

    def near(dr, dc):
        return (lax.rem(row + dr + 4, 4), lax.rem(col + dc + 64, 64))

    around = [(1, 0), (-1, 0), (0, 1), (0, -1), (1, 1), (1, -1), (-1, 1), (-1, -1)]

    barrier = pltpu.get_barrier_semaphore()

    def greet(where):
        pl.semaphore_signal(barrier, inc=1, device_id=where, device_id_type=MESH)

    loads = [
        pltpu.make_async_copy(src, dst, in_sem.at[n])
        for n, (src, dst) in enumerate(
            (
                (img, tiles.at[48:96, 128:640]),
                (w0_in, w0_raw),
                (wm_in, wm_raw),
                (gains_in, norm_raw.at[0]),
                (shifts_in, norm_raw.at[1]),
                (cot, cot_raw),
            )
        )
    ]
    for load in loads:
        load.start()
    partners = [(hops((dy, dx, 0)), plane_peer((dy, dx, dc))[1]) for dy, dx, dc in PLANE_OFFSETS]
    partners += [(hops((0, 0, dz)), depth_peer(dz)) for dz in DEPTH_OFFSETS]
    partners.sort(key=lambda partner: -partner[0])
    for distance, where in partners:
        if distance >= 3:
            greet(where)
    for dr, dc in around:
        greet(near(dr, dc))
    for distance, where in partners:
        if distance < 3:
            greet(where)


    loads[0].wait()
    pl.semaphore_wait(barrier, len(around) + len(PLANE_OFFSETS) + len(DEPTH_OFFSETS))

    copies = []
    for n, (dr, dc) in enumerate(around):
        span = slice(128, 640) if dc == 0 else (slice(512, 640) if dc == 1 else slice(128, 256))
        lanes = slice(128, 640) if dc == 0 else (slice(0, 128) if dc == 1 else slice(640, 768))
        first = 48 * (1 - dr)
        copies.append(
            pltpu.make_async_remote_copy(
                src_ref=tiles.at[48:96, span],
                dst_ref=tiles.at[first : first + 48, lanes],
                send_sem=img_send.at[n],
                recv_sem=img_recv.at[n],
                device_id=near(dr, dc),
                device_id_type=MESH,
            )
        )
    for copy in copies:
        copy.start()

    def steps(v, edges):
        return sum(jnp.where(v >= e, 1, 0) for e in edges)

    src = lax.broadcasted_iota(jnp.int32, (512, 256), 0)
    dst = lax.broadcasted_iota(jnp.int32, (1, 256), 1)
    dst_q, dst_b = dst // 8, dst % 8
    dst_a = steps(dst_q, range(3, 21, 3))
    dst_c = dst_q - 3 * dst_a
    place = jnp.where((dst_b < 7) & (dst_q < 21), CH * dst_b + STEM_ROWS * dst_c + dst_a, -1)
    choose[...] = jnp.where(src == place, 1.0, 0.0).astype(BF16)
    diff = lax.broadcasted_iota(jnp.int32, (768, 384), 0) - 2 * lax.broadcasted_iota(
        jnp.int32, (768, 384), 1
    )
    sel[0] = jnp.where(diff == 124, 1.0, 0.0).astype(BF16)
    sel[1] = jnp.where(diff == 125, 1.0, 0.0).astype(BF16)

    m = lax.broadcasted_iota(jnp.int32, (64, 144), 0)
    n = lax.broadcasted_iota(jnp.int32, (64, 144), 1)
    m_c = steps(m, (21, 42, 63))
    m_r = m - 21 * m_c
    n_t = steps(n, (48, 96))
    n_in = n - 48 * n_t
    n_c = steps(n_in, (16, 32))
    n_r = 16 * n_t + n_in - 16 * n_c
    pick = jnp.where((m_c == n_c) & (n_r == m_r + 13), 1.0, 0.0).astype(BF16)

    w0_flat[...] = jnp.zeros(w0_flat.shape, F32)
    for load in loads[1:]:
        load.wait()

    for k in range(21):
        w0_flat[8 * k : 8 * k + 7, 0:CH] = w0_raw[k].astype(F32)
    w0 = dot_nt(w0_flat[...].T[0:CH, :].astype(BF16), choose[...])
    for i in range(ROWS):
        wbig[CH * i : CH * (i + 1), :] = (pltpu.roll(w0, 2 * i, 1) if i else w0).astype(BF16)
    w0_flat[0:3, 0:CH] = norm_raw[0]
    w0_flat[8:11, 0:CH] = norm_raw[1]
    columns = w0_flat[0:16, :].T
    gain = [columns[0:CH, k : k + 1] for k in range(3)]
    shift = [columns[0:CH, 8 + k : 9 + k] for k in range(3)]

    for copy in copies:
        copy.wait()

    def scale_tile(rows, lanes, factor):
        tiles[rows, lanes] = (tiles[rows, lanes].astype(F32) * factor).astype(BF16)

    scale_tile(slice(0, 48), slice(0, 768), not_top)
    scale_tile(slice(96, 144), slice(0, 768), not_bottom)
    scale_tile(slice(0, 144), slice(0, 128), not_left)
    scale_tile(slice(0, 144), slice(640, 768), not_right)

    image_rows = dot(pick, tiles[...]).astype(BF16)
    planes = [dot(image_rows, sel[0]), dot(image_rows, sel[1])]
    for b in range(7):
        shift_by = (b - 3) // 2 + 2
        plane = planes[(b - 3) % 2]
        moved = pltpu.roll(plane, 384 - shift_by, 1) if shift_by else plane
        patches[CH * b : CH * (b + 1), :] = moved[:, 0:COLS].astype(BF16)
    patches[448:512, :] = jnp.zeros((64, COLS), BF16)

    lane128 = lax.broadcasted_iota(jnp.int32, (CH, 128), 1)
    lane256 = lax.broadcasted_iota(jnp.int32, (CH, COLS), 1)
    lane1 = lax.broadcasted_iota(jnp.int32, (1, 128), 1)

    def fold(v):
        return v[:, 0:128] + v[:, 128:256]

    def to_row(first, second):
        both = jnp.where(lane128 == 0, first, jnp.where(lane128 == 1, second, 0.0)).T
        return jnp.concatenate([both[0:1, :], both[1:2, :]], axis=1)

    def to_columns(row_value):
        turned = jnp.broadcast_to(row_value, (8, 128)).T
        return turned[0:CH, 0:1], turned[CH : 2 * CH, 0:1]

    def drain(buf, count, sem):
        part = buf.at[0:count]
        pltpu.make_async_copy(part, part, sem).wait()

    def send(src, dst, send_sem, recv_sem, where):
        pltpu.make_async_remote_copy(
            src_ref=src,
            dst_ref=dst,
            send_sem=send_sem,
            recv_sem=recv_sem,
            device_id=where,
            device_id_type=MESH,
        ).start()

    def exchange(index, value, combine, before, within, meanwhile):
        if index == 0:
            return first_exchange(value, combine, before, within, meanwhile)
        buf, sems = ar_a.at[index], (ar_send.at[index, 0], ar_recv.at[index, 0])
        buf[pl.ds(core, 1)] = value[None]
        send(buf.at[core], buf.at[core], *sems, other_core)
        before()
        drain(buf, 1, sems[1])
        value = combine(buf[...], float(LOCAL))
        drain(buf, 1, sems[0])
        buf, sems = ar_b.at[index], (ar_send.at[index, 1], ar_recv.at[index, 1])
        buf[pl.ds(chip_rank, 1)] = value[None]
        for place, offset in enumerate(CHIP_OFFSETS):
            if hops(offset) == 3 and hops(CHIP_OFFSETS[place - 1]) == 4:
                within()
            send(buf.at[chip_rank], buf.at[chip_rank], *sems, chip_peer(offset))
        meanwhile()
        drain(buf, CHIPS - 1, sems[1])
        drain(buf, CHIPS - 1, sems[0])
        return combine(buf[...], float(LOCAL * 2))

    def first_exchange(value, combine, before, within, meanwhile):
        sems = (ar_send.at[0, 0], ar_recv.at[0, 0])
        first_a[pl.ds(plane_rank, 1)] = value[None]
        for offset in PLANE_OFFSETS:
            send(first_a.at[plane_rank], first_a.at[plane_rank], *sems, plane_peer(offset)[1])
        before()
        within()
        meanwhile()
        drain(first_a, PLANE - 1, sems[1])
        drain(first_a, PLANE - 1, sems[0])
        value = combine(first_a[...], float(LOCAL))
        sems = (ar_send.at[0, 1], ar_recv.at[0, 1])
        first_b[pl.ds(chip_z, 1)] = value[None]
        for dz in DEPTH_OFFSETS:
            where = depth_peer(dz)
            send(first_b.at[chip_z], first_b.at[chip_z], *sems, where)
        drain(first_b, DEPTH - 1, sems[1])
        drain(first_b, DEPTH - 1, sems[0])
        return combine(first_b[...], float(LOCAL * PLANE))

    def total_of(got):
        if got.shape[0] == CHIPS:
            got = jnp.sum(got.reshape(8, 16, 1, 128), axis=0)
        return jnp.sum(got, axis=0)

    def combine_moments(got, count):
        total = total_of(got)
        mean = total * (1.0 / got.shape[0])
        off = got - mean[None]
        spread = total_of(off * off) * count
        return jnp.where(lane1 < CH, mean, total + pltpu.roll(spread, CH, 1))

    def combine_sums(got, count):
        return total_of(got)

    def pack_halo(index, ref):
        for side, lane in ((0, 0), (1, COLS - 1)):
            pack = jnp.zeros((CH, 128), F32)
            for i in range(ROWS):
                pack = jnp.where(lane128 == i, ref[i, :, lane : lane + 1], pack)
            pack = jnp.concatenate([pack, jnp.zeros((128 - CH, 128), F32)], axis=0)
            colsend[index, side] = pack.T[0:ROWS, :]

    def send_halo(index, ref):
        started = []
        for n, (dr, dc) in enumerate(around):
            if dc == 0:
                src = ref.at[ROWS - 1 if dr == 1 else 0]
                dst = rowhalo.at[index, 0 if dr == 1 else 1]
            else:
                src = colsend.at[index, 1 if dc == 1 else 0]
                dst = colrecv.at[index, (0 if dc == 1 else 3) + 1 - dr]
            copy = pltpu.make_async_remote_copy(
                src_ref=src,
                dst_ref=dst,
                send_sem=halo_send.at[index, n],
                recv_sem=halo_recv.at[index, n],
                device_id=near(dr, dc),
                device_id_type=MESH,
            )
            copy.start()
            started.append(copy)
        return started

    def build(dst, center, top, bottom, sides):
        for r in range(ROWS + 2):
            value = top if r == 0 else (bottom if r == ROWS + 1 else center(r - 1))
            lane = ROWS - 1 if r == 0 else (2 * ROWS if r == ROWS + 1 else ROWS + r - 1)
            before = jnp.where(lane256 == 0, sides[:, lane : lane + 1], pltpu.roll(value, 1, 1))
            lane += 3 * ROWS
            after = jnp.where(
                lane256 == COLS - 1, sides[:, lane : lane + 1], pltpu.roll(value, COLS - 1, 1)
            )
            base = 3 * CH * r
            dst[base : base + CH, :] = before.astype(BF16)
            dst[base + CH : base + 2 * CH, :] = value.astype(BF16)
            dst[base + 2 * CH : base + 3 * CH, :] = after.astype(BF16)

    lane48 = lax.broadcasted_iota(jnp.int32, (1, 6 * ROWS), 1)
    edge = jnp.where(lane48 < 3 * ROWS, not_left, not_right)
    in_side = jnp.where(lane48 < 3 * ROWS, lane48, lane48 - 3 * ROWS)
    edge = edge * jnp.where(in_side < ROWS, not_top, jnp.where(in_side < 2 * ROWS, 1.0, not_bottom))

    def build_with_halo(dst, center, apply_halo, index):
        top = apply_halo("row", 0) * not_top
        bottom = apply_halo("row", 1) * not_bottom
        build(dst, center, top, bottom, apply_halo("col", None) * edge)

    def conv(weight, src, out, after=None):
        for i in range(ROWS):
            value = dot(weight, src[3 * CH * i : 3 * CH * i + TAPS, :])
            if after is None:
                total = fold(value) if i == 0 else total + fold(value)
            out[i] = value if after is None else after(i, value)
        return total if after is None else None

    def moments(index, total, *hidden):
        ref = pre.at[index]
        mean = jnp.sum(total, axis=1, keepdims=True) * (1.0 / LOCAL)
        total = jnp.zeros((CH, 128), F32)
        for i in range(ROWS):
            off = ref[i] - mean
            total = total + fold(off * off)
        local = to_row(mean, jnp.sum(total, axis=1, keepdims=True))
        mean, squares = to_columns(exchange(index, local, combine_moments, *hidden))
        return mean, lax.rsqrt(squares * (1.0 / PIXELS) + EPS)

    def halo_block(index, kind, place):
        if kind == "row":
            return rowhalo[index, place]
        return colrecv[index].reshape(6 * ROWS, 128).T[0:CH, :]

    mean, inv = [None] * 3, [None] * 3

    def forward_norm(index, total, meanwhile):
        halo, ref = [], pre.at[index]
        mean[index], inv[index] = moments(
            index,
            total,
            lambda: pack_halo(index, ref),
            lambda: halo.extend(send_halo(index, ref)),
            meanwhile,
        )
        for copy in halo:
            copy.wait()

    def forward_rows(index, i):
        normed_white = (pre[index, i] - mean[index]) * inv[index]
        white[index, i] = normed_white
        normed = gain[index] * normed_white + shift[index]
        sig = jax.nn.sigmoid(normed)
        slope[index, i] = sig * (1.0 + normed * (1.0 - sig))
        return normed * sig

    def forward_build(index, dst):
        def outside(kind, place):
            block = halo_block(index, kind, place)
            normed = gain[index] * ((block - mean[index]) * inv[index]) + shift[index]
            return normed * jax.nn.sigmoid(normed)

        build_with_halo(dst, lambda i: forward_rows(index, i), outside, index)

    def taps_of(layer):
        return [wm_raw[9 * layer + t].astype(F32) for t in range(9)]

    def lay_taps(parts, target):
        for t in range(0, 9, 2):
            part = parts[t : t + 2]
            value = jnp.concatenate(part, axis=1) if len(part) == 2 else part[0]
            target[:, CH * t : CH * (t + len(part))] = value.astype(BF16)

    def lay_weights():
        for layer in range(2):
            lay_taps(taps_of(layer), wm.at[layer])

    def lay_turned():
        gsend[...] = jnp.zeros(gsend.shape, F32)
        for layer in range(2):
            parts = taps_of(layer)
            lay_taps([parts[8 - t].T for t in range(9)], wt.at[layer])

    def spread_cotangent():
        cot_flat[...] = cot_raw[...].astype(F32)
        for i in range(ROWS):
            cot_rows[i] = cot_flat[:, i, :]

    stem = dot(wbig[...], patches[...])
    for i in range(ROWS):
        pre[0, i] = stem[CH * i : CH * (i + 1), :]
    total = sum(fold(stem[CH * i : CH * (i + 1), :]) for i in range(ROWS))
    forward_norm(0, total, lay_weights)
    forward_build(0, x0)
    total = conv(wm[0], x0, pre.at[1])
    forward_norm(1, total, spread_cotangent)
    forward_build(1, x1)
    total = conv(wm[1], x1, pre.at[2])
    forward_norm(2, total, lay_turned)
    for i in range(ROWS):
        act_rows[i] = forward_rows(2, i)
        up[2, i] = cot_rows[i] * slope[2, i]

    def norm_sums(index, *hidden):
        shift_total = jnp.zeros((CH, 128), F32)
        gain_total = jnp.zeros((CH, 128), F32)
        for i in range(ROWS):
            shift_total = shift_total + fold(up[index, i])
            gain_total = gain_total + fold(up[index, i] * white[index, i])
        local = to_row(
            jnp.sum(shift_total, axis=1, keepdims=True), jnp.sum(gain_total, axis=1, keepdims=True)
        )
        sums = exchange(3 + index, local, combine_sums, *hidden)
        shifts_out[index : index + 1, :] = sums[:, 0:CH]
        gains_out[index : index + 1, :] = sums[:, CH : 2 * CH]
        shift_sum, gain_sum = to_columns(sums)
        return shift_sum * (1.0 / PIXELS), gain_sum * (1.0 / PIXELS)

    def down(index, sums, up_value, whitened):
        return (gain[index] * inv[index]) * (up_value - sums[0] - whitened * sums[1])

    def backward_norm(index, halo_index, meanwhile):
        halo, ref = [], up.at[index]
        sums = norm_sums(
            index,
            lambda: pack_halo(halo_index, ref),
            lambda: halo.extend(send_halo(halo_index, ref)),
            meanwhile,
        )

        def center(i):
            return down(index, sums, up[index, i], white[index, i])

        def outside(kind, place):
            whitened = (halo_block(index, kind, place) - mean[index]) * inv[index]
            return down(index, sums, halo_block(halo_index, kind, place), whitened)

        for copy in halo:
            copy.wait()
        build_with_halo(dmap, center, outside, index)

    def kernel_grad(src):
        total = jnp.zeros((CH, TAPS), F32)
        for i in range(ROWS):
            base = 3 * CH * (i + 1) + CH
            total = total + dot_nt(dmap[base : base + CH, :], src[3 * CH * i : 3 * CH * i + TAPS, :])
        return total

    def put(buf, value):
        for k in range(PLANE):
            buf[k, :, 0 : value.shape[1]] = value[2 * k : 2 * k + 2, :]

    def scatter(n, mine, got):
        got[pl.ds(plane_rank, 1)] = mine[pl.ds(plane_rank, 1)]
        for offset in PLANE_OFFSETS:
            rank, where = plane_peer(offset)
            send(mine.at[rank], got.at[plane_rank], fin_send.at[n, 0], fin_recv.at[n, 0], where)

    def along_depth(n, got, depth):
        drain(got, PLANE - 1, fin_recv.at[n, 0])
        depth[pl.ds(chip_z, 1)] = jnp.sum(got[...], axis=0)[None]
        for dz in DEPTH_OFFSETS:
            where = depth_peer(dz)
            send(depth.at[chip_z], depth.at[chip_z], fin_send.at[n, 1], fin_recv.at[n, 1], where)

    def spread(n, depth, full):
        drain(depth, DEPTH - 1, fin_recv.at[n, 1])
        full[pl.ds(plane_rank, 1)] = jnp.sum(depth[...], axis=0)[None]
        for offset in PLANE_OFFSETS:
            where = plane_peer(offset)[1]
            send(full.at[plane_rank], full.at[plane_rank], fin_send.at[n, 2], fin_recv.at[n, 2], where)

    def collect(n, full, lanes):
        drain(full, PLANE - 1, fin_recv.at[n, 2])
        for k in range(PLANE):
            rows_full[2 * k : 2 * k + 2, 0:lanes] = full[k]

    leaving = []

    def leave(src, dst):
        copy = pltpu.make_async_copy(src, dst, out_sem.at[len(leaving)])
        copy.start()
        leaving.append(copy)

    def finish_mid(layer):
        collect(layer, gfull.at[layer], 640)
        for t in range(9):
            mid_out[9 * layer + t] = rows_full[:, CH * t : CH * (t + 1)]
        span = pl.ds(9 * layer, 9)
        leave(mid_out.at[span], mid_hbm.at[span])

    def grad_stage_1(layer, src):
        put(gsend.at[layer], kernel_grad(src))
        scatter(layer, gsend.at[layer], grecv.at[layer])

    def turn_activation():
        for i in range(ROWS):
            cot_flat[:, i, :] = act_rows[i]
        act_out[...] = cot_flat[...].astype(BF16)
        leave(act_out, act_hbm)

    backward_norm(2, 3, turn_activation)
    conv(wt[1], dmap, up.at[1], lambda i, value: value * slope[1, i])
    backward_norm(1, 4, lambda: grad_stage_1(1, x1))
    conv(wt[0], dmap, up.at[0], lambda i, value: value * slope[0, i])

    def last_shadow():
        along_depth(1, grecv.at[1], gdepth.at[1])
        grad_stage_1(0, x0)

    def nothing():
        pass

    sums = norm_sums(0, nothing, nothing, last_shadow)
    leave(gains_out, gains_hbm)
    leave(shifts_out, shifts_hbm)
    for i in range(ROWS):
        dstem[CH * i : CH * (i + 1), :] = down(0, sums, up[0, i], white[0, i]).astype(BF16)
    banded = dot_nt(dstem[...], patches[...])
    total = banded[0:CH, :]
    for i in range(1, ROWS):
        total = total + pltpu.roll(banded[CH * i : CH * (i + 1), :], 512 - 2 * i, 1)
    high = total.astype(BF16)
    rest = total - high.astype(F32)
    mid = rest.astype(BF16)
    low = (rest - mid.astype(F32)).astype(BF16)
    put(ssend, dot(high, choose[...]) + dot(mid, choose[...]) + dot(low, choose[...]))
    scatter(2, ssend, srecv)
    along_depth(0, grecv.at[0], gdepth.at[0])
    spread(1, gdepth.at[1], gfull.at[1])
    along_depth(2, srecv, sdepth)
    spread(0, gdepth.at[0], gfull.at[0])
    finish_mid(1)
    spread(2, sdepth, sfull)
    finish_mid(0)
    collect(2, sfull, 256)
    turned = rows_full[:, 0:256].T
    stem_out[...] = turned[0:168, :].reshape(STEM_ROWS, 8, CH)[:, 0:7, :]
    leave(stem_out, stem_hbm)
    for n, (a, b, c) in enumerate(
        ((gsend.at[0], gdepth.at[0], gfull.at[0]), (gsend.at[1], gdepth.at[1], gfull.at[1]), (ssend, sdepth, sfull))
    ):
        drain(a, PLANE - 1, fin_send.at[n, 0])
        drain(b, DEPTH - 1, fin_send.at[n, 1])
        drain(c, PLANE - 1, fin_send.at[n, 2])
    for copy in leaving:
        copy.wait()


def write_out(*refs):
    ins, outs, held, sems = refs[0:5], refs[5:10], refs[10:15], refs[15]
    arriving = [pltpu.make_async_copy(a, b, sems.at[0, n]) for n, (a, b) in enumerate(zip(ins, held))]
    leaving = [pltpu.make_async_copy(a, b, sems.at[1, n]) for n, (a, b) in enumerate(zip(held, outs))]
    for copy in arriving:
        copy.start()
    for first, second in zip(arriving, leaving):
        first.wait()
        second.start()
    for copy in leaving:
        copy.wait()


def shards(slide_band, cotangent, stem_weight, mid_weight, norm_gains, norm_shifts):
    img = slide_band.reshape(48, 512)
    w0 = stem_weight.transpose(1, 3, 2, 0).reshape(STEM_ROWS, 7, CH)
    wm = mid_weight.transpose(0, 2, 3, 1, 4).reshape(18, CH, CH)
    hbm = pl.BlockSpec(memory_space=pltpu.HBM)
    dma = pltpu.SemaphoreType.DMA
    shapes = (
        jax.ShapeDtypeStruct((CH, ROWS, COLS), BF16),
        jax.ShapeDtypeStruct((STEM_ROWS, 7, CH), F32),
        jax.ShapeDtypeStruct((18, CH, CH), F32),
        jax.ShapeDtypeStruct((3, CH), F32),
        jax.ShapeDtypeStruct((3, CH), F32),
    )
    results = pl.pallas_call(
        kernel,
        out_shape=shapes,
        in_specs=[hbm] * 6,
        out_specs=(hbm,) * 5,
        scratch_shapes=[
            pltpu.VMEM((CH, ROWS, COLS), BF16),
            pltpu.VMEM((STEM_ROWS, 7, CH), F32),
            pltpu.VMEM((18, CH, CH), F32),
            pltpu.VMEM((3, CH), F32),
            pltpu.VMEM((3, CH), F32),
            pltpu.VMEM((CH, ROWS, COLS), BF16),
            pltpu.VMEM((STEM_ROWS, 7, CH), BF16),
            pltpu.VMEM((18, CH, CH), BF16),
            pltpu.VMEM((2, 3, CH), F32),
            pltpu.VMEM((256, 128), F32),
            pltpu.VMEM((2, CH, TAPS), BF16),
            pltpu.VMEM((2, CH, TAPS), BF16),
            pltpu.VMEM((CH, ROWS, COLS), F32),
            pltpu.VMEM((ROWS, CH, COLS), F32),
            pltpu.VMEM((ROWS, CH, COLS), F32),
            pltpu.VMEM((512, 256), BF16),
            pltpu.VMEM((144, 768), BF16),
            pltpu.VMEM((2, 768, 384), BF16),
            pltpu.VMEM((512, COLS), BF16),
            pltpu.VMEM((512, 512), BF16),
            pltpu.VMEM((3 * CH * (ROWS + 2), COLS), BF16),
            pltpu.VMEM((3 * CH * (ROWS + 2), COLS), BF16),
            pltpu.VMEM((3 * CH * (ROWS + 2), COLS), BF16),
            pltpu.VMEM((512, COLS), BF16),
            pltpu.VMEM((3, ROWS, CH, COLS), F32),
            pltpu.VMEM((3, ROWS, CH, COLS), F32),
            pltpu.VMEM((3, ROWS, CH, COLS), F32),
            pltpu.VMEM((3, ROWS, CH, COLS), F32),
            pltpu.VMEM((5, 2, CH, COLS), F32),
            pltpu.VMEM((5, 2, ROWS, 128), F32),
            pltpu.VMEM((5, 6, ROWS, 128), F32),
            pltpu.VMEM((PLANE, 1, 128), F32),
            pltpu.VMEM((DEPTH, 1, 128), F32),
            pltpu.VMEM((6, 2, 1, 128), F32),
            pltpu.VMEM((6, CHIPS, 1, 128), F32),
            pltpu.VMEM((2, PLANE, 2, 640), F32),
            pltpu.VMEM((2, PLANE, 2, 640), F32),
            pltpu.VMEM((2, DEPTH, 2, 640), F32),
            pltpu.VMEM((2, PLANE, 2, 640), F32),
            pltpu.VMEM((PLANE, 2, 256), F32),
            pltpu.VMEM((PLANE, 2, 256), F32),
            pltpu.VMEM((DEPTH, 2, 256), F32),
            pltpu.VMEM((PLANE, 2, 256), F32),
            pltpu.VMEM((CH, 640), F32),
            dma((6,)), dma((6,)),
            dma((8,)), dma((8,)), dma((5, 8)), dma((5, 8)),
            dma((6, 2)), dma((6, 2)), dma((3, 3)), dma((3, 3)),
        ],
        compiler_params=pltpu.CompilerParams(
            collective_id=0, has_side_effects=True, vmem_limit_bytes=VMEM_BYTES
        ),
    )(img, cotangent, w0, wm, norm_gains, norm_shifts)
    act, stem, mid, gains, shifts = pl.pallas_call(
        write_out,
        out_shape=shapes,
        in_specs=[hbm] * 5,
        out_specs=(hbm,) * 5,
        scratch_shapes=[pltpu.VMEM(a.shape, a.dtype) for a in shapes] + [dma((2, 5))],
        compiler_params=pltpu.CompilerParams(vmem_limit_bytes=VMEM_BYTES),
    )(*results)
    return (
        act,
        stem.reshape(7, 3, 7, CH).transpose(3, 0, 2, 1),
        mid.reshape(2, 3, 3, CH, CH).transpose(0, 3, 1, 2, 4),
        gains,
        shifts,
    )


def solution(mesh):
    return jax.shard_map(
        shards,
        mesh=mesh,
        in_specs=(P(None, "row", "col"), P(None, "row", "col"), P(), P(), P(), P()),
        out_specs=(P(None, "row", "col"), P(), P(), P(), P()),
        check_vma=False,
    )
```
